32 devices in a mesh: wide: 8 (over y, x, core), narrow: 4 (over z).
Axes of the slice: x: 2, y: 2, z: 4, core: 2. Of those that a mesh axis runs over, the one named last changes fastest.
Arguments:
- tokens: bfloat16 [32768, 1024], P(('wide', 'narrow')), may hold values from -6 to 6
- segment_ids: int32 [32, 1024], P(('wide', 'narrow')), may hold values from 0 to 7, never falling along the last dimension, each value on 1 to 512 neighbouring positions
- expert_ids: int32 [32768, 1], P(('wide', 'narrow')), may hold values from 0 to 7, as said below
- first_gain: float32 [1024], replicated, may hold values from 0.5 to 1.5
- first_shift: float32 [1024], replicated, may hold values from -1.25 to 1.25
- qkv_weight: bfloat16 [1024, 3072], replicated, may hold values from -0.1875 to 0.1875
- query_bias: float32 [1024], replicated, may hold values from -1.25 to 1.25
- value_bias: float32 [1024], replicated, may hold values from -1.25 to 1.25
- out_weight: bfloat16 [1024, 1024], replicated, may hold values from -0.75 to 0.75
- out_bias: float32 [1024], replicated, may hold values from -1.25 to 1.25
- second_gain: float32 [1024], replicated, may hold values from 0.5 to 1.5
- second_shift: float32 [1024], replicated, may hold values from -1.25 to 1.25
- up_weights: bfloat16 [8, 1024, 4096], P('wide'), may hold values from -0.1875 to 0.1875
- up_bias: float32 [8, 4096], P('wide'), may hold values from -1.25 to 1.25
- down_weights: bfloat16 [8, 4096, 1024], P('wide'), may hold values from -0.09375 to 0.09375
- down_bias: float32 [8, 1024], P('wide'), may hold values from -0.625 to 0.625
- cotangent: bfloat16 [32768, 1024], P(('wide', 'narrow')), may hold values from -6 to 6
Outputs:
- output: bfloat16 [32768, 1024], P(('wide', 'narrow'))
- input_grad: bfloat16 [32768, 1024], P(('wide', 'narrow'))
- first_gain_grad: float32 [1024], P(('wide', 'narrow'))
- first_shift_grad: float32 [1024], P(('wide', 'narrow'))
- qkv_grad: float32 [1024, 3072], P(('wide', 'narrow'))
- query_bias_grad: float32 [1024], P(('wide', 'narrow'))
- value_bias_grad: float32 [1024], P(('wide', 'narrow'))
- out_weight_grad: float32 [1024, 1024], P(('wide', 'narrow'))
- out_bias_grad: float32 [1024], P(('wide', 'narrow'))
- second_gain_grad: float32 [1024], P(('wide', 'narrow'))
- second_shift_grad: float32 [1024], P(('wide', 'narrow'))
- up_grad: float32 [8, 1024, 4096], P('wide', 'narrow')
- up_bias_grad: float32 [8, 4096], P('wide', 'narrow')
- down_grad: float32 [8, 4096, 1024], P('wide', 'narrow')
- down_bias_grad: float32 [8, 1024], P('wide', 'narrow')
The draws below stay inside these ranges and needn't reach their ends.
Inputs may be any that keep to these rules, and one draw needn't show every extreme that they name: `expert_ids`: among the 1024 tokens of one row (the tokens of one device) no expert is named by more than 160 tokens; one expert, the same for every row, is named by exactly 160 tokens of every row.
All inputs are finite; a program needn't handle non-finite values.
Results may differ from the reference program's by a relative error of at most 0.012.
Values may be sent and summed in bfloat16 or wider, within the bound.
No kernel may reach another device: no remote copies, remote signals or barrier semaphores. Data moves between devices by JAX's collectives and lax.ppermute only.
A program may use at most 384 MiB of HBM per device.

```python
import math
import jax
import jax.numpy as jnp
import numpy as np
from jax import lax

D = 1024
HEAD_DIM = 64
FF = 4096
EXPERT_COUNT = 8
TOK_DEV = 1024
SEGS = 8
ROWS = 32
TOKENS = 32768
CAP = 160


def draw_expert_ids(key, part):
    key = jax.random.fold_in(key, 11)
    whole_random_key, extra_random_key, row_random_key = jax.random.split(key, 3)
    full_expert = jax.random.randint(whole_random_key, (), 0, EXPERT_COUNT).astype(jnp.int32)
    extra_noise_amplitude = jax.random.randint(extra_random_key, (EXPERT_COUNT,), 0, 4).astype(jnp.int32)
    remaining_slots = (EXPERT_COUNT - 1) * CAP
    slot_owner_expert = ((full_expert + 1 + jnp.arange(remaining_slots, dtype=jnp.int32) // CAP) % EXPERT_COUNT).astype(jnp.int32)

    def draw_row(row_seed):
        score_key, order_key = jax.random.split(row_seed)
        noise_amplitude = jax.random.randint(score_key, (remaining_slots,), 0, 4096).astype(jnp.int32)
        router_scores = (extra_noise_amplitude[slot_owner_expert] * 4096 + noise_amplitude) * remaining_slots + jnp.arange(remaining_slots, dtype=jnp.int32)
        _, picked = lax.top_k(router_scores.astype(jnp.int32), TOK_DEV - CAP)
        row_experts = jnp.concatenate([jnp.zeros((CAP,), jnp.int32) + full_expert, slot_owner_expert[picked].astype(jnp.int32)])
        return row_experts[jax.random.permutation(order_key, TOK_DEV)]
    all_rows = jax.vmap(draw_row)(jax.random.split(row_random_key, ROWS))
    return all_rows.reshape(TOKENS, 1).astype(jnp.int32)


def strengthened(values, key, source, target, parts, factor):
    def block_of(dim):
        return (jnp.arange(values.shape[dim]) // (values.shape[dim] // parts)).reshape((-1,) + (1,) * (values.ndim - 1 - dim))

    first = jax.random.permutation(key, parts)[block_of(target)]
    other_side = (block_of(target) + parts // 2) % parts
    return jnp.where((block_of(source) == first) | (block_of(source) == other_side), factor * values, values)


def levels(own_key, shape, cuts, low, high):
    def one(dim, shards_of):
        draws = jax.random.uniform(jax.random.fold_in(jax.random.fold_in(own_key, 6), dim), (shards_of,), jnp.float32, low / len(cuts), high / len(cuts))
        return jnp.repeat(jnp.exp(draws), shape[dim] // shards_of).reshape((-1,) + (1,) * (len(shape) - dim - 1))

    gain = one(*cuts[0])
    for cut in cuts[1:]:
        gain = gain * one(*cut)
    return gain


def split_up(number_of, total, limit, skew):
    loads = [(1 << 20) // math.isqrt(standing ** skew) + 1 for standing in range(2, number_of + 1)]
    rest, counts = total - limit - (number_of - 1), [1] * (number_of - 1)
    while rest > 0:
        movable = [i for i in range(number_of - 1) if counts[i] < limit]
        whole, left = sum([loads[i] for i in movable]), rest
        for i in movable:
            addition = min(limit - counts[i], max(1, left * loads[i] // whole), rest)
            counts[i] = counts[i] + addition
            rest = rest - addition
    return np.array([limit] + counts)


def ragged_sizes(rng, number_of, total, bound, lean):
    if number_of == 2:
        one = jax.random.randint(rng, (), max(1, total - bound), min(bound, total - 1) + 1)
        return jnp.stack([one, total - one])
    sizes = jnp.asarray(split_up(number_of, total, bound, lean), jnp.int32)
    twos = (number_of - 1) // 2
    giver, sink = sizes[1:1 + 2 * twos:2], sizes[2:2 + 2 * twos:2]
    margin = jnp.minimum(giver - 1, bound - sink)
    moved = jax.random.randint(jax.random.fold_in(rng, 1), (twos,), 0, 1 << 20) % (margin + 1)
    sizes = sizes.at[1:1 + 2 * twos:2].set(giver - moved).at[2:2 + 2 * twos:2].set(sink + moved)
    return sizes[jax.random.permutation(jax.random.fold_in(rng, 2), number_of)]


def bell_draw(key, shape, scale, bound, cuts=(), held_as=jnp.bfloat16):
    values = jax.random.normal(key, shape, jnp.float32) * scale
    if len(cuts) > 0:
        values = levels(key, shape, cuts, -0.22, 0.18) * values
    return jnp.clip(values, min=-bound, max=bound).astype(held_as)


def noise_with(own_key, dims, width, reach, cuts, heavy, kind=jnp.bfloat16):
    values = width * jax.random.normal(own_key, dims, jnp.float32)
    if cuts:
        values = values * levels(own_key, dims, cuts, -0.22, 0.18)
    return jnp.clip(strengthened(values, jax.random.fold_in(own_key, 3), *heavy), -reach, reach).astype(kind)


def setup_inputs(seed: int = 0) -> dict:
    key_list = jax.random.split(jax.random.key(seed), 18)
    tokens = bell_draw(key_list[0], (TOKENS, D), 1.0, 6.0, ((0, 32),))
    segment_ids = jax.vmap(lambda own: jnp.searchsorted(jnp.cumsum(ragged_sizes(own, SEGS, TOK_DEV, TOK_DEV // 2, 1)), jnp.arange(TOK_DEV), side="right"))(jax.random.split(key_list[1], ROWS)).reshape((ROWS, TOK_DEV)).astype(jnp.int32)
    expert_ids = draw_expert_ids(jax.random.fold_in(key_list[17], 71), 0)
    first_gain = jnp.clip(1.0 + 0.1 * jax.random.normal(key_list[3], (D,), jnp.float32), 0.5, 1.5)
    first_shift = bell_draw(key_list[4], (D,), 0.2, 1.25, (), jnp.float32)
    qkv_weight = bell_draw(key_list[5], (D, 3 * D), D ** -0.5, 0.1875)
    query_bias = bell_draw(key_list[6], (D,), 0.2, 1.25, (), jnp.float32)
    value_bias = bell_draw(key_list[7], (D,), 0.2, 1.25, (), jnp.float32)
    out_weight = bell_draw(key_list[8], (D, D), (D // 16) ** -0.5, 0.75)
    out_bias = bell_draw(key_list[9], (D,), 0.2, 1.25, (), jnp.float32)
    second_gain = jnp.clip(1.0 + 0.1 * jax.random.normal(key_list[10], (D,), jnp.float32), 0.5, 1.5)
    second_shift = bell_draw(key_list[11], (D,), 0.2, 1.25, (), jnp.float32)
    up_weights = bell_draw(key_list[12], (EXPERT_COUNT, D, FF), D ** -0.5, 0.1875, ((0, 8),))
    up_bias = bell_draw(key_list[13], (EXPERT_COUNT, FF), 0.2, 1.25, ((0, 8),), jnp.float32)
    down_weights = bell_draw(key_list[14], (EXPERT_COUNT, FF, D), FF ** -0.5, 0.09375, ((0, 8),))
    down_bias = bell_draw(key_list[15], (EXPERT_COUNT, D), 0.1, 0.625, ((0, 8),), jnp.float32)
    cotangent = noise_with(key_list[16], (TOKENS, D), 1.0, 6.0, ((0, 32),), (0, 1, 32, 2.75))
    return dict(tokens=tokens, segment_ids=segment_ids, expert_ids=expert_ids, first_gain=first_gain, first_shift=first_shift, qkv_weight=qkv_weight, query_bias=query_bias, value_bias=value_bias, out_weight=out_weight, out_bias=out_bias, second_gain=second_gain, second_shift=second_shift, up_weights=up_weights, up_bias=up_bias, down_weights=down_weights, down_bias=down_bias, cotangent=cotangent)


HIGHEST_PRECISION = lax.Precision.HIGHEST
EPSILON = 1e-05
MASKED = -1e+30

@jax.custom_vjp
def low(v):
    return lax.optimization_barrier(v.astype(jnp.bfloat16)).astype(jnp.float32)

@jax.custom_vjp
def low_back(v):
    return v

def low_keep(v):
    return (low(v), None)

def low_pass(kept, grad):
    return (grad,)

def back_keep(v):
    return (v, None)

def back_low(kept, grad):
    return (low(grad),)
low.defvjp(low_keep, low_pass)
low_back.defvjp(back_keep, back_low)

def layer_norm(values, norm_gain, norm_shift):
    average = lax.optimization_barrier(jnp.mean(values, axis=-1, keepdims=True))
    centred = values - average
    spread = lax.optimization_barrier(jnp.mean(centred * centred, axis=-1, keepdims=True))
    return centred * lax.rsqrt(spread + EPSILON) * norm_gain + norm_shift

def attend_row(pieces):
    queries, keys, values, segment = pieces
    row_length = queries.shape[0]
    head_count = queries.shape[1] // HEAD_DIM
    query_heads = queries.reshape(row_length, head_count, HEAD_DIM)
    key_heads = keys.reshape(row_length, head_count, HEAD_DIM)
    value_heads = values.reshape(row_length, head_count, HEAD_DIM)
    raw_scores = jnp.einsum('qhd,khd->hqk', query_heads, key_heads, precision=HIGHEST_PRECISION)
    router_scores = low_back(raw_scores * HEAD_DIM ** (-0.5))
    places = jnp.arange(row_length)
    allowed = (places[None, :] <= places[:, None]) & (segment[None, :] == segment[:, None])
    masked = jnp.where(allowed[None], router_scores, MASKED)
    highest = lax.optimization_barrier(jnp.max(masked, axis=-1, keepdims=True))
    weights = jnp.exp(masked - highest)
    weights_low = low(weights / lax.optimization_barrier(jnp.sum(weights, axis=-1, keepdims=True)))
    attended = jnp.einsum('hqk,khd->qhd', weights_low, value_heads, precision=HIGHEST_PRECISION)
    return attended.reshape(row_length, head_count * HEAD_DIM)

def expert_apply(pieces):
    expert_rows, up_matrix, up_shift, down_matrix, down_shift = pieces
    pre_active = low_back(jnp.dot(expert_rows, up_matrix, precision=HIGHEST_PRECISION) + up_shift)
    active = low(jax.nn.gelu(pre_active, approximate=True))
    return low(jnp.dot(active, down_matrix, precision=HIGHEST_PRECISION) + down_shift)

def layer_forward(inputs, first_gain, first_shift, qkv_weight, query_bias, value_bias, out_weight, out_bias, second_gain, second_shift, up_weights, up_bias, down_weights, down_bias, segment_ids, slots):
    normed_first = low(layer_norm(inputs, first_gain, first_shift))
    projected = jnp.dot(normed_first, qkv_weight, precision=HIGHEST_PRECISION)
    queries = low(low_back(projected[:, :D] + query_bias))
    keys = low(low_back(projected[:, D:2 * D]))
    values = low(low_back(projected[:, 2 * D:] + value_bias))
    row_shape = (ROWS, TOK_DEV, D)
    attended = lax.map(jax.checkpoint(attend_row), (queries.reshape(row_shape), keys.reshape(row_shape), values.reshape(row_shape), segment_ids))
    attended = low(low_back(attended.reshape(TOKENS, D)))
    branch = low_back(jnp.dot(attended, out_weight, precision=HIGHEST_PRECISION))
    hidden = inputs + (branch + out_bias)
    expert_input = low(low_back(layer_norm(hidden, second_gain, second_shift)))
    buffer_rows = jnp.zeros((EXPERT_COUNT * ROWS * CAP, D), jnp.float32).at[slots].set(expert_input)
    buffer_rows = buffer_rows.reshape(EXPERT_COUNT, ROWS * CAP, D)
    expert_out = lax.map(jax.checkpoint(expert_apply), (buffer_rows, up_weights, up_bias, down_weights, down_bias))
    expert_mix = expert_out.reshape(EXPERT_COUNT * ROWS * CAP, D)[slots]
    return hidden + expert_mix

def reference(tokens, segment_ids, expert_ids, first_gain, first_shift, qkv_weight, query_bias, value_bias, out_weight, out_bias, second_gain, second_shift, up_weights, up_bias, down_weights, down_bias, cotangent):
    chosen = expert_ids[:, 0].reshape(ROWS, TOK_DEV).astype(jnp.int32)
    onehot = (chosen[:, :, None] == jnp.arange(EXPERT_COUNT, dtype=jnp.int32)[None, None, :]).astype(jnp.int32)
    earlier = jnp.cumsum(onehot, axis=1) - onehot
    position = lax.optimization_barrier(jnp.sum(earlier * onehot, axis=2)).astype(jnp.int32)
    row_place = jnp.arange(ROWS, dtype=jnp.int32)[:, None]
    slots = (chosen * (ROWS * CAP) + row_place * CAP + position).reshape(TOKENS).astype(jnp.int32)

    def forward(*floats):
        return layer_forward(*floats, segment_ids, slots)
    floats = (tokens.astype(jnp.float32), first_gain.astype(jnp.float32), first_shift.astype(jnp.float32), qkv_weight.astype(jnp.float32), query_bias.astype(jnp.float32), value_bias.astype(jnp.float32), out_weight.astype(jnp.float32), out_bias.astype(jnp.float32), second_gain.astype(jnp.float32), second_shift.astype(jnp.float32), up_weights.astype(jnp.float32), up_bias.astype(jnp.float32), down_weights.astype(jnp.float32), down_bias.astype(jnp.float32))
    output, pullback = jax.vjp(forward, *floats)
    grads = pullback(cotangent.astype(jnp.float32))
    return (output.astype(jnp.bfloat16), grads[0].astype(jnp.bfloat16), grads[1], grads[2], grads[3], grads[4], grads[5], grads[6], grads[7], grads[8], grads[9], grads[10], grads[11], grads[12], grads[13])
```

```python
import functools

import jax
import jax.numpy as jnp
from jax import lax
from jax.experimental import pallas as pl
from jax.experimental.pallas import tpu as pltpu
from jax.sharding import PartitionSpec as P

HEAD_DIM = 64
EPSILON = 1e-05
MASKED = -1e30
TILE = 128
REACH = 512
LOW = jnp.bfloat16
FULL = jnp.float32
VMEM_BYTES = 56 * 2**20


def params():
    return pltpu.CompilerParams(vmem_limit_bytes=VMEM_BYTES)


def cost(flops, moved):
    return pl.CostEstimate(flops=1024, bytes_accessed=1024, transcendentals=0)


def shape_of(dims, dtype):
    return jax.ShapeDtypeStruct(dims, dtype)


def whole(dims):
    return pl.BlockSpec(dims, lambda *_: (0,) * len(dims))


def dot_nn(a, b):
    return jnp.dot(a, b, preferred_element_type=FULL)


def dot_nt(a, b):
    return lax.dot_general(a, b, (((1,), (1,)), ((), ())), preferred_element_type=FULL)


def dot_tn(a, b):
    return lax.dot_general(a, b, (((0,), (0,)), ((), ())), preferred_element_type=FULL)


def normed(values):
    average = jnp.mean(values, axis=-1, keepdims=True)
    centred = values - average
    spread = jnp.mean(centred * centred, axis=-1, keepdims=True)
    inverse = lax.rsqrt(spread + EPSILON)
    return centred * inverse, inverse


def norm_back(grad, gain, xhat, inverse):
    scaled = grad * gain
    first = jnp.mean(scaled, axis=-1, keepdims=True)
    second = jnp.mean(scaled * xhat, axis=-1, keepdims=True)
    return inverse * (scaled - first - xhat * second)


def gelu_pair(v):
    slope = 0.7978845608028654
    cube = 0.044715 * slope
    square = v * v
    t = jnp.tanh(v * (slope + cube * square))
    half = 0.5 * v
    active = half + half * t
    grad = (0.5 + 0.5 * t) + half * (1.0 - t * t) * (slope + (3.0 * cube) * square)
    return active, grad


def project_kernel(tokens_ref, gain_ref, shift_ref, weight_ref, bias_ref, normed_ref, out_ref):
    xhat, _ = normed(tokens_ref[...].astype(FULL))
    low = (xhat * gain_ref[...] + shift_ref[...]).astype(LOW)
    normed_ref[...] = low
    out_ref[...] = (dot_nn(low, weight_ref[...]) + bias_ref[...]).astype(LOW)


def project(tokens, gain, shift, weight, bias, rows=256):
    count, width = tokens.shape
    out = weight.shape[1]
    return pl.pallas_call(
        project_kernel,
        grid=(count // rows,),
        in_specs=[
            pl.BlockSpec((rows, width), lambda i: (i, 0)),
            whole((1, width)),
            whole((1, width)),
            whole((width, out)),
            whole((1, out)),
        ],
        out_specs=[
            pl.BlockSpec((rows, width), lambda i: (i, 0)),
            pl.BlockSpec((rows, out), lambda i: (i, 0)),
        ],
        out_shape=[shape_of((count, width), LOW), shape_of((count, out), LOW)],
        compiler_params=params(),
        name="project",
        cost_estimate=cost(2 * count * width * out, 2 * (2 * count * width + width * out + count * out)),
    )(tokens, gain, shift, weight, bias)


def fill_mask(column_ref, line_ref, mask_ref, reach):
    blocks = line_ref.shape[1] // TILE
    key_row = lax.broadcasted_iota(jnp.int32, (TILE, TILE), 0)
    query_lane = lax.broadcasted_iota(jnp.int32, (TILE, TILE), 1)
    for i in range(blocks):
        line = line_ref[:, i * TILE : (i + 1) * TILE]
        for step in range(reach):
            j = i - (reach - 1) + step
            if j < 0:
                continue
            same = column_ref[j * TILE : (j + 1) * TILE, :] == line
            if j == i:
                same = same & (key_row <= query_lane)
            mask_ref[i, step * TILE : (step + 1) * TILE, :] = jnp.where(same, 0.0, MASKED)


def split_heads(block):
    lane = lax.broadcasted_iota(jnp.int32, block.shape, 1)
    zero = jnp.zeros_like(block)
    return jnp.concatenate(
        [jnp.where(lane < HEAD_DIM, block, zero), jnp.where(lane < HEAD_DIM, zero, block)], axis=0
    )


def join_heads(pair):
    return jnp.concatenate([pair[:HEAD_DIM, :TILE], pair[HEAD_DIM : 2 * HEAD_DIM, TILE:]], axis=0)


def twice(values):
    return jnp.concatenate([values, values], axis=1)


def attend_kernel(
    reach, count_ref, q_ref, k_ref, v_ref, column_ref, line_ref, out_ref, log_ref, mask_ref, vt_ref
):
    pairs = [slice(p * TILE, (p + 1) * TILE) for p in range(q_ref.shape[1] // TILE)]

    @pl.when(pl.program_id(0) == 0)
    def _():
        fill_mask(column_ref, line_ref, mask_ref, reach)

    for p, cols in enumerate(pairs):
        vt_ref[p, :TILE, :] = v_ref[:, cols].T
        vt_ref[p, TILE:, :] = jnp.ones((vt_ref.shape[1] - TILE, vt_ref.shape[2]), LOW)

    def block(i, carry):
        here = pl.ds(pl.multiple_of(i * TILE, TILE), TILE)
        for n in range(1, reach + 1):

            @pl.when(count_ref[i] == n)
            def _():
                window = pl.ds(pl.multiple_of((i - (n - 1)) * TILE, TILE), n * TILE)
                mask = twice(mask_ref[i, (reach - n) * TILE :, :])
                queries = [split_heads(q_ref[here, c] * jnp.asarray(HEAD_DIM**-0.5, LOW)) for c in pairs]
                scores = [dot_nt(k_ref[window, c], q) + mask for c, q in zip(pairs, queries)]
                highest = [jnp.max(s, axis=0, keepdims=True) for s in scores]
                weights = [jnp.exp(s - h).astype(LOW) for s, h in zip(scores, highest)]
                mixed = [dot_nn(vt_ref[p, :, window], w) for p, w in enumerate(weights)]
                for p, cols in enumerate(pairs):
                    totals = mixed[p][TILE : TILE + 1, :]
                    value = mixed[p][:TILE, :] * (1.0 / totals)
                    out_ref[here, cols] = join_heads(value).T.astype(LOW)
                    logs = highest[p] + jnp.log(totals)
                    log_ref[p, 0:1, here] = logs[:, :TILE]
                    log_ref[p, 1:2, here] = logs[:, TILE:]

        return carry

    lax.fori_loop(0, q_ref.shape[0] // TILE, block, 0)


def attend(counts, projected, column, line, reach, group=8):
    rows = projected.shape[0]
    width = projected.shape[1] // 3
    steps = width // (TILE * group)
    cols = TILE * group
    return pl.pallas_call(
        functools.partial(attend_kernel, reach),
        grid_spec=pltpu.PrefetchScalarGridSpec(
            num_scalar_prefetch=1,
            grid=(steps,),
            in_specs=[
                pl.BlockSpec((rows, cols), lambda j, _: (0, j)),
                pl.BlockSpec((rows, cols), lambda j, _: (0, j + steps)),
                pl.BlockSpec((rows, cols), lambda j, _: (0, j + 2 * steps)),
                whole((rows, 1)),
                whole((1, rows)),
            ],
            out_specs=[
                pl.BlockSpec((rows, cols), lambda j, _: (0, j)),
                pl.BlockSpec((group, 8, rows), lambda j, _: (j, 0, 0)),
            ],
            scratch_shapes=[
                pltpu.VMEM((rows // TILE, reach * TILE, TILE), FULL),
                pltpu.VMEM((group, TILE + 16, rows), LOW),
            ],
        ),
        out_shape=[shape_of((rows, width), LOW), shape_of((width // TILE, 8, rows), FULL)],
        compiler_params=params(),
        name="attend",
        cost_estimate=cost(24 * rows * rows * width, 10 * rows * width),
    )(counts, projected, projected, projected, column, line)


def attend_back_kernel(
    reach,
    count_ref,
    q_ref,
    k_ref,
    v_ref,
    out_ref,
    grad_ref,
    log_ref,
    column_ref,
    line_ref,
    back_ref,
    bias_ref,
    mask_ref,
    kt_ref,
    dk_ref,
    dv_ref,
):
    pairs = [slice(p * TILE, (p + 1) * TILE) for p in range(q_ref.shape[1] // TILE)]

    @pl.when(pl.program_id(0) == 0)
    def _():
        fill_mask(column_ref, line_ref, mask_ref, reach)

    scale = HEAD_DIM**-0.5
    for p, cols in enumerate(pairs):
        kt_ref[p] = k_ref[:, cols].T
    dk_ref[...] = jnp.zeros_like(dk_ref)
    dv_ref[...] = jnp.zeros_like(dv_ref)

    def block(i, carry):
        here = pl.ds(pl.multiple_of(i * TILE, TILE), TILE)
        for n in range(1, reach + 1):

            @pl.when(count_ref[i] == n)
            def _():
                window = pl.ds(pl.multiple_of((i - (n - 1)) * TILE, TILE), n * TILE)
                mask = twice(mask_ref[i, (reach - n) * TILE :, :])
                queries = [split_heads(q_ref[here, c] * jnp.asarray(scale, LOW)) for c in pairs]
                grads = [split_heads(grad_ref[here, c]) for c in pairs]
                dots = []
                logs = []
                for p, c in enumerate(pairs):
                    product = (grad_ref[here, c].astype(FULL) * out_ref[here, c].astype(FULL)).T
                    dots.append(
                        jnp.concatenate(
                            [
                                jnp.sum(product[:HEAD_DIM, :], axis=0, keepdims=True),
                                jnp.sum(product[HEAD_DIM:, :], axis=0, keepdims=True),
                            ],
                            axis=1,
                        )
                    )
                    logs.append(
                        jnp.concatenate([log_ref[p, 0:1, here], log_ref[p, 1:2, here]], axis=1)
                    )
                scores = [dot_nt(k_ref[window, c], q) + mask for c, q in zip(pairs, queries)]
                prob_grad = [dot_nt(v_ref[window, c], g) for c, g in zip(pairs, grads)]
                exact = [jnp.exp(s - l) for s, l in zip(scores, logs)]
                score_grad = [
                    (e * (g - d)).astype(LOW) for e, g, d in zip(exact, prob_grad, dots)
                ]
                for p, c in enumerate(pairs):
                    dv_ref[window, c] += dot_nn(exact[p].astype(LOW), grads[p])
                    dk_ref[window, c] += dot_nn(score_grad[p], queries[p])
                    back = join_heads(dot_nn(kt_ref[p, :, window], score_grad[p])) * scale
                    back_ref[0, here, c] = back.T.astype(LOW)

        return carry

    lax.fori_loop(0, q_ref.shape[0] // TILE, block, 0)
    back_ref[1, :, :] = dk_ref[...].astype(LOW)
    value_grad = dv_ref[...].astype(LOW)
    back_ref[2, :, :] = value_grad
    bias_ref[0:1, :] = jnp.sum(back_ref[0, :, :].astype(FULL), axis=0, keepdims=True)
    bias_ref[1:2, :] = jnp.sum(value_grad.astype(FULL), axis=0, keepdims=True)


def attend_back(counts, projected, attended, grad, logs, column, line, reach, group=4):
    rows = projected.shape[0]
    width = projected.shape[1] // 3
    steps = width // (TILE * group)
    cols = TILE * group
    return pl.pallas_call(
        functools.partial(attend_back_kernel, reach),
        grid_spec=pltpu.PrefetchScalarGridSpec(
            num_scalar_prefetch=1,
            grid=(steps,),
            in_specs=[
                pl.BlockSpec((rows, cols), lambda j, _: (0, j)),
                pl.BlockSpec((rows, cols), lambda j, _: (0, j + steps)),
                pl.BlockSpec((rows, cols), lambda j, _: (0, j + 2 * steps)),
                pl.BlockSpec((rows, cols), lambda j, _: (0, j)),
                pl.BlockSpec((rows, cols), lambda j, _: (0, j)),
                pl.BlockSpec((group, 8, rows), lambda j, _: (j, 0, 0)),
                whole((rows, 1)),
                whole((1, rows)),
            ],
            out_specs=[
                pl.BlockSpec((3, rows, cols), lambda j, _: (0, 0, j)),
                pl.BlockSpec((8, cols), lambda j, _: (0, j)),
            ],
            scratch_shapes=[
                pltpu.VMEM((rows // TILE, reach * TILE, TILE), FULL),
                pltpu.VMEM((group, TILE, rows), LOW),
                pltpu.VMEM((rows, cols), FULL),
                pltpu.VMEM((rows, cols), FULL),
            ],
        ),
        out_shape=[shape_of((3, rows, width), LOW), shape_of((8, width), FULL)],
        compiler_params=params(),
        name="attend_back",
        cost_estimate=cost(36 * rows * rows * width, 20 * rows * width),
    )(counts, projected, projected, projected, attended, grad, logs, column, line)


def one_hot(hit):
    return jnp.where(hit, 1.0, 0.0).astype(LOW)


def dispatch_kernel(slot_ref, rows_ref, out_ref):
    tile = out_ref.shape[0]
    place = pl.program_id(0) * tile + lax.broadcasted_iota(jnp.int32, (tile, slot_ref.shape[1]), 0)
    out_ref[...] = dot_nn(one_hot(place == slot_ref[...]), rows_ref[...]).astype(LOW)


def dispatch(slot_line, rows, slots, tile=256):
    count, width = rows.shape
    return pl.pallas_call(
        dispatch_kernel,
        grid=(slots // tile,),
        in_specs=[whole((1, count)), whole((count, width))],
        out_specs=pl.BlockSpec((tile, width), lambda i: (i, 0)),
        out_shape=shape_of((slots, width), LOW),
        compiler_params=params(),
        name="dispatch",
        cost_estimate=cost(2 * slots * count * width, 2 * (count + slots) * width),
    )(slot_line, rows)


def picked(slot_ref, slotted):
    lane = lax.broadcasted_iota(jnp.int32, (slot_ref.shape[0], slotted.shape[0]), 1)
    return dot_nn(one_hot(lane == slot_ref[...]), slotted)


def combine_kernel(slot_ref, slotted_ref, hidden_ref, out_ref):
    out_ref[...] = (hidden_ref[...] + picked(slot_ref, slotted_ref[...])).astype(LOW)


def combine(slot_column, slotted, hidden, rows=256):
    count, width = hidden.shape
    return pl.pallas_call(
        combine_kernel,
        grid=(count // rows,),
        in_specs=[
            pl.BlockSpec((rows, 1), lambda i: (i, 0)),
            whole(slotted.shape),
            pl.BlockSpec((rows, width), lambda i: (i, 0)),
        ],
        out_specs=pl.BlockSpec((rows, width), lambda i: (i, 0)),
        out_shape=shape_of((count, width), LOW),
        compiler_params=params(),
        name="combine",
        cost_estimate=cost(2 * slotted.shape[0] * count * width, 10 * count * width),
    )(slot_column, slotted, hidden)


def mix_kernel(
    tiles,
    attended_ref,
    weight_ref,
    bias_ref,
    tokens_ref,
    gain_ref,
    shift_ref,
    slot_ref,
    hidden_ref,
    send_ref,
    rows_ref,
):
    step = pl.program_id(0)
    size = attended_ref.shape[0]

    @pl.when(step < tiles)
    def _():
        branch = dot_nn(attended_ref[...], weight_ref[...]) + bias_ref[...]
        hidden = tokens_ref[...].astype(FULL) + branch
        hidden_ref[...] = hidden
        xhat, _ = normed(hidden)
        rows_ref[pl.ds(pl.multiple_of(step * size, size), size), :] = (
            xhat * gain_ref[...] + shift_ref[...]
        ).astype(LOW)

    @pl.when(step >= tiles)
    def _():
        tile = send_ref.shape[0]
        place = (step - tiles) * tile + lax.broadcasted_iota(
            jnp.int32, (tile, slot_ref.shape[1]), 0
        )
        send_ref[...] = dot_nn(one_hot(place == slot_ref[...]), rows_ref[...]).astype(LOW)


def mix(attended, weight, bias, tokens, gain, shift, slot_line, slots, rows=256, tile=256):
    count, width = tokens.shape
    tiles = count // rows
    by_row = pl.BlockSpec((rows, width), lambda i: (jnp.minimum(i, tiles - 1), 0))
    return pl.pallas_call(
        functools.partial(mix_kernel, tiles),
        grid=(tiles + slots // tile,),
        in_specs=[
            by_row,
            whole(weight.shape),
            whole((1, width)),
            by_row,
            whole((1, width)),
            whole((1, width)),
            whole((1, count)),
        ],
        out_specs=[
            by_row,
            pl.BlockSpec((tile, width), lambda i: (jnp.maximum(i - tiles, 0), 0)),
        ],
        out_shape=[shape_of((count, width), FULL), shape_of((slots, width), LOW)],
        scratch_shapes=[pltpu.VMEM((count, width), LOW)],
        compiler_params=params(),
        name="mix",
        cost_estimate=cost(2 * (width + slots) * count * width, 14 * count * width),
    )(attended, weight, bias, tokens, gain, shift, slot_line)


def expert_first_kernel(rows_ref, grad_ref, up_ref, bias_ref, active_ref, slope_ref, down_ref):
    size = 256
    for r in range(rows_ref.shape[0] // size):
        part = slice(r * size, (r + 1) * size)
        active, slope = gelu_pair(dot_nn(rows_ref[part, :], up_ref[0]) + bias_ref[...])
        active_ref[part, :] = active.astype(LOW)
        slope_ref[part, :] = slope.astype(LOW)
    down_ref[...] = dot_tn(active_ref[...], grad_ref[...]).astype(LOW)


def expert_first(rows, grads, up, bias, chunk=512):
    count, width = rows.shape
    hidden = up.shape[2]
    by_chunk = pl.BlockSpec((count, chunk), lambda i: (0, i))
    return pl.pallas_call(
        expert_first_kernel,
        grid=(hidden // chunk,),
        in_specs=[
            whole((count, width)),
            whole((count, width)),
            pl.BlockSpec((1, width, chunk), lambda i: (0, 0, i)),
            pl.BlockSpec((1, chunk), lambda i: (0, i)),
        ],
        out_specs=[by_chunk, by_chunk, pl.BlockSpec((chunk, width), lambda i: (i, 0))],
        out_shape=[
            shape_of((count, hidden), LOW),
            shape_of((count, hidden), LOW),
            shape_of((hidden, width), LOW),
        ],
        compiler_params=params(),
        name="expert_first",
        cost_estimate=cost(5 * count * width * hidden, 6 * count * hidden + 4 * width * hidden),
    )(rows, grads, up, bias)


def expert_second_kernel(
    rows_ref, grad_ref, up_ref, down_ref, slope_ref, up_grad_ref, bias_ref, back_ref, total_ref
):
    step = pl.program_id(0)
    low = (dot_nt(grad_ref[...], down_ref[0]) * slope_ref[...].astype(FULL)).astype(LOW)
    bias_ref[...] = jnp.sum(low.astype(FULL), axis=0, keepdims=True)
    up_grad_ref[...] = dot_tn(rows_ref[...], low).astype(LOW)
    back = dot_nt(low, up_ref[0])

    @pl.when(step == 0)
    def _():
        total_ref[...] = back

    @pl.when(step > 0)
    def _():
        total_ref[...] += back

    @pl.when(step == pl.num_programs(0) - 1)
    def _():
        back_ref[...] = total_ref[...].astype(LOW)


def expert_second(rows, grads, up, down, slope, chunk=512):
    count, width = rows.shape
    hidden = up.shape[2]
    return pl.pallas_call(
        expert_second_kernel,
        grid=(hidden // chunk,),
        in_specs=[
            whole((count, width)),
            whole((count, width)),
            pl.BlockSpec((1, width, chunk), lambda i: (0, 0, i)),
            pl.BlockSpec((1, chunk, width), lambda i: (0, i, 0)),
            pl.BlockSpec((count, chunk), lambda i: (0, i)),
        ],
        out_specs=[
            pl.BlockSpec((width, chunk), lambda i: (0, i)),
            pl.BlockSpec((1, chunk), lambda i: (0, i)),
            whole((count, width)),
        ],
        out_shape=[
            shape_of((width, hidden), LOW),
            shape_of((1, hidden), FULL),
            shape_of((count, width), LOW),
        ],
        scratch_shapes=[pltpu.VMEM((count, width), FULL)],
        compiler_params=params(),
        name="expert_second",
        cost_estimate=cost(6 * count * width * hidden, 2 * count * hidden + 6 * width * hidden),
    )(rows, grads, up, down, slope)


def expert_out_kernel(active_ref, down_ref, bias_ref, out_ref):
    out_ref[...] = (dot_nn(active_ref[...], down_ref[0]) + bias_ref[...]).astype(LOW)


def expert_out(active, down, bias, rows=256):
    count, hidden = active.shape
    width = down.shape[2]
    return pl.pallas_call(
        expert_out_kernel,
        grid=(count // rows,),
        in_specs=[
            pl.BlockSpec((rows, hidden), lambda i: (i, 0)),
            whole((1, hidden, width)),
            whole((1, width)),
        ],
        out_specs=pl.BlockSpec((rows, width), lambda i: (i, 0)),
        out_shape=shape_of((count, width), LOW),
        compiler_params=params(),
        name="expert_out",
        cost_estimate=cost(2 * count * width * hidden, 2 * count * hidden + 2 * width * hidden),
    )(active, down, bias)


def middle_back_kernel(
    slot_ref,
    slotted_ref,
    hidden_ref,
    cotangent_ref,
    gain_ref,
    weight_ref,
    attended_ref,
    hidden_grad_ref,
    attended_grad_ref,
    weight_grad_ref,
    sums_ref,
    total_ref,
):
    step = pl.program_id(0)
    grad = picked(slot_ref, slotted_ref[...])
    xhat, inverse = normed(hidden_ref[...])
    hidden_grad = cotangent_ref[...].astype(FULL) + norm_back(grad, gain_ref[...], xhat, inverse)
    hidden_grad_ref[...] = hidden_grad
    low = hidden_grad.astype(LOW)
    attended_grad_ref[...] = dot_nt(low, weight_ref[...]).astype(LOW)
    weight_grad = dot_tn(attended_ref[...], low)
    sums = [
        jnp.sum(grad * xhat, axis=0, keepdims=True),
        jnp.sum(grad, axis=0, keepdims=True),
        jnp.sum(hidden_grad, axis=0, keepdims=True),
    ]

    @pl.when(step == 0)
    def _():
        total_ref[...] = weight_grad
        for i, part in enumerate(sums):
            sums_ref[i : i + 1, :] = part

    @pl.when(step > 0)
    def _():
        total_ref[...] += weight_grad
        for i, part in enumerate(sums):
            sums_ref[i : i + 1, :] += part

    @pl.when(step == pl.num_programs(0) - 1)
    def _():
        weight_grad_ref[...] = total_ref[...].astype(LOW)


def middle_back(slot_column, slotted, hidden, cotangent, gain, weight, attended, rows=256):
    count, width = hidden.shape
    by_row = pl.BlockSpec((rows, width), lambda i: (i, 0))
    return pl.pallas_call(
        middle_back_kernel,
        grid=(count // rows,),
        in_specs=[
            pl.BlockSpec((rows, 1), lambda i: (i, 0)),
            whole(slotted.shape),
            by_row,
            by_row,
            whole((1, width)),
            whole(weight.shape),
            by_row,
        ],
        out_specs=[by_row, by_row, whole(weight.shape), whole((8, width))],
        out_shape=[
            shape_of((count, width), FULL),
            shape_of((count, width), LOW),
            shape_of(weight.shape, LOW),
            shape_of((8, width), FULL),
        ],
        scratch_shapes=[pltpu.VMEM(weight.shape, FULL)],
        compiler_params=params(),
        name="middle_back",
        cost_estimate=cost(2 * (slotted.shape[0] + 2 * width) * count * width, 20 * count * width),
    )(slot_column, slotted, hidden, cotangent, gain, weight, attended)


def project_grad_kernel(normed_ref, stacked_ref, out_ref):
    out_ref[...] = dot_tn(normed_ref[...], stacked_ref[0]).astype(LOW)


def project_grad(normed_low, stacked, chunk=512):
    count, width = normed_low.shape
    each = width // chunk
    return pl.pallas_call(
        project_grad_kernel,
        grid=(3 * each,),
        in_specs=[
            whole((count, width)),
            pl.BlockSpec((1, count, chunk), lambda i: (i // each, 0, i % each)),
        ],
        out_specs=pl.BlockSpec((width, chunk), lambda i: (0, i)),
        out_shape=shape_of((width, 3 * width), LOW),
        compiler_params=params(),
        name="project_grad",
        cost_estimate=cost(6 * count * width * width, 8 * count * width + 6 * width * width),
    )(normed_low, stacked)


def first_back_kernel(
    stacked_ref, weight_ref, tokens_ref, gain_ref, hidden_grad_ref, out_ref, sums_ref
):
    step = pl.program_id(0)
    width = tokens_ref.shape[1]
    grad = dot_nt(stacked_ref[0], weight_ref[:, :width])
    for i in range(1, 3):
        grad += dot_nt(stacked_ref[i], weight_ref[:, i * width : (i + 1) * width])
    xhat, inverse = normed(tokens_ref[...].astype(FULL))
    out_ref[...] = (
        hidden_grad_ref[...] + norm_back(grad, gain_ref[...], xhat, inverse)
    ).astype(LOW)
    sums = [
        jnp.sum(grad * xhat, axis=0, keepdims=True),
        jnp.sum(grad, axis=0, keepdims=True),
    ]

    @pl.when(step == 0)
    def _():
        for i, part in enumerate(sums):
            sums_ref[i : i + 1, :] = part

    @pl.when(step > 0)
    def _():
        for i, part in enumerate(sums):
            sums_ref[i : i + 1, :] += part


def first_back(stacked, weight, tokens, gain, hidden_grad, rows=256):
    count, width = tokens.shape
    by_row = pl.BlockSpec((rows, width), lambda i: (i, 0))
    return pl.pallas_call(
        first_back_kernel,
        grid=(count // rows,),
        in_specs=[
            pl.BlockSpec((3, rows, width), lambda i: (0, i, 0)),
            whole(weight.shape),
            by_row,
            whole((1, width)),
            by_row,
        ],
        out_specs=[by_row, whole((8, width))],
        out_shape=[shape_of((count, width), LOW), shape_of((8, width), FULL)],
        compiler_params=params(),
        name="first_back",
        cost_estimate=cost(6 * count * width * width, 14 * count * width + 6 * width * width),
    )(stacked, weight, tokens, gain, hidden_grad)


def wide_sum(values, order):
    size = lax.axis_size("wide")
    place = lax.axis_index("wide")
    bits = size.bit_length() - 1
    kept = values.reshape((2,) * bits + (values.shape[0] // size, values.shape[1]))
    left = list(range(bits))[::-1]
    for bit in order(bits):
        axis = left.index(bit)
        mine = (place >> bit) & 1
        ours = lax.dynamic_index_in_dim(kept, mine, axis, keepdims=False)
        theirs = lax.dynamic_index_in_dim(kept, 1 - mine, axis, keepdims=False)
        got = lax.ppermute(theirs, "wide", [(i, i ^ (1 << bit)) for i in range(size)])
        kept = (ours.astype(FULL) + got.astype(FULL)).astype(LOW)
        left.remove(bit)
    return kept


def rising(bits):
    return list(range(bits))


def falling(bits):
    return [0] + list(range(bits - 1, 0, -1))


def wide_sum_halves(values):
    half = values.shape[1] // 2
    return [wide_sum(values[:, :half], rising), wide_sum(values[:, half:], falling)]


def narrow_sum(values):
    size = lax.axis_size("narrow")
    place = lax.axis_index("narrow")
    blocks = values.reshape((size, values.shape[0] // size) + values.shape[1:])
    arrived = []
    for way in (1, -1):
        got = None
        for step in range(1, size):
            goal = place + way * (size - step)
            block = lax.dynamic_index_in_dim(blocks, jnp.clip(goal, 0, size - 1), 0, keepdims=False)
            if got is not None:
                block = (block.astype(FULL) + got.astype(FULL)).astype(LOW)
            pairs = [(i, i + way) for i in range(size) if 0 <= i + way * (size - step) < size]
            got = lax.ppermute(block, "narrow", pairs)
        arrived.append(got)
    own = lax.dynamic_index_in_dim(blocks, place, 0, keepdims=False).astype(FULL)
    return own + arrived[0].astype(FULL) + arrived[1].astype(FULL)


def body(
    tokens,
    segment_ids,
    expert_ids,
    first_gain,
    first_shift,
    qkv_weight,
    query_bias,
    value_bias,
    out_weight,
    out_bias,
    second_gain,
    second_shift,
    up_weights,
    up_bias,
    down_weights,
    down_bias,
    cotangent,
):
    row_length, width = tokens.shape
    wide_size = lax.axis_size("wide")
    narrow_size = lax.axis_size("narrow")
    expert_total = wide_size * up_weights.shape[0]
    capacity = max(2, row_length * 5 // (4 * expert_total))
    slots = expert_total * capacity
    reach = min(REACH, row_length) // TILE + 1

    def line(vector):
        return vector.reshape(1, -1)

    def swap(rows):
        return lax.all_to_all(
            rows.reshape(expert_total, capacity, width),
            "wide",
            split_axis=0,
            concat_axis=0,
            tiled=True,
        ).reshape(slots, width)

    chosen = expert_ids[:, 0]
    onehot = (chosen[:, None] == jnp.arange(expert_total, dtype=jnp.int32)[None, :]).astype(
        jnp.int32
    )
    earlier = jnp.cumsum(onehot, axis=0) - onehot
    slot_index = chosen * capacity + jnp.sum(earlier * onehot, axis=1)
    slot_line, slot_column = slot_index[None, :], slot_index[:, None]
    segment = segment_ids[0]
    opening = segment[::TILE]
    begins = jnp.sum((segment[None, :] < opening[:, None]).astype(jnp.int32), axis=1)
    counts = jnp.arange(opening.shape[0], dtype=jnp.int32) - begins // TILE + 1
    segment_column, segment_line = segment[:, None], segment[None, :]

    send_grad = dispatch(slot_line, cotangent, slots)
    send_grad, tokens = lax.optimization_barrier((send_grad, tokens))
    got_grad = swap(send_grad)

    bias = jnp.concatenate([query_bias, jnp.zeros_like(query_bias), value_bias])
    normed_low, projected = project(
        tokens, line(first_gain), line(first_shift), qkv_weight, line(bias)
    )
    attended, logs = attend(counts, projected, segment_column, segment_line, reach)
    attended, got_grad = lax.optimization_barrier((attended, got_grad))
    hidden, send = mix(
        attended,
        out_weight,
        line(out_bias),
        tokens,
        line(second_gain),
        line(second_shift),
        slot_line,
        slots,
    )
    got_rows = swap(send)

    active, slope, down_local = expert_first(got_rows, got_grad, up_weights, up_bias)
    down_sum = lax.psum_scatter(down_local, "narrow", scatter_dimension=0, tiled=True)
    up_local, up_bias_local, back = expert_second(
        got_rows, got_grad, up_weights, down_weights, slope
    )
    up_sum = narrow_sum(up_local)
    returned_back = swap(back)
    result = expert_out(active, down_weights, down_bias)
    result, returned_back = lax.optimization_barrier((result, returned_back))
    returned = swap(result)

    hidden_grad, attended_grad, out_weight_local, middle_sums = middle_back(
        slot_column,
        returned_back,
        hidden,
        cotangent,
        line(second_gain),
        out_weight,
        attended,
    )
    out_parts = wide_sum_halves(out_weight_local)
    stacked, bias_sums = attend_back(
        counts, projected, attended, attended_grad, logs, segment_column, segment_line, reach
    )
    output = combine(slot_column, returned, hidden)
    qkv_local = project_grad(normed_low, stacked)
    qkv_parts = wide_sum_halves(qkv_local)
    input_grad, first_sums = first_back(
        stacked, qkv_weight, tokens, line(first_gain), hidden_grad
    )

    vectors = jnp.concatenate(
        [first_sums[:2], bias_sums[:2], middle_sums[2:3], middle_sums[:2], first_sums[:1]], axis=0
    )
    vector_part = wide_sum(
        jnp.pad(vectors.T, ((0, 0), (0, TILE - vectors.shape[0]))).astype(LOW), rising
    )
    share = row_length // (wide_size * narrow_size)
    down_bias_local = jnp.sum(got_grad.astype(FULL), axis=0)
    expert_bias = jnp.concatenate(
        [up_bias_local.reshape(narrow_size, -1), down_bias_local.reshape(narrow_size, -1)], axis=1
    )
    bias_columns = -(-expert_bias.shape[1] // share)
    expert_bias = jnp.pad(
        expert_bias, ((0, 0), (0, bias_columns * share - expert_bias.shape[1]))
    ).reshape(narrow_size * share, bias_columns)
    pieces = out_parts + qkv_parts + [vector_part[:, : vectors.shape[0]], expert_bias.astype(LOW)]
    filled = sum(piece.shape[1] for piece in pieces)
    pieces.append(jnp.zeros((narrow_size * share, -filled % TILE), LOW))
    summed = narrow_sum(jnp.concatenate(pieces, axis=1))
    out_weight_grad = summed[:, :width]
    qkv_grad = summed[:, width : 4 * width]
    vector_sum = summed[:, 4 * width : 4 * width + vectors.shape[0]]
    bias_sum = summed[:, 4 * width + vectors.shape[0] : filled].reshape(1, -1)
    up_share = up_bias.shape[1] // narrow_size
    down_share = width // narrow_size
    return (
        output,
        input_grad,
        vector_sum[:, 0],
        vector_sum[:, 1],
        qkv_grad,
        vector_sum[:, 2],
        vector_sum[:, 3],
        out_weight_grad,
        vector_sum[:, 4],
        vector_sum[:, 5],
        vector_sum[:, 6],
        up_sum[None],
        bias_sum[:, :up_share],
        down_sum.astype(FULL)[None],
        bias_sum[:, up_share : up_share + down_share],
    )


def solution(mesh):
    return jax.shard_map(
        body,
        mesh=mesh,
        in_specs=(
            P(("wide", "narrow"), None),
            P(("wide", "narrow"), None),
            P(("wide", "narrow"), None),
            P(),
            P(),
            P(),
            P(),
            P(),
            P(),
            P(),
            P(),
            P(),
            P("wide", None, None),
            P("wide", None),
            P("wide", None, None),
            P("wide", None),
            P(("wide", "narrow"), None),
        ),
        out_specs=(
            P(("wide", "narrow"), None),
            P(("wide", "narrow"), None),
            P(("wide", "narrow")),
            P(("wide", "narrow")),
            P(("wide", "narrow"), None),
            P(("wide", "narrow")),
            P(("wide", "narrow")),
            P(("wide", "narrow"), None),
            P(("wide", "narrow")),
            P(("wide", "narrow")),
            P(("wide", "narrow")),
            P("wide", "narrow", None),
            P("wide", "narrow"),
            P("wide", "narrow", None),
            P("wide", "narrow"),
        ),
        check_vma=False,
    )
```

```python
import functools

import jax
import jax.numpy as jnp
from jax import lax
from jax.experimental import pallas as pl
from jax.experimental.pallas import tpu as pltpu
from jax.sharding import PartitionSpec as P

HEAD_DIM = 64
EPSILON = 1e-05
MASKED = -1e30
TILE = 128
REACH = 512
LOW = jnp.bfloat16
FULL = jnp.float32
VMEM_BYTES = 56 * 2**20


def params():
    return pltpu.CompilerParams(vmem_limit_bytes=VMEM_BYTES)


def cost():
    return pl.CostEstimate(flops=1024, bytes_accessed=1024, transcendentals=0)


def shape_of(dims, dtype):
    return jax.ShapeDtypeStruct(dims, dtype)


def whole(dims):
    return pl.BlockSpec(dims, lambda *_: (0,) * len(dims))


def dot_nn(a, b):
    return jnp.dot(a, b, preferred_element_type=FULL)


def dot_nt(a, b):
    return lax.dot_general(a, b, (((1,), (1,)), ((), ())), preferred_element_type=FULL)


def dot_tn(a, b):
    return lax.dot_general(a, b, (((0,), (0,)), ((), ())), preferred_element_type=FULL)


def after(values, *others):
    return lax.optimization_barrier((values,) + others)[0]


def after2(first, *values):
    return lax.optimization_barrier(values + (first,))[:-1]


def normed(values):
    average = jnp.mean(values, axis=-1, keepdims=True)
    centred = values - average
    spread = jnp.mean(centred * centred, axis=-1, keepdims=True)
    inverse = lax.rsqrt(spread + EPSILON)
    return centred * inverse, inverse


def norm_back(grad, gain, xhat, inverse):
    scaled = grad * gain
    first = jnp.mean(scaled, axis=-1, keepdims=True)
    second = jnp.mean(scaled * xhat, axis=-1, keepdims=True)
    return inverse * (scaled - first - xhat * second)


GELU_SLOPE = 0.7978845608028654
GELU_CUBE = 0.044715 * GELU_SLOPE
LOG2_E = 1.4426950408889634


def gelu_gate(v, square):
    power = v * (-2.0 * LOG2_E * GELU_SLOPE - (2.0 * LOG2_E * GELU_CUBE) * square)
    below = 1.0 + jnp.exp2(jnp.minimum(power, 100.0))
    guess = pl.reciprocal(below, approx=True)
    return guess * (2.0 - below * guess)


def gelu(v):
    return v * gelu_gate(v, v * v)


def gelu_pair(v):
    square = v * v
    gate = gelu_gate(v, square)
    active = v * gate
    grad = gate + (active - active * gate) * (2.0 * GELU_SLOPE + (6.0 * GELU_CUBE) * square)
    return active, grad


def project_kernel(tokens_ref, gain_ref, shift_ref, weight_ref, bias_ref, normed_ref, out_ref):
    xhat, _ = normed(tokens_ref[...].astype(FULL))
    low = (xhat * gain_ref[...] + shift_ref[...]).astype(LOW)
    normed_ref[...] = low
    out_ref[...] = (dot_nn(low, weight_ref[...]) + bias_ref[...]).astype(LOW)


def project(tokens, gain, shift, weight, bias, rows=256):
    count, width = tokens.shape
    out = weight.shape[1]
    return pl.pallas_call(
        project_kernel,
        grid=(count // rows,),
        in_specs=[
            pl.BlockSpec((rows, width), lambda i: (i, 0)),
            whole((1, width)),
            whole((1, width)),
            whole((width, out)),
            whole((1, out)),
        ],
        out_specs=[
            pl.BlockSpec((rows, width), lambda i: (i, 0)),
            pl.BlockSpec((rows, out), lambda i: (i, 0)),
        ],
        out_shape=[shape_of((count, width), LOW), shape_of((count, out), LOW)],
        compiler_params=params(),
        name="project",
        cost_estimate=cost(),
    )(tokens, gain, shift, weight, bias)


def fill_mask(column_ref, line_ref, mask_ref, reach):
    blocks = line_ref.shape[1] // TILE
    key_row = lax.broadcasted_iota(jnp.int32, (TILE, TILE), 0)
    query_lane = lax.broadcasted_iota(jnp.int32, (TILE, TILE), 1)
    for i in range(blocks):
        line = line_ref[:, i * TILE : (i + 1) * TILE]
        for step in range(reach):
            j = i - (reach - 1) + step
            if j < 0:
                continue
            same = column_ref[j * TILE : (j + 1) * TILE, :] == line
            if j == i:
                same = same & (key_row <= query_lane)
            mask_ref[i, step * TILE : (step + 1) * TILE, :] = jnp.where(same, 0.0, MASKED)


def split_heads(block):
    lane = lax.broadcasted_iota(jnp.int32, block.shape, 1)
    zero = jnp.zeros_like(block)
    return jnp.concatenate(
        [jnp.where(lane < HEAD_DIM, block, zero), jnp.where(lane < HEAD_DIM, zero, block)], axis=0
    )


def join_heads(pair):
    return jnp.concatenate([pair[:HEAD_DIM, :TILE], pair[HEAD_DIM : 2 * HEAD_DIM, TILE:]], axis=0)


def twice(values):
    return jnp.concatenate([values, values], axis=1)


def attend_kernel(
    reach, count_ref, q_ref, k_ref, v_ref, column_ref, line_ref, out_ref, log_ref, mask_ref, vt_ref
):
    pairs = [slice(p * TILE, (p + 1) * TILE) for p in range(q_ref.shape[1] // TILE)]

    @pl.when(pl.program_id(0) == 0)
    def _():
        fill_mask(column_ref, line_ref, mask_ref, reach)

    for p, cols in enumerate(pairs):
        vt_ref[p, :TILE, :] = v_ref[:, cols].T
        vt_ref[p, TILE:, :] = jnp.ones((vt_ref.shape[1] - TILE, vt_ref.shape[2]), LOW)

    def block(i, carry):
        here = pl.ds(pl.multiple_of(i * TILE, TILE), TILE)
        for n in range(1, reach + 1):

            @pl.when(count_ref[i] == n)
            def _():
                window = pl.ds(pl.multiple_of((i - (n - 1)) * TILE, TILE), n * TILE)
                mask = twice(mask_ref[i, (reach - n) * TILE :, :])
                queries = [split_heads(q_ref[here, c] * jnp.asarray(HEAD_DIM**-0.5, LOW)) for c in pairs]
                scores = [dot_nt(k_ref[window, c], q) + mask for c, q in zip(pairs, queries)]
                highest = [jnp.max(s, axis=0, keepdims=True) for s in scores]
                weights = [jnp.exp(s - h).astype(LOW) for s, h in zip(scores, highest)]
                mixed = [dot_nn(vt_ref[p, :, window], w) for p, w in enumerate(weights)]
                for p, cols in enumerate(pairs):
                    totals = mixed[p][TILE : TILE + 1, :]
                    value = mixed[p][:TILE, :] * (1.0 / totals)
                    out_ref[here, cols] = join_heads(value).T.astype(LOW)
                    logs = highest[p] + jnp.log(totals)
                    log_ref[p, 0:1, here] = logs[:, :TILE]
                    log_ref[p, 1:2, here] = logs[:, TILE:]

        return carry

    lax.fori_loop(0, q_ref.shape[0] // TILE, block, 0)


def attend(counts, projected, column, line, reach, group=8):
    rows = projected.shape[0]
    width = projected.shape[1] // 3
    steps = width // (TILE * group)
    cols = TILE * group
    return pl.pallas_call(
        functools.partial(attend_kernel, reach),
        grid_spec=pltpu.PrefetchScalarGridSpec(
            num_scalar_prefetch=1,
            grid=(steps,),
            in_specs=[
                pl.BlockSpec((rows, cols), lambda j, _: (0, j)),
                pl.BlockSpec((rows, cols), lambda j, _: (0, j + steps)),
                pl.BlockSpec((rows, cols), lambda j, _: (0, j + 2 * steps)),
                whole((rows, 1)),
                whole((1, rows)),
            ],
            out_specs=[
                pl.BlockSpec((rows, cols), lambda j, _: (0, j)),
                pl.BlockSpec((group, 8, rows), lambda j, _: (j, 0, 0)),
            ],
            scratch_shapes=[
                pltpu.VMEM((rows // TILE, reach * TILE, TILE), FULL),
                pltpu.VMEM((group, TILE + 16, rows), LOW),
            ],
        ),
        out_shape=[shape_of((rows, width), LOW), shape_of((width // TILE, 8, rows), FULL)],
        compiler_params=params(),
        name="attend",
        cost_estimate=cost(),
    )(counts, projected, projected, projected, column, line)


def attend_back_kernel(
    reach,
    count_ref,
    q_ref,
    k_ref,
    v_ref,
    out_ref,
    grad_ref,
    log_ref,
    column_ref,
    line_ref,
    back_ref,
    bias_ref,
    mask_ref,
    kt_ref,
    dk_ref,
    dv_ref,
):
    pairs = [slice(p * TILE, (p + 1) * TILE) for p in range(q_ref.shape[1] // TILE)]

    @pl.when(pl.program_id(0) == 0)
    def _():
        fill_mask(column_ref, line_ref, mask_ref, reach)

    scale = HEAD_DIM**-0.5
    for p, cols in enumerate(pairs):
        kt_ref[p] = k_ref[:, cols].T
    dk_ref[...] = jnp.zeros_like(dk_ref)
    dv_ref[...] = jnp.zeros_like(dv_ref)

    def block(i, carry):
        here = pl.ds(pl.multiple_of(i * TILE, TILE), TILE)
        for n in range(1, reach + 1):

            @pl.when(count_ref[i] == n)
            def _():
                window = pl.ds(pl.multiple_of((i - (n - 1)) * TILE, TILE), n * TILE)
                mask = twice(mask_ref[i, (reach - n) * TILE :, :])
                queries = [split_heads(q_ref[here, c] * jnp.asarray(scale, LOW)) for c in pairs]
                grads = [split_heads(grad_ref[here, c]) for c in pairs]
                dots = []
                logs = []
                for p, c in enumerate(pairs):
                    product = (grad_ref[here, c].astype(FULL) * out_ref[here, c].astype(FULL)).T
                    dots.append(
                        jnp.concatenate(
                            [
                                jnp.sum(product[:HEAD_DIM, :], axis=0, keepdims=True),
                                jnp.sum(product[HEAD_DIM:, :], axis=0, keepdims=True),
                            ],
                            axis=1,
                        )
                    )
                    logs.append(
                        jnp.concatenate([log_ref[p, 0:1, here], log_ref[p, 1:2, here]], axis=1)
                    )
                scores = [dot_nt(k_ref[window, c], q) + mask for c, q in zip(pairs, queries)]
                prob_grad = [dot_nt(v_ref[window, c], g) for c, g in zip(pairs, grads)]
                exact = [jnp.exp(s - l) for s, l in zip(scores, logs)]
                score_grad = [
                    (e * (g - d)).astype(LOW) for e, g, d in zip(exact, prob_grad, dots)
                ]
                for p, c in enumerate(pairs):
                    dv_ref[window, c] += dot_nn(exact[p].astype(LOW), grads[p])
                    dk_ref[window, c] += dot_nn(score_grad[p], queries[p])
                    back = join_heads(dot_nn(kt_ref[p, :, window], score_grad[p])) * scale
                    back_ref[0, here, c] = back.T.astype(LOW)

        return carry

    lax.fori_loop(0, q_ref.shape[0] // TILE, block, 0)
    back_ref[1, :, :] = dk_ref[...].astype(LOW)
    value_grad = dv_ref[...].astype(LOW)
    back_ref[2, :, :] = value_grad
    bias_ref[0:1, :] = jnp.sum(back_ref[0, :, :].astype(FULL), axis=0, keepdims=True)
    bias_ref[1:2, :] = jnp.sum(value_grad.astype(FULL), axis=0, keepdims=True)


def attend_back(counts, projected, attended, grad, logs, column, line, reach, part, parts):
    rows = projected.shape[0]
    width = projected.shape[1] // 3
    cols = width // parts
    group = cols // TILE
    return pl.pallas_call(
        functools.partial(attend_back_kernel, reach),
        grid_spec=pltpu.PrefetchScalarGridSpec(
            num_scalar_prefetch=1,
            grid=(1,),
            in_specs=[
                pl.BlockSpec((rows, cols), lambda j, _: (0, part)),
                pl.BlockSpec((rows, cols), lambda j, _: (0, part + parts)),
                pl.BlockSpec((rows, cols), lambda j, _: (0, part + 2 * parts)),
                pl.BlockSpec((rows, cols), lambda j, _: (0, part)),
                pl.BlockSpec((rows, cols), lambda j, _: (0, part)),
                pl.BlockSpec((group, 8, rows), lambda j, _: (part, 0, 0)),
                whole((rows, 1)),
                whole((1, rows)),
            ],
            out_specs=[whole((3, rows, cols)), whole((8, cols))],
            scratch_shapes=[
                pltpu.VMEM((rows // TILE, reach * TILE, TILE), FULL),
                pltpu.VMEM((group, TILE, rows), LOW),
                pltpu.VMEM((rows, cols), FULL),
                pltpu.VMEM((rows, cols), FULL),
            ],
        ),
        out_shape=[shape_of((3, rows, cols), LOW), shape_of((8, cols), FULL)],
        compiler_params=params(),
        name="attend_back",
        cost_estimate=cost(),
    )(counts, projected, projected, projected, attended, grad, logs, column, line)


def one_hot(hit):
    return jnp.where(hit, 1.0, 0.0).astype(LOW)


def dispatch_kernel(slot_ref, rows_ref, out_ref):
    tile = out_ref.shape[0]
    place = pl.program_id(0) * tile + lax.broadcasted_iota(jnp.int32, (tile, slot_ref.shape[1]), 0)
    out_ref[...] = dot_nn(one_hot(place == slot_ref[...]), rows_ref[...]).astype(LOW)


def dispatch(slot_line, rows, slots, tile=256):
    count, width = rows.shape
    return pl.pallas_call(
        dispatch_kernel,
        grid=(slots // tile,),
        in_specs=[whole((1, count)), whole((count, width))],
        out_specs=pl.BlockSpec((tile, width), lambda i: (i, 0)),
        out_shape=shape_of((slots, width), LOW),
        compiler_params=params(),
        name="dispatch",
        cost_estimate=cost(),
    )(slot_line, rows)


def picked(slot_ref, slotted):
    lane = lax.broadcasted_iota(jnp.int32, (slot_ref.shape[0], slotted.shape[0]), 1)
    return dot_nn(one_hot(lane == slot_ref[...]), slotted)


def combine_kernel(slot_ref, slotted_ref, hidden_ref, out_ref):
    out_ref[...] = (hidden_ref[...] + picked(slot_ref, slotted_ref[...])).astype(LOW)


def combine(slot_column, slotted, hidden, rows=256):
    count, width = hidden.shape
    return pl.pallas_call(
        combine_kernel,
        grid=(count // rows,),
        in_specs=[
            pl.BlockSpec((rows, 1), lambda i: (i, 0)),
            whole(slotted.shape),
            pl.BlockSpec((rows, width), lambda i: (i, 0)),
        ],
        out_specs=pl.BlockSpec((rows, width), lambda i: (i, 0)),
        out_shape=shape_of((count, width), LOW),
        compiler_params=params(),
        name="combine",
        cost_estimate=cost(),
    )(slot_column, slotted, hidden)


def mix_kernel(
    tiles,
    attended_ref,
    weight_ref,
    bias_ref,
    tokens_ref,
    gain_ref,
    shift_ref,
    slot_ref,
    hidden_ref,
    *refs,
):
    *send_refs, rows_ref = refs
    step = pl.program_id(0)
    size = attended_ref.shape[0]

    @pl.when(step < tiles)
    def _():
        branch = dot_nn(attended_ref[...], weight_ref[...]) + bias_ref[...]
        hidden = tokens_ref[...].astype(FULL) + branch
        hidden_ref[...] = hidden
        xhat, _ = normed(hidden)
        rows_ref[pl.ds(pl.multiple_of(step * size, size), size), :] = (
            xhat * gain_ref[...] + shift_ref[...]
        ).astype(LOW)

    @pl.when(step >= tiles)
    def _():
        tile = send_refs[0].shape[0]
        place = (step - tiles) * tile + lax.broadcasted_iota(
            jnp.int32, (tile, slot_ref.shape[1]), 0
        )
        spread = dot_nn(one_hot(place == slot_ref[...]), rows_ref[...]).astype(LOW)
        at = 0
        for send_ref in send_refs:
            cols = send_ref.shape[1]
            send_ref[...] = spread[:, at : at + cols]
            at += cols


def mix(attended, weight, bias, tokens, gain, shift, slot_line, slots, sizes, rows=256, tile=256):
    count, width = tokens.shape
    tiles = count // rows
    by_row = pl.BlockSpec((rows, width), lambda i: (jnp.minimum(i, tiles - 1), 0))
    return pl.pallas_call(
        functools.partial(mix_kernel, tiles),
        grid=(tiles + slots // tile,),
        in_specs=[
            by_row,
            whole(weight.shape),
            whole((1, width)),
            by_row,
            whole((1, width)),
            whole((1, width)),
            whole((1, count)),
        ],
        out_specs=[by_row]
        + [pl.BlockSpec((tile, cols), lambda i: (jnp.maximum(i - tiles, 0), 0)) for cols in sizes],
        out_shape=[shape_of((count, width), FULL)]
        + [shape_of((slots, cols), LOW) for cols in sizes],
        scratch_shapes=[pltpu.VMEM((count, width), LOW)],
        compiler_params=params(),
        name="mix",
        cost_estimate=cost(),
    )(attended, weight, bias, tokens, gain, shift, slot_line)


def up_product(rows_refs, part, up):
    total = None
    at = 0
    for rows_ref in rows_refs:
        cols = rows_ref.shape[1]
        more = dot_nn(rows_ref[part, :], up[at : at + cols, :])
        total = more if total is None else total + more
        at += cols
    return total


def expert_first_kernel(parts, with_down, at_ref, *refs):
    rows_refs, refs = refs[:parts], refs[parts:]
    grad_ref, up_ref, bias_ref = refs[:3]
    active_ref, slope_ref, *down_refs = refs[-3:] if with_down else refs[-2:]
    size = 256
    for r in range(grad_ref.shape[0] // size):
        part = slice(r * size, (r + 1) * size)
        active, slope = gelu_pair(up_product(rows_refs, part, up_ref[0]) + bias_ref[...])
        active_ref[part, :] = active.astype(LOW)
        slope_ref[part, :] = slope.astype(LOW)
    for down_ref in down_refs:
        down_ref[...] = dot_tn(active_ref[...], grad_ref[...]).astype(LOW)


def expert_first(half, rows, grads, up, bias, kept=(), chunk=512):
    with_down = not kept
    count, width = grads.shape
    hidden = up.shape[2]
    steps = hidden // (2 * chunk)
    by_chunk = pl.BlockSpec((count, chunk), lambda i, at: (0, at[0] * steps + i))
    first = 4 + len(rows)
    return pl.pallas_call(
        functools.partial(expert_first_kernel, len(rows), with_down),
        grid_spec=pltpu.PrefetchScalarGridSpec(
            num_scalar_prefetch=1,
            grid=(steps,),
            in_specs=[whole(part.shape) for part in rows]
            + [
                whole((count, width)),
                pl.BlockSpec((1, width, chunk), lambda i, at: (0, 0, at[0] * steps + i)),
                pl.BlockSpec((1, chunk), lambda i, at: (0, at[0] * steps + i)),
            ]
            + [pl.BlockSpec(memory_space=pl.ANY) for _ in kept],
            out_specs=[by_chunk, by_chunk]
            + [pl.BlockSpec((chunk, width), lambda i, at: (i, 0))] * with_down,
        ),
        out_shape=[shape_of((count, hidden), LOW), shape_of((count, hidden), LOW)]
        + [shape_of((hidden // 2, width), LOW)] * with_down,
        input_output_aliases={first + i: i for i in range(len(kept))},
        compiler_params=params(),
        name="expert_first",
        cost_estimate=cost(),
    )(half.reshape(1), *rows, grads, up, bias, *kept)


def down_grad_kernel(at_ref, active_ref, grad_ref, out_ref):
    out_ref[...] = dot_tn(active_ref[...], grad_ref[...]).astype(LOW)


def down_grad(half, active, grads, chunk=512):
    count, width = grads.shape
    size = active.shape[1] // 2
    steps = size // chunk
    return pl.pallas_call(
        down_grad_kernel,
        grid_spec=pltpu.PrefetchScalarGridSpec(
            num_scalar_prefetch=1,
            grid=(steps,),
            in_specs=[
                pl.BlockSpec((count, chunk), lambda i, at: (0, at[0] * steps + i)),
                whole((count, width)),
            ],
            out_specs=pl.BlockSpec((chunk, width), lambda i, at: (i, 0)),
        ),
        out_shape=shape_of((size, width), LOW),
        compiler_params=params(),
        name="down_grad",
        cost_estimate=cost(),
    )(half.reshape(1), active, grads)


def neighbour_kernel(parts, at_ref, *refs):
    rows_refs, refs = refs[:parts], refs[parts:]
    grad_ref, up_ref, bias_ref, own_ref, down_ref, active_ref = refs

    @pl.when(at_ref[1] == 1)
    def _():
        size = 256
        for r in range(grad_ref.shape[0] // size):
            part = slice(r * size, (r + 1) * size)
            active = gelu(up_product(rows_refs, part, up_ref[0]) + bias_ref[...])
            active_ref[part, :] = active.astype(LOW)
        down = dot_tn(active_ref[...], grad_ref[...])
        down_ref[...] = (own_ref[...].astype(FULL) + down).astype(LOW)


def neighbour_down(at, rows, grads, up, bias, own, chunk=512):
    count, width = grads.shape
    half = up.shape[2] // 2
    steps = half // chunk
    return pl.pallas_call(
        functools.partial(neighbour_kernel, len(rows)),
        grid_spec=pltpu.PrefetchScalarGridSpec(
            num_scalar_prefetch=1,
            grid=(steps,),
            in_specs=[whole(part.shape) for part in rows]
            + [
                whole((count, width)),
                pl.BlockSpec((1, width, chunk), lambda i, at: (0, 0, at[0] * steps + i)),
                pl.BlockSpec((1, chunk), lambda i, at: (0, at[0] * steps + i)),
                pl.BlockSpec((chunk, width), lambda i, at: (i, 0)),
            ],
            out_specs=pl.BlockSpec((chunk, width), lambda i, at: (i, 0)),
            scratch_shapes=[pltpu.VMEM((count, chunk), LOW)],
        ),
        out_shape=shape_of((half, width), LOW),
        compiler_params=params(),
        name="neighbour_down",
        cost_estimate=cost(),
    )(at, *rows, grads, up, bias, own)


def expert_second_kernel(parts, at_ref, *refs):
    rows_refs, refs = refs[:parts], refs[parts:]
    grad_ref, down_ref, slope_ref, low_ref, bias_ref, *block_refs, product_ref = refs
    low = (dot_nt(grad_ref[...], down_ref[0]) * slope_ref[...].astype(FULL)).astype(LOW)
    low_ref[...] = low
    bias_ref[...] = jnp.sum(low.astype(FULL), axis=0, keepdims=True)
    at = 0
    for rows_ref in rows_refs:
        cols = rows_ref.shape[1]
        product_ref[at : at + cols, :] = dot_tn(rows_ref[...], low).astype(LOW)
        at += cols
    for i, block_ref in enumerate(block_refs):
        size = block_ref.shape[0]
        block_ref[...] = product_ref[pl.ds(pl.multiple_of(at_ref[i] * size, size), size), :]


def expert_second(order, rows, grads, down, slope, chunk=512):
    count, width = grads.shape
    hidden = slope.shape[1]
    blocks = len(order)
    by_chunk = pl.BlockSpec((count, chunk), lambda i, _: (0, i))
    return pl.pallas_call(
        functools.partial(expert_second_kernel, len(rows)),
        grid_spec=pltpu.PrefetchScalarGridSpec(
            num_scalar_prefetch=1,
            grid=(hidden // chunk,),
            in_specs=[whole(part.shape) for part in rows]
            + [
                whole((count, width)),
                pl.BlockSpec((1, chunk, width), lambda i, _: (0, i, 0)),
                by_chunk,
            ],
            out_specs=[by_chunk, pl.BlockSpec((1, chunk), lambda i, _: (0, i))]
            + [pl.BlockSpec((width // blocks, chunk), lambda i, _: (0, i))] * blocks,
            scratch_shapes=[pltpu.VMEM((width, chunk), LOW)],
        ),
        out_shape=[shape_of((count, hidden), LOW), shape_of((1, hidden), FULL)]
        + [shape_of((width // blocks, hidden), LOW)] * blocks,
        compiler_params=params(),
        name="expert_second",
        cost_estimate=cost(),
    )(jnp.stack(order).astype(jnp.int32), *rows, grads, down, slope)


def expert_back_kernel(low_ref, up_ref, out_ref):
    out_ref[...] = dot_nt(low_ref[...], up_ref[0]).astype(LOW)


def expert_back(low, up, rows=256):
    count, hidden = low.shape
    width = up.shape[1]
    return pl.pallas_call(
        expert_back_kernel,
        grid=(count // rows,),
        in_specs=[pl.BlockSpec((rows, hidden), lambda i: (i, 0)), whole((1, width, hidden))],
        out_specs=pl.BlockSpec((rows, width), lambda i: (i, 0)),
        out_shape=shape_of((count, width), LOW),
        compiler_params=params(),
        name="expert_back",
        cost_estimate=cost(),
    )(low, up)


def expert_out_kernel(active_ref, down_ref, bias_ref, out_ref):
    out_ref[...] = (dot_nn(active_ref[...], down_ref[0]) + bias_ref[...]).astype(LOW)


def expert_out(active, down, bias, rows=256):
    count, hidden = active.shape
    width = down.shape[2]
    return pl.pallas_call(
        expert_out_kernel,
        grid=(count // rows,),
        in_specs=[
            pl.BlockSpec((rows, hidden), lambda i: (i, 0)),
            whole((1, hidden, width)),
            whole((1, width)),
        ],
        out_specs=pl.BlockSpec((rows, width), lambda i: (i, 0)),
        out_shape=shape_of((count, width), LOW),
        compiler_params=params(),
        name="expert_out",
        cost_estimate=cost(),
    )(active, down, bias)


def middle_back_kernel(
    core_ref,
    slot_ref,
    slotted_ref,
    hidden_ref,
    cotangent_ref,
    gain_ref,
    weight_ref,
    attended_ref,
    hidden_grad_ref,
    attended_grad_ref,
    kept_ref,
    sent_ref,
    sums_ref,
    total_ref,
):
    step = pl.program_id(0)
    grad = picked(slot_ref, slotted_ref[...])
    xhat, inverse = normed(hidden_ref[...])
    hidden_grad = cotangent_ref[...].astype(FULL) + norm_back(grad, gain_ref[...], xhat, inverse)
    hidden_grad_ref[...] = hidden_grad
    low = hidden_grad.astype(LOW)
    attended_grad_ref[...] = dot_nt(low, weight_ref[...]).astype(LOW)
    weight_grad = dot_tn(attended_ref[...], low)
    sums = [
        jnp.sum(grad * xhat, axis=0, keepdims=True),
        jnp.sum(grad, axis=0, keepdims=True),
        jnp.sum(hidden_grad, axis=0, keepdims=True),
    ]

    @pl.when(step == 0)
    def _():
        total_ref[...] = weight_grad
        for i, part in enumerate(sums):
            sums_ref[i : i + 1, :] = part

    @pl.when(step > 0)
    def _():
        total_ref[...] += weight_grad
        for i, part in enumerate(sums):
            sums_ref[i : i + 1, :] += part

    @pl.when(step == pl.num_programs(0) - 1)
    def _():
        cores_apart(total_ref, core_ref[0], kept_ref, sent_ref)


def middle_back(
    core, slot_column, slotted, hidden, cotangent, gain, weight, attended, rows=256
):
    count, width = hidden.shape
    wide = lax.axis_size("wide")
    part = (wide // 2, width // wide, width)
    by_row = pl.BlockSpec((rows, width), lambda i, _: (i, 0))
    return pl.pallas_call(
        middle_back_kernel,
        grid_spec=pltpu.PrefetchScalarGridSpec(
            num_scalar_prefetch=1,
            grid=(count // rows,),
            in_specs=[
                pl.BlockSpec((rows, 1), lambda i, _: (i, 0)),
                whole(slotted.shape),
                by_row,
                by_row,
                whole((1, width)),
                whole(weight.shape),
                by_row,
            ],
            out_specs=[by_row, by_row, whole(part), whole(part), whole((8, width))],
            scratch_shapes=[pltpu.VMEM(weight.shape, FULL)],
        ),
        out_shape=[
            shape_of((count, width), FULL),
            shape_of((count, width), LOW),
            shape_of(part, LOW),
            shape_of(part, LOW),
            shape_of((8, width), FULL),
        ],
        compiler_params=params(),
        name="middle_back",
        cost_estimate=cost(),
    )(core, slot_column, slotted, hidden, cotangent, gain, weight, attended)


def project_grad_kernel(core_ref, normed_ref, stacked_ref, kept_ref, sent_ref, product_ref):
    product_ref[...] = dot_tn(normed_ref[...], stacked_ref[0])
    cores_apart(product_ref, core_ref[0], kept_ref, sent_ref)


def project_grad(core, normed_low, stacked):
    count, width = normed_low.shape
    chunk = stacked.shape[2]
    wide = lax.axis_size("wide")
    part = (wide // 2, width // wide)
    half = pl.BlockSpec(part + (chunk,), lambda i, _: (0, 0, i))
    return pl.pallas_call(
        project_grad_kernel,
        grid_spec=pltpu.PrefetchScalarGridSpec(
            num_scalar_prefetch=1,
            grid=(3,),
            in_specs=[
                whole((count, width)),
                pl.BlockSpec((1, count, chunk), lambda i, _: (i, 0, 0)),
            ],
            out_specs=[half, half],
            scratch_shapes=[pltpu.VMEM((width, chunk), FULL)],
        ),
        out_shape=[shape_of(part + (3 * chunk,), LOW)] * 2,
        compiler_params=params(),
        name="project_grad",
        cost_estimate=cost(),
    )(core, normed_low, stacked)


def first_back_kernel(
    parts, weight_ref, tokens_ref, gain_ref, hidden_grad_ref, *refs
):
    stacked_refs, (out_ref, sums_ref) = refs[:parts], refs[parts:]
    step = pl.program_id(0)
    width = tokens_ref.shape[1]
    cols = width // parts
    grad = None
    for part, stacked_ref in enumerate(stacked_refs):
        for i in range(3):
            at = i * width + part * cols
            more = dot_nt(stacked_ref[i], weight_ref[:, at : at + cols])
            grad = more if grad is None else grad + more
    xhat, inverse = normed(tokens_ref[...].astype(FULL))
    out_ref[...] = (
        hidden_grad_ref[...] + norm_back(grad, gain_ref[...], xhat, inverse)
    ).astype(LOW)
    sums = [
        jnp.sum(grad * xhat, axis=0, keepdims=True),
        jnp.sum(grad, axis=0, keepdims=True),
    ]

    @pl.when(step == 0)
    def _():
        for i, part in enumerate(sums):
            sums_ref[i : i + 1, :] = part

    @pl.when(step > 0)
    def _():
        for i, part in enumerate(sums):
            sums_ref[i : i + 1, :] += part


def first_back(stacked, weight, tokens, gain, hidden_grad, rows=256):
    count, width = tokens.shape
    by_row = pl.BlockSpec((rows, width), lambda i: (i, 0))
    return pl.pallas_call(
        functools.partial(first_back_kernel, len(stacked)),
        grid=(count // rows,),
        in_specs=[whole(weight.shape), by_row, whole((1, width)), by_row]
        + [pl.BlockSpec((3, rows, part.shape[2]), lambda i: (0, i, 0)) for part in stacked],
        out_specs=[by_row, whole((8, width))],
        out_shape=[shape_of((count, width), LOW), shape_of((8, width), FULL)],
        compiler_params=params(),
        name="first_back",
        cost_estimate=cost(),
    )(weight, tokens, gain, hidden_grad, *stacked)


def merge_kernel(shape, flagged, at_ref, *refs):
    count = sum(sum(groups) for groups in shape)
    place = 0
    for out_ref, groups in zip(refs[count:], shape):
        column = 0
        for size in groups:
            total = None
            for i in range(place, place + size):
                part = refs[i][0].astype(FULL)
                if flagged[i]:
                    part = jnp.where(at_ref[count + i] == 1, part, 0.0)
                total = part if total is None else total + part
            place += size
            cols = total.shape[1]
            out_ref[:, column : column + cols] = total.astype(out_ref.dtype)
            column += cols


def merge_all(results, dtype=LOW, tile=512):
    terms = [term for groups in results for group in groups for term in group]
    flagged = [len(term) > 2 for term in terms]
    counts = [term[2] if len(term) > 2 else 1 for term in terms]
    terms = [term[:2] for term in terms]
    rows = terms[0][0].shape[1]
    widths = [sum(group[0][0].shape[2] for group in groups) for groups in results]
    tile = min(tile, rows)
    columns = sum(widths) + sum(blocks.shape[2] for blocks, _ in terms)
    while tile > 16 and tile * columns * 4 > VMEM_BYTES // 2:
        tile //= 2
    at = jnp.stack([jnp.asarray(x, jnp.int32) for x in [index for _, index in terms] + counts])
    return pl.pallas_call(
        functools.partial(
            merge_kernel, [[len(group) for group in groups] for groups in results], flagged
        ),
        grid_spec=pltpu.PrefetchScalarGridSpec(
            num_scalar_prefetch=1,
            grid=(rows // tile,),
            in_specs=[
                pl.BlockSpec((1, tile, blocks.shape[2]), lambda i, at, j=j: (at[j], i, 0))
                for j, (blocks, _) in enumerate(terms)
            ],
            out_specs=[pl.BlockSpec((tile, width), lambda i, at: (i, 0)) for width in widths],
        ),
        out_shape=[shape_of((rows, width), dtype) for width in widths],
        compiler_params=params(),
        name="merge",
        cost_estimate=cost(),
    )(at, *[blocks for blocks, _ in terms])


def merge(groups, dtype=LOW):
    return merge_all([groups], dtype)[0]


def one(values):
    return (values[None], 0)


def swap_cores(values):
    size = lax.axis_size("wide")
    return lax.ppermute(values, "wide", [(i, i ^ 1) for i in range(size)])


def flat(blocks):
    return (blocks.reshape(1, -1, blocks.shape[-1]), 0)


def all_of(blocks):
    return [(blocks, i) for i in range(blocks.shape[0])]


def swap_chips(values):
    size = lax.axis_size("wide")
    groups = [list(range(core, size, 2)) for core in range(2)]
    blocks = values.reshape(size // 2, -1, values.shape[1])
    return lax.all_to_all(
        blocks, "wide", split_axis=0, concat_axis=0, tiled=True, axis_index_groups=groups
    )


def swap_narrow(values):
    blocks = values.reshape(lax.axis_size("narrow"), -1, values.shape[1])
    return lax.all_to_all(blocks, "narrow", split_axis=0, concat_axis=0, tiled=True)


def cores_apart(values_ref, core, kept_ref, sent_ref):
    chips = kept_ref.shape[0]
    rows = kept_ref.shape[1]
    for chip in range(chips):
        kept_ref[chip] = values_ref[pl.ds((2 * chip + core) * rows, rows), :].astype(LOW)
        sent_ref[chip] = values_ref[pl.ds((2 * chip + 1 - core) * rows, rows), :].astype(LOW)


def body(
    tokens,
    segment_ids,
    expert_ids,
    first_gain,
    first_shift,
    qkv_weight,
    query_bias,
    value_bias,
    out_weight,
    out_bias,
    second_gain,
    second_shift,
    up_weights,
    up_bias,
    down_weights,
    down_bias,
    cotangent,
):
    row_length, width = tokens.shape
    wide_size = lax.axis_size("wide")
    narrow_size = lax.axis_size("narrow")
    expert_total = wide_size * up_weights.shape[0]
    capacity = max(2, row_length * 5 // (4 * expert_total))
    slots = expert_total * capacity
    reach = min(REACH, row_length) // TILE + 1

    def line(vector):
        return vector.reshape(1, -1)

    def swap(rows):
        return lax.all_to_all(
            rows.reshape(expert_total, capacity, -1),
            "wide",
            split_axis=0,
            concat_axis=0,
            tiled=True,
        ).reshape(slots, -1)

    chosen = expert_ids[:, 0]
    onehot = (chosen[:, None] == jnp.arange(expert_total, dtype=jnp.int32)[None, :]).astype(
        jnp.int32
    )
    earlier = jnp.cumsum(onehot, axis=0) - onehot
    slot_index = chosen * capacity + jnp.sum(earlier * onehot, axis=1)
    slot_line, slot_column = slot_index[None, :], slot_index[:, None]
    segment = segment_ids[0]
    opening = segment[::TILE]
    begins = jnp.sum((segment[None, :] < opening[:, None]).astype(jnp.int32), axis=1)
    counts = jnp.arange(opening.shape[0], dtype=jnp.int32) - begins // TILE + 1
    segment_column, segment_line = segment[:, None], segment[None, :]

    assert narrow_size == 4
    place = lax.axis_index("narrow")
    inward = [(0, 1), (3, 2)]
    outward = [(1, 0), (2, 3)]
    across = [(1, 2), (2, 1)]
    low_side = (place < 2).astype(jnp.int32)
    is_inner = ((place == 1) | (place == 2)).astype(jnp.int32)
    first_half = (place % 2).astype(jnp.int32)
    far, middle, near, outer = 3 * low_side, 1 + low_side, 2 - low_side, 3 - 3 * low_side
    core = (lax.axis_index("wide") % 2).astype(jnp.int32).reshape(1)

    def along(values, pairs):
        return lax.ppermute(values, "narrow", pairs)

    next_cotangent = lax.ppermute(cotangent, "narrow", inward)
    next_slot = lax.ppermute(slot_line, "narrow", inward)
    send_grad = dispatch(slot_line, cotangent, slots)
    got_grad = swap(send_grad)

    bias = jnp.concatenate([query_bias, jnp.zeros_like(query_bias), value_bias])
    normed_low, projected = project(
        after(tokens, send_grad), line(first_gain), line(first_shift), qkv_weight, line(bias)
    )
    attended, logs = attend(counts, projected, segment_column, segment_line, reach)
    attended, got_grad = lax.optimization_barrier((attended, got_grad))
    hidden, send_low, send_high = mix(
        attended,
        out_weight,
        line(out_bias),
        tokens,
        line(second_gain),
        line(second_shift),
        slot_line,
        slots,
        (3 * width // 8, 5 * width // 8),
    )
    got_low = swap(send_low)
    next_send = dispatch(after(next_slot, hidden), next_cotangent, slots)
    next_low = along(got_low, inward)
    got_high = swap(after(send_high, got_low, next_send))
    next_grad = swap(after(next_send, got_high, next_low))
    next_high = along(got_high, inward)
    rows = [got_low, got_high]

    active, slope, down_first = expert_first(first_half, rows, got_grad, up_weights, up_bias)
    first_blocks = down_first.reshape(2, -1, width)
    near_send = merge([[(first_blocks, low_side)]])
    near_part = along(near_send, inward)
    active, slope = expert_first(
        1 - first_half,
        rows,
        after(got_grad, near_send),
        up_weights,
        up_bias,
        (active, slope),
    )
    far_part = neighbour_down(
        jnp.stack([first_half, is_inner]),
        [next_low, next_high],
        after(next_grad, active),
        up_weights,
        up_bias,
        down_first,
    )
    crossed = along(far_part, across).reshape(2, -1, width)
    up_low, up_bias_local, up_far, up_middle, up_near, up_outer = expert_second(
        [far, middle, near, outer], rows, after(got_grad, far_part), down_weights, slope
    )
    from_far, from_middle, from_near = [along(up, inward) for up in (up_far, up_middle, up_near)]
    back = expert_back(after(up_low, near_part), up_weights)
    returned_back = swap(back)
    result = expert_out(active, after(down_weights, back), down_bias)
    down_second = down_grad(1 - first_half, active, after(got_grad, result))
    returned = swap(after(result, down_second))
    second_blocks = down_second.reshape(2, -1, width)

    hidden_grad, attended_grad, out_weight_kept, out_weight_sent, middle_sums = middle_back(
        core,
        slot_column,
        after(returned_back, down_second),
        hidden,
        cotangent,
        line(second_gain),
        out_weight,
        attended,
    )
    out_weight_got = swap_cores(out_weight_sent)
    far_send = merge([[one(up_far), one(after(from_far, attended_grad))]])
    far_crossed = along(far_send, across)
    outer_send = merge(
        [[(second_blocks, 1 - low_side), (after(crossed, attended_grad), 1 - low_side)]]
    )
    outer_part = along(outer_send, outward)

    def heads_back(part, grad):
        return attend_back(
            counts, projected, attended, grad, logs, segment_column, segment_line, reach, part, 2
        )

    stacked_first, bias_first = heads_back(0, after(attended_grad, far_send, outer_send))
    first_kept, first_sent = project_grad(core, normed_low, stacked_first)
    first_got = swap_cores(first_sent)
    middle_send = merge([[one(up_middle), one(after(from_middle, first_sent))]])
    middle_crossed = along(middle_send, across)
    first_group = merge(
        [
            [flat(out_weight_kept), flat(out_weight_got)],
            [flat(first_kept), flat(after(first_got, middle_send))],
        ]
    )
    first_chips = swap_chips(first_group)
    stacked_second, bias_second = heads_back(1, after(attended_grad, first_group))
    up_outer_send = merge([[one(up_outer), one(after(far_crossed, stacked_second))]])
    up_outer_part = along(up_outer_send, outward)
    second_kept, second_sent = project_grad(
        core, normed_low, after(stacked_second, up_outer_send, outer_part, returned)
    )
    second_got = swap_cores(second_sent)
    output = combine(slot_column, returned, after(hidden, second_sent, middle_crossed, from_near))
    second_group = merge([[flat(second_kept), flat(after(second_got, output))]])
    second_chips = swap_chips(second_group)
    input_grad, first_sums = first_back(
        [stacked_first, stacked_second],
        qkv_weight,
        tokens,
        line(first_gain),
        after(hidden_grad, second_group, first_chips),
    )

    lane_rows = width // wide_size
    down_bias_local = jnp.sum(got_grad.astype(FULL), axis=0)
    expert_bias = jnp.concatenate(
        [up_bias_local.reshape(narrow_size, -1), down_bias_local.reshape(narrow_size, -1)], axis=1
    )
    own_rows = lane_rows // narrow_size
    bias_columns = -(-expert_bias.shape[1] // (own_rows * TILE)) * TILE
    expert_bias = jnp.pad(
        expert_bias, ((0, 0), (0, bias_columns * own_rows - expert_bias.shape[1]))
    ).reshape(lane_rows, bias_columns)
    own_group = merge(
        [
            all_of(first_chips),
            all_of(after(second_chips, input_grad, up_outer_part)),
            [one(expert_bias.astype(LOW))],
        ]
    )
    lines = swap_narrow(own_group)

    vectors = jnp.concatenate(
        [
            first_sums[:2],
            jnp.concatenate([bias_first[:2], bias_second[:2]], axis=1),
            middle_sums[2:3],
            middle_sums[:2],
            first_sums[:1],
        ],
        axis=0,
    )
    devices = wide_size * narrow_size
    share = width // devices
    spread = vectors.reshape(8, devices, share).transpose(1, 0, 2).reshape(devices, 1, 8 * share)
    gathered = lax.all_to_all(
        after(spread, own_group),
        ("wide", "narrow"),
        split_axis=0,
        concat_axis=0,
        tiled=True,
    )
    vector_sum = jnp.sum(gathered, axis=0).reshape(8, share)
    shared = merge([all_of(lines)], FULL)
    half = width // 2
    out_weight_grad = shared[:, :width]
    qkv_grad = jnp.concatenate(
        [
            shared[:, width + (3 * part + i) * half : width + (3 * part + i + 1) * half]
            for i in range(3)
            for part in range(2)
        ],
        axis=1,
    )
    bias_sum = shared[:, 4 * width :].reshape(1, -1)
    up_share = up_bias.shape[1] // narrow_size
    down_share = width // narrow_size
    down_sum = merge(
        [
            [
                (second_blocks, low_side, is_inner),
                (first_blocks, 1 - low_side, 1 - is_inner),
                one(near_part),
                one(outer_part),
                (crossed, place - 2 + 2 * low_side),
            ]
        ],
        FULL,
    )
    up_sum = merge(
        [
            [
                one(up_near) + (is_inner,),
                one(up_outer) + (1 - is_inner,),
                one(from_near),
                one(up_outer_part),
                one(middle_crossed),
            ]
        ],
        FULL,
    )
    return (
        output,
        input_grad,
        vector_sum[0],
        vector_sum[1],
        qkv_grad,
        vector_sum[2],
        vector_sum[3],
        out_weight_grad,
        vector_sum[4],
        vector_sum[5],
        vector_sum[6],
        up_sum[None],
        bias_sum[:, :up_share],
        down_sum[None],
        bias_sum[:, up_share : up_share + down_share],
    )


def solution(mesh):
    return jax.shard_map(
        body,
        mesh=mesh,
        in_specs=(
            P(("wide", "narrow"), None),
            P(("wide", "narrow"), None),
            P(("wide", "narrow"), None),
            P(),
            P(),
            P(),
            P(),
            P(),
            P(),
            P(),
            P(),
            P(),
            P("wide", None, None),
            P("wide", None),
            P("wide", None, None),
            P("wide", None),
            P(("wide", "narrow"), None),
        ),
        out_specs=(
            P(("wide", "narrow"), None),
            P(("wide", "narrow"), None),
            P(("wide", "narrow")),
            P(("wide", "narrow")),
            P(("wide", "narrow"), None),
            P(("wide", "narrow")),
            P(("wide", "narrow")),
            P(("wide", "narrow"), None),
            P(("wide", "narrow")),
            P(("wide", "narrow")),
            P(("wide", "narrow")),
            P("wide", "narrow", None),
            P("wide", "narrow"),
            P("wide", "narrow", None),
            P("wide", "narrow"),
        ),
        check_vma=False,
    )
```

```python
import functools

import jax
import jax.numpy as jnp
from jax import lax
from jax.experimental import pallas as pl
from jax.experimental.pallas import tpu as pltpu
from jax.sharding import PartitionSpec as P

HEAD_DIM = 64
EPSILON = 1e-05
MASKED = -1e30
TILE = 128
REACH = 512
LOW = jnp.bfloat16
FULL = jnp.float32
VMEM_BYTES = 56 * 2**20


def params():
    return pltpu.CompilerParams(vmem_limit_bytes=VMEM_BYTES)


def cost():
    return pl.CostEstimate(flops=1024, bytes_accessed=1024, transcendentals=0)


def shape_of(dims, dtype):
    return jax.ShapeDtypeStruct(dims, dtype)


def whole(dims):
    return pl.BlockSpec(dims, lambda *_: (0,) * len(dims))


def dot_nn(a, b):
    return jnp.dot(a, b, preferred_element_type=FULL)


def dot_nt(a, b):
    return lax.dot_general(a, b, (((1,), (1,)), ((), ())), preferred_element_type=FULL)


def dot_tn(a, b):
    return lax.dot_general(a, b, (((0,), (0,)), ((), ())), preferred_element_type=FULL)


def after(values, *others):
    return lax.optimization_barrier((values,) + others)[0]


def after2(first, *values):
    return lax.optimization_barrier(values + (first,))[:-1]


def normed(values):
    average = jnp.mean(values, axis=-1, keepdims=True)
    centred = values - average
    spread = jnp.mean(centred * centred, axis=-1, keepdims=True)
    inverse = lax.rsqrt(spread + EPSILON)
    return centred * inverse, inverse


def norm_back(grad, gain, xhat, inverse):
    scaled = grad * gain
    first = jnp.mean(scaled, axis=-1, keepdims=True)
    second = jnp.mean(scaled * xhat, axis=-1, keepdims=True)
    return inverse * (scaled - first - xhat * second)


GELU_SLOPE = 0.7978845608028654
GELU_CUBE = 0.044715 * GELU_SLOPE
LOG2_E = 1.4426950408889634


def gelu_gate(v, square):
    power = v * (-2.0 * LOG2_E * GELU_SLOPE - (2.0 * LOG2_E * GELU_CUBE) * square)
    below = 1.0 + jnp.exp2(jnp.minimum(power, 100.0))
    guess = pl.reciprocal(below, approx=True)
    return guess * (2.0 - below * guess)


def gelu(v):
    return v * gelu_gate(v, v * v)


def gelu_pair(v):
    square = v * v
    gate = gelu_gate(v, square)
    active = v * gate
    grad = gate + (active - active * gate) * (2.0 * GELU_SLOPE + (6.0 * GELU_CUBE) * square)
    return active, grad


def project_kernel(tokens_ref, gain_ref, shift_ref, weight_ref, bias_ref, normed_ref, out_ref):
    xhat, _ = normed(tokens_ref[...].astype(FULL))
    low = (xhat * gain_ref[...] + shift_ref[...]).astype(LOW)
    normed_ref[...] = low
    out_ref[...] = (dot_nn(low, weight_ref[...]) + bias_ref[...]).astype(LOW)


def project(tokens, gain, shift, weight, bias, rows=256):
    count, width = tokens.shape
    out = weight.shape[1]
    return pl.pallas_call(
        project_kernel,
        grid=(count // rows,),
        in_specs=[
            pl.BlockSpec((rows, width), lambda i: (i, 0)),
            whole((1, width)),
            whole((1, width)),
            whole((width, out)),
            whole((1, out)),
        ],
        out_specs=[
            pl.BlockSpec((rows, width), lambda i: (i, 0)),
            pl.BlockSpec((rows, out), lambda i: (i, 0)),
        ],
        out_shape=[shape_of((count, width), LOW), shape_of((count, out), LOW)],
        compiler_params=params(),
        name="project",
        cost_estimate=cost(),
    )(tokens, gain, shift, weight, bias)


def fill_mask(column_ref, line_ref, mask_ref, reach):
    blocks = line_ref.shape[1] // TILE
    key_row = lax.broadcasted_iota(jnp.int32, (TILE, TILE), 0)
    query_lane = lax.broadcasted_iota(jnp.int32, (TILE, TILE), 1)
    for i in range(blocks):
        line = line_ref[:, i * TILE : (i + 1) * TILE]
        for step in range(reach):
            j = i - (reach - 1) + step
            if j < 0:
                continue
            same = column_ref[j * TILE : (j + 1) * TILE, :] == line
            if j == i:
                same = same & (key_row <= query_lane)
            mask_ref[i, step * TILE : (step + 1) * TILE, :] = jnp.where(same, 0.0, MASKED)


def split_heads(block):
    lane = lax.broadcasted_iota(jnp.int32, block.shape, 1)
    zero = jnp.zeros_like(block)
    return jnp.concatenate(
        [jnp.where(lane < HEAD_DIM, block, zero), jnp.where(lane < HEAD_DIM, zero, block)], axis=0
    )


def join_heads(pair):
    return jnp.concatenate([pair[:HEAD_DIM, :TILE], pair[HEAD_DIM : 2 * HEAD_DIM, TILE:]], axis=0)


def twice(values):
    return jnp.concatenate([values, values], axis=1)


def attend_kernel(
    reach, count_ref, q_ref, k_ref, v_ref, column_ref, line_ref, out_ref, log_ref, mask_ref, vt_ref
):
    pairs = [slice(p * TILE, (p + 1) * TILE) for p in range(q_ref.shape[1] // TILE)]

    @pl.when(pl.program_id(0) == 0)
    def _():
        fill_mask(column_ref, line_ref, mask_ref, reach)

    for p, cols in enumerate(pairs):
        vt_ref[p, :TILE, :] = v_ref[:, cols].T
        vt_ref[p, TILE:, :] = jnp.ones((vt_ref.shape[1] - TILE, vt_ref.shape[2]), LOW)

    def block(i, carry):
        here = pl.ds(pl.multiple_of(i * TILE, TILE), TILE)
        for n in range(1, reach + 1):

            @pl.when(count_ref[i] == n)
            def _():
                window = pl.ds(pl.multiple_of((i - (n - 1)) * TILE, TILE), n * TILE)
                mask = twice(mask_ref[i, (reach - n) * TILE :, :])
                queries = [split_heads(q_ref[here, c] * jnp.asarray(HEAD_DIM**-0.5, LOW)) for c in pairs]
                scores = [dot_nt(k_ref[window, c], q) + mask for c, q in zip(pairs, queries)]
                highest = [jnp.max(s, axis=0, keepdims=True) for s in scores]
                weights = [jnp.exp(s - h).astype(LOW) for s, h in zip(scores, highest)]
                mixed = [dot_nn(vt_ref[p, :, window], w) for p, w in enumerate(weights)]
                for p, cols in enumerate(pairs):
                    totals = mixed[p][TILE : TILE + 1, :]
                    value = mixed[p][:TILE, :] * (1.0 / totals)
                    out_ref[here, cols] = join_heads(value).T.astype(LOW)
                    logs = highest[p] + jnp.log(totals)
                    log_ref[p, 0:1, here] = logs[:, :TILE]
                    log_ref[p, 1:2, here] = logs[:, TILE:]

        return carry

    lax.fori_loop(0, q_ref.shape[0] // TILE, block, 0)


def attend(counts, projected, column, line, reach, group=8):
    rows = projected.shape[0]
    width = projected.shape[1] // 3
    steps = width // (TILE * group)
    cols = TILE * group
    return pl.pallas_call(
        functools.partial(attend_kernel, reach),
        grid_spec=pltpu.PrefetchScalarGridSpec(
            num_scalar_prefetch=1,
            grid=(steps,),
            in_specs=[
                pl.BlockSpec((rows, cols), lambda j, _: (0, j)),
                pl.BlockSpec((rows, cols), lambda j, _: (0, j + steps)),
                pl.BlockSpec((rows, cols), lambda j, _: (0, j + 2 * steps)),
                whole((rows, 1)),
                whole((1, rows)),
            ],
            out_specs=[
                pl.BlockSpec((rows, cols), lambda j, _: (0, j)),
                pl.BlockSpec((group, 8, rows), lambda j, _: (j, 0, 0)),
            ],
            scratch_shapes=[
                pltpu.VMEM((rows // TILE, reach * TILE, TILE), FULL),
                pltpu.VMEM((group, TILE + 16, rows), LOW),
            ],
        ),
        out_shape=[shape_of((rows, width), LOW), shape_of((width // TILE, 8, rows), FULL)],
        compiler_params=params(),
        name="attend",
        cost_estimate=cost(),
    )(counts, projected, projected, projected, column, line)


def attend_back_kernel(
    reach,
    count_ref,
    q_ref,
    k_ref,
    v_ref,
    out_ref,
    grad_ref,
    log_ref,
    column_ref,
    line_ref,
    back_ref,
    bias_ref,
    mask_ref,
    kt_ref,
    dk_ref,
    dv_ref,
):
    pairs = [slice(p * TILE, (p + 1) * TILE) for p in range(q_ref.shape[1] // TILE)]

    @pl.when(pl.program_id(0) == 0)
    def _():
        fill_mask(column_ref, line_ref, mask_ref, reach)

    scale = HEAD_DIM**-0.5
    for p, cols in enumerate(pairs):
        kt_ref[p] = k_ref[:, cols].T
    dk_ref[...] = jnp.zeros_like(dk_ref)
    dv_ref[...] = jnp.zeros_like(dv_ref)

    def block(i, carry):
        here = pl.ds(pl.multiple_of(i * TILE, TILE), TILE)
        for n in range(1, reach + 1):

            @pl.when(count_ref[i] == n)
            def _():
                window = pl.ds(pl.multiple_of((i - (n - 1)) * TILE, TILE), n * TILE)
                mask = twice(mask_ref[i, (reach - n) * TILE :, :])
                queries = [split_heads(q_ref[here, c] * jnp.asarray(scale, LOW)) for c in pairs]
                grads = [split_heads(grad_ref[here, c]) for c in pairs]
                dots = []
                logs = []
                for p, c in enumerate(pairs):
                    product = (grad_ref[here, c].astype(FULL) * out_ref[here, c].astype(FULL)).T
                    dots.append(
                        jnp.concatenate(
                            [
                                jnp.sum(product[:HEAD_DIM, :], axis=0, keepdims=True),
                                jnp.sum(product[HEAD_DIM:, :], axis=0, keepdims=True),
                            ],
                            axis=1,
                        )
                    )
                    logs.append(
                        jnp.concatenate([log_ref[p, 0:1, here], log_ref[p, 1:2, here]], axis=1)
                    )
                scores = [dot_nt(k_ref[window, c], q) + mask for c, q in zip(pairs, queries)]
                prob_grad = [dot_nt(v_ref[window, c], g) for c, g in zip(pairs, grads)]
                exact = [jnp.exp(s - l) for s, l in zip(scores, logs)]
                score_grad = [
                    (e * (g - d)).astype(LOW) for e, g, d in zip(exact, prob_grad, dots)
                ]
                for p, c in enumerate(pairs):
                    dv_ref[window, c] += dot_nn(exact[p].astype(LOW), grads[p])
                    dk_ref[window, c] += dot_nn(score_grad[p], queries[p])
                    back = join_heads(dot_nn(kt_ref[p, :, window], score_grad[p])) * scale
                    back_ref[0, here, c] = back.T.astype(LOW)

        return carry

    lax.fori_loop(0, q_ref.shape[0] // TILE, block, 0)
    back_ref[1, :, :] = dk_ref[...].astype(LOW)
    value_grad = dv_ref[...].astype(LOW)
    back_ref[2, :, :] = value_grad
    bias_ref[0:1, :] = jnp.sum(back_ref[0, :, :].astype(FULL), axis=0, keepdims=True)
    bias_ref[1:2, :] = jnp.sum(value_grad.astype(FULL), axis=0, keepdims=True)


def attend_back(counts, projected, attended, grad, logs, column, line, reach, part, parts):
    rows = projected.shape[0]
    width = projected.shape[1] // 3
    cols = width // parts
    group = cols // TILE
    return pl.pallas_call(
        functools.partial(attend_back_kernel, reach),
        grid_spec=pltpu.PrefetchScalarGridSpec(
            num_scalar_prefetch=1,
            grid=(1,),
            in_specs=[
                pl.BlockSpec((rows, cols), lambda j, _: (0, part)),
                pl.BlockSpec((rows, cols), lambda j, _: (0, part + parts)),
                pl.BlockSpec((rows, cols), lambda j, _: (0, part + 2 * parts)),
                pl.BlockSpec((rows, cols), lambda j, _: (0, part)),
                pl.BlockSpec((rows, cols), lambda j, _: (0, part)),
                pl.BlockSpec((group, 8, rows), lambda j, _: (part, 0, 0)),
                whole((rows, 1)),
                whole((1, rows)),
            ],
            out_specs=[whole((3, rows, cols)), whole((8, cols))],
            scratch_shapes=[
                pltpu.VMEM((rows // TILE, reach * TILE, TILE), FULL),
                pltpu.VMEM((group, TILE, rows), LOW),
                pltpu.VMEM((rows, cols), FULL),
                pltpu.VMEM((rows, cols), FULL),
            ],
        ),
        out_shape=[shape_of((3, rows, cols), LOW), shape_of((8, cols), FULL)],
        compiler_params=params(),
        name="attend_back",
        cost_estimate=cost(),
    )(counts, projected, projected, projected, attended, grad, logs, column, line)


def slots_kernel(experts, capacity, chosen_ref, out_ref):
    count = chosen_ref.shape[1]
    place = lax.broadcasted_iota(jnp.int32, (experts, count), 0)
    mine = place == chosen_ref[...]
    earlier = lax.broadcasted_iota(jnp.int32, (count, count), 0) < lax.broadcasted_iota(
        jnp.int32, (count, count), 1
    )
    before = dot_nn(one_hot(mine), one_hot(earlier))
    base = (place * capacity).astype(FULL)
    out_ref[...] = jnp.sum(jnp.where(mine, before + base, 0.0), axis=0, keepdims=True).astype(
        jnp.int32
    )


def slots_of(chosen, experts, capacity):
    return pl.pallas_call(
        functools.partial(slots_kernel, experts, capacity),
        out_shape=shape_of(chosen.shape, jnp.int32),
        compiler_params=params(),
        name="slots",
        cost_estimate=cost(),
    )(chosen)


def one_hot(hit):
    return jnp.where(hit, 1.0, 0.0).astype(LOW)


def dispatch_kernel(slot_ref, rows_ref, out_ref):
    tile = out_ref.shape[0]
    place = pl.program_id(0) * tile + lax.broadcasted_iota(jnp.int32, (tile, slot_ref.shape[1]), 0)
    out_ref[...] = dot_nn(one_hot(place == slot_ref[...]), rows_ref[...]).astype(LOW)


def dispatch(slot_line, rows, slots, tile=256):
    count, width = rows.shape
    return pl.pallas_call(
        dispatch_kernel,
        grid=(slots // tile,),
        in_specs=[whole((1, count)), whole((count, width))],
        out_specs=pl.BlockSpec((tile, width), lambda i: (i, 0)),
        out_shape=shape_of((slots, width), LOW),
        compiler_params=params(),
        name="dispatch",
        cost_estimate=cost(),
    )(slot_line, rows)


def picked(slot_ref, slotted):
    lane = lax.broadcasted_iota(jnp.int32, (slot_ref.shape[0], slotted.shape[0]), 1)
    return dot_nn(one_hot(lane == slot_ref[...]), slotted)


def combine_kernel(slot_ref, slotted_ref, hidden_ref, out_ref):
    out_ref[...] = (hidden_ref[...] + picked(slot_ref, slotted_ref[...])).astype(LOW)


def combine(slot_column, slotted, hidden, rows=256):
    count, width = hidden.shape
    return pl.pallas_call(
        combine_kernel,
        grid=(count // rows,),
        in_specs=[
            pl.BlockSpec((rows, 1), lambda i: (i, 0)),
            whole(slotted.shape),
            pl.BlockSpec((rows, width), lambda i: (i, 0)),
        ],
        out_specs=pl.BlockSpec((rows, width), lambda i: (i, 0)),
        out_shape=shape_of((count, width), LOW),
        compiler_params=params(),
        name="combine",
        cost_estimate=cost(),
    )(slot_column, slotted, hidden)


def mix_kernel(
    tiles,
    attended_ref,
    weight_ref,
    bias_ref,
    tokens_ref,
    gain_ref,
    shift_ref,
    slot_ref,
    hidden_ref,
    *refs,
):
    *send_refs, rows_ref = refs
    step = pl.program_id(0)
    size = attended_ref.shape[0]

    @pl.when(step < tiles)
    def _():
        branch = dot_nn(attended_ref[...], weight_ref[...]) + bias_ref[...]
        hidden = tokens_ref[...].astype(FULL) + branch
        hidden_ref[...] = hidden
        xhat, _ = normed(hidden)
        rows_ref[pl.ds(pl.multiple_of(step * size, size), size), :] = (
            xhat * gain_ref[...] + shift_ref[...]
        ).astype(LOW)

    @pl.when(step >= tiles)
    def _():
        tile = send_refs[0].shape[0]
        place = (step - tiles) * tile + lax.broadcasted_iota(
            jnp.int32, (tile, slot_ref.shape[1]), 0
        )
        spread = dot_nn(one_hot(place == slot_ref[...]), rows_ref[...]).astype(LOW)
        at = 0
        for send_ref in send_refs:
            cols = send_ref.shape[1]
            send_ref[...] = spread[:, at : at + cols]
            at += cols


def mix(attended, weight, bias, tokens, gain, shift, slot_line, slots, sizes, rows=256, tile=256):
    count, width = tokens.shape
    tiles = count // rows
    by_row = pl.BlockSpec((rows, width), lambda i: (jnp.minimum(i, tiles - 1), 0))
    return pl.pallas_call(
        functools.partial(mix_kernel, tiles),
        grid=(tiles + slots // tile,),
        in_specs=[
            by_row,
            whole(weight.shape),
            whole((1, width)),
            by_row,
            whole((1, width)),
            whole((1, width)),
            whole((1, count)),
        ],
        out_specs=[by_row]
        + [pl.BlockSpec((tile, cols), lambda i: (jnp.maximum(i - tiles, 0), 0)) for cols in sizes],
        out_shape=[shape_of((count, width), FULL)]
        + [shape_of((slots, cols), LOW) for cols in sizes],
        scratch_shapes=[pltpu.VMEM((count, width), LOW)],
        compiler_params=params(),
        name="mix",
        cost_estimate=cost(),
    )(attended, weight, bias, tokens, gain, shift, slot_line)


def up_product(rows_refs, part, up):
    total = None
    at = 0
    for rows_ref in rows_refs:
        cols = rows_ref.shape[1]
        more = dot_nn(rows_ref[part, :], up[at : at + cols, :])
        total = more if total is None else total + more
        at += cols
    return total


def expert_first_kernel(parts, with_down, at_ref, *refs):
    rows_refs, refs = refs[:parts], refs[parts:]
    grad_ref, up_ref, bias_ref = refs[:3]
    active_ref, slope_ref, *down_refs = refs[-3:] if with_down else refs[-2:]
    size = 256
    for r in range(grad_ref.shape[0] // size):
        part = slice(r * size, (r + 1) * size)
        active, slope = gelu_pair(up_product(rows_refs, part, up_ref[0]) + bias_ref[...])
        active_ref[part, :] = active.astype(LOW)
        slope_ref[part, :] = slope.astype(LOW)
    for down_ref in down_refs:
        down_ref[...] = dot_tn(active_ref[...], grad_ref[...]).astype(LOW)


def expert_first(half, rows, grads, up, bias, kept=(), chunk=512):
    with_down = not kept
    count, width = grads.shape
    hidden = up.shape[2]
    steps = hidden // (2 * chunk)
    by_chunk = pl.BlockSpec((count, chunk), lambda i, at: (0, at[0] * steps + i))
    first = 4 + len(rows)
    return pl.pallas_call(
        functools.partial(expert_first_kernel, len(rows), with_down),
        grid_spec=pltpu.PrefetchScalarGridSpec(
            num_scalar_prefetch=1,
            grid=(steps,),
            in_specs=[whole(part.shape) for part in rows]
            + [
                whole((count, width)),
                pl.BlockSpec((1, width, chunk), lambda i, at: (0, 0, at[0] * steps + i)),
                pl.BlockSpec((1, chunk), lambda i, at: (0, at[0] * steps + i)),
            ]
            + [pl.BlockSpec(memory_space=pl.ANY) for _ in kept],
            out_specs=[by_chunk, by_chunk]
            + [pl.BlockSpec((chunk, width), lambda i, at: (i, 0))] * with_down,
        ),
        out_shape=[shape_of((count, hidden), LOW), shape_of((count, hidden), LOW)]
        + [shape_of((hidden // 2, width), LOW)] * with_down,
        input_output_aliases={first + i: i for i in range(len(kept))},
        compiler_params=params(),
        name="expert_first",
        cost_estimate=cost(),
    )(half.reshape(1), *rows, grads, up, bias, *kept)


def down_grad_kernel(at_ref, active_ref, grad_ref, out_ref):
    out_ref[...] = dot_tn(active_ref[...], grad_ref[...]).astype(LOW)


def down_grad(half, active, grads, chunk=512):
    count, width = grads.shape
    size = active.shape[1] // 2
    steps = size // chunk
    return pl.pallas_call(
        down_grad_kernel,
        grid_spec=pltpu.PrefetchScalarGridSpec(
            num_scalar_prefetch=1,
            grid=(steps,),
            in_specs=[
                pl.BlockSpec((count, chunk), lambda i, at: (0, at[0] * steps + i)),
                whole((count, width)),
            ],
            out_specs=pl.BlockSpec((chunk, width), lambda i, at: (i, 0)),
        ),
        out_shape=shape_of((size, width), LOW),
        compiler_params=params(),
        name="down_grad",
        cost_estimate=cost(),
    )(half.reshape(1), active, grads)


def neighbour_kernel(parts, at_ref, *refs):
    rows_refs, refs = refs[:parts], refs[parts:]
    grad_ref, up_ref, bias_ref, own_ref, down_ref, active_ref = refs

    @pl.when(at_ref[1] == 1)
    def _():
        size = 256
        for r in range(grad_ref.shape[0] // size):
            part = slice(r * size, (r + 1) * size)
            active = gelu(up_product(rows_refs, part, up_ref[0]) + bias_ref[...])
            active_ref[part, :] = active.astype(LOW)
        down = dot_tn(active_ref[...], grad_ref[...])
        down_ref[...] = (own_ref[...].astype(FULL) + down).astype(LOW)


def neighbour_down(at, rows, grads, up, bias, own, chunk=512):
    count, width = grads.shape
    half = up.shape[2] // 2
    steps = half // chunk
    return pl.pallas_call(
        functools.partial(neighbour_kernel, len(rows)),
        grid_spec=pltpu.PrefetchScalarGridSpec(
            num_scalar_prefetch=1,
            grid=(steps,),
            in_specs=[whole(part.shape) for part in rows]
            + [
                whole((count, width)),
                pl.BlockSpec((1, width, chunk), lambda i, at: (0, 0, at[0] * steps + i)),
                pl.BlockSpec((1, chunk), lambda i, at: (0, at[0] * steps + i)),
                pl.BlockSpec((chunk, width), lambda i, at: (i, 0)),
            ],
            out_specs=pl.BlockSpec((chunk, width), lambda i, at: (i, 0)),
            scratch_shapes=[pltpu.VMEM((count, chunk), LOW)],
        ),
        out_shape=shape_of((half, width), LOW),
        compiler_params=params(),
        name="neighbour_down",
        cost_estimate=cost(),
    )(at, *rows, grads, up, bias, own)


def expert_second_kernel(parts, at_ref, *refs):
    rows_refs, refs = refs[:parts], refs[parts:]
    grad_ref, down_ref, slope_ref, low_ref, bias_ref, *block_refs, product_ref = refs
    low = (dot_nt(grad_ref[...], down_ref[0]) * slope_ref[...].astype(FULL)).astype(LOW)
    low_ref[...] = low
    bias_ref[...] = jnp.sum(low.astype(FULL), axis=0, keepdims=True)
    at = 0
    for rows_ref in rows_refs:
        cols = rows_ref.shape[1]
        product_ref[at : at + cols, :] = dot_tn(rows_ref[...], low).astype(LOW)
        at += cols
    for i, block_ref in enumerate(block_refs):
        size = block_ref.shape[0]
        block_ref[...] = product_ref[pl.ds(pl.multiple_of(at_ref[i] * size, size), size), :]


def expert_second(order, rows, grads, down, slope, chunk=512):
    count, width = grads.shape
    hidden = slope.shape[1]
    blocks = len(order)
    by_chunk = pl.BlockSpec((count, chunk), lambda i, _: (0, i))
    return pl.pallas_call(
        functools.partial(expert_second_kernel, len(rows)),
        grid_spec=pltpu.PrefetchScalarGridSpec(
            num_scalar_prefetch=1,
            grid=(hidden // chunk,),
            in_specs=[whole(part.shape) for part in rows]
            + [
                whole((count, width)),
                pl.BlockSpec((1, chunk, width), lambda i, _: (0, i, 0)),
                by_chunk,
            ],
            out_specs=[by_chunk, pl.BlockSpec((1, chunk), lambda i, _: (0, i))]
            + [pl.BlockSpec((width // blocks, chunk), lambda i, _: (0, i))] * blocks,
            scratch_shapes=[pltpu.VMEM((width, chunk), LOW)],
        ),
        out_shape=[shape_of((count, hidden), LOW), shape_of((1, hidden), FULL)]
        + [shape_of((width // blocks, hidden), LOW)] * blocks,
        compiler_params=params(),
        name="expert_second",
        cost_estimate=cost(),
    )(jnp.stack(order).astype(jnp.int32), *rows, grads, down, slope)


def expert_back_kernel(low_ref, up_ref, out_ref):
    out_ref[...] = dot_nt(low_ref[...], up_ref[0]).astype(LOW)


def expert_back(low, up, rows=256):
    count, hidden = low.shape
    width = up.shape[1]
    return pl.pallas_call(
        expert_back_kernel,
        grid=(count // rows,),
        in_specs=[pl.BlockSpec((rows, hidden), lambda i: (i, 0)), whole((1, width, hidden))],
        out_specs=pl.BlockSpec((rows, width), lambda i: (i, 0)),
        out_shape=shape_of((count, width), LOW),
        compiler_params=params(),
        name="expert_back",
        cost_estimate=cost(),
    )(low, up)


def expert_out_kernel(active_ref, down_ref, bias_ref, out_ref):
    out_ref[...] = (dot_nn(active_ref[...], down_ref[0]) + bias_ref[...]).astype(LOW)


def expert_out(active, down, bias, rows=256):
    count, hidden = active.shape
    width = down.shape[2]
    return pl.pallas_call(
        expert_out_kernel,
        grid=(count // rows,),
        in_specs=[
            pl.BlockSpec((rows, hidden), lambda i: (i, 0)),
            whole((1, hidden, width)),
            whole((1, width)),
        ],
        out_specs=pl.BlockSpec((rows, width), lambda i: (i, 0)),
        out_shape=shape_of((count, width), LOW),
        compiler_params=params(),
        name="expert_out",
        cost_estimate=cost(),
    )(active, down, bias)


def middle_back_kernel(
    core_ref,
    slot_ref,
    slotted_ref,
    hidden_ref,
    cotangent_ref,
    gain_ref,
    weight_ref,
    attended_ref,
    hidden_grad_ref,
    attended_grad_ref,
    kept_ref,
    sent_ref,
    sums_ref,
    total_ref,
):
    step = pl.program_id(0)
    grad = picked(slot_ref, slotted_ref[...])
    xhat, inverse = normed(hidden_ref[...])
    hidden_grad = cotangent_ref[...].astype(FULL) + norm_back(grad, gain_ref[...], xhat, inverse)
    hidden_grad_ref[...] = hidden_grad
    low = hidden_grad.astype(LOW)
    attended_grad_ref[...] = dot_nt(low, weight_ref[...]).astype(LOW)
    weight_grad = dot_tn(attended_ref[...], low)
    sums = [
        jnp.sum(grad * xhat, axis=0, keepdims=True),
        jnp.sum(grad, axis=0, keepdims=True),
        jnp.sum(hidden_grad, axis=0, keepdims=True),
    ]

    @pl.when(step == 0)
    def _():
        total_ref[...] = weight_grad
        for i, part in enumerate(sums):
            sums_ref[i : i + 1, :] = part

    @pl.when(step > 0)
    def _():
        total_ref[...] += weight_grad
        for i, part in enumerate(sums):
            sums_ref[i : i + 1, :] += part

    @pl.when(step == pl.num_programs(0) - 1)
    def _():
        cores_apart(total_ref, core_ref[0], kept_ref, sent_ref)


def middle_back(
    core, slot_column, slotted, hidden, cotangent, gain, weight, attended, rows=256
):
    count, width = hidden.shape
    wide = lax.axis_size("wide")
    part = (wide // 2, width // wide, width)
    by_row = pl.BlockSpec((rows, width), lambda i, _: (i, 0))
    return pl.pallas_call(
        middle_back_kernel,
        grid_spec=pltpu.PrefetchScalarGridSpec(
            num_scalar_prefetch=1,
            grid=(count // rows,),
            in_specs=[
                pl.BlockSpec((rows, 1), lambda i, _: (i, 0)),
                whole(slotted.shape),
                by_row,
                by_row,
                whole((1, width)),
                whole(weight.shape),
                by_row,
            ],
            out_specs=[by_row, by_row, whole(part), whole(part), whole((8, width))],
            scratch_shapes=[pltpu.VMEM(weight.shape, FULL)],
        ),
        out_shape=[
            shape_of((count, width), FULL),
            shape_of((count, width), LOW),
            shape_of(part, LOW),
            shape_of(part, LOW),
            shape_of((8, width), FULL),
        ],
        compiler_params=params(),
        name="middle_back",
        cost_estimate=cost(),
    )(core, slot_column, slotted, hidden, cotangent, gain, weight, attended)


def project_grad_kernel(core_ref, normed_ref, stacked_ref, kept_ref, sent_ref, product_ref):
    product_ref[...] = dot_tn(normed_ref[...], stacked_ref[0])
    cores_apart(product_ref, core_ref[0], kept_ref, sent_ref)


def project_grad(core, normed_low, stacked):
    count, width = normed_low.shape
    chunk = stacked.shape[2]
    wide = lax.axis_size("wide")
    part = (wide // 2, width // wide)
    half = pl.BlockSpec(part + (chunk,), lambda i, _: (0, 0, i))
    return pl.pallas_call(
        project_grad_kernel,
        grid_spec=pltpu.PrefetchScalarGridSpec(
            num_scalar_prefetch=1,
            grid=(3,),
            in_specs=[
                whole((count, width)),
                pl.BlockSpec((1, count, chunk), lambda i, _: (i, 0, 0)),
            ],
            out_specs=[half, half],
            scratch_shapes=[pltpu.VMEM((width, chunk), FULL)],
        ),
        out_shape=[shape_of(part + (3 * chunk,), LOW)] * 2,
        compiler_params=params(),
        name="project_grad",
        cost_estimate=cost(),
    )(core, normed_low, stacked)


def first_back_kernel(
    parts, weight_ref, tokens_ref, gain_ref, hidden_grad_ref, *refs
):
    stacked_refs, (out_ref, sums_ref) = refs[:parts], refs[parts:]
    step = pl.program_id(0)
    width = tokens_ref.shape[1]
    cols = width // parts
    grad = None
    for part, stacked_ref in enumerate(stacked_refs):
        for i in range(3):
            at = i * width + part * cols
            more = dot_nt(stacked_ref[i], weight_ref[:, at : at + cols])
            grad = more if grad is None else grad + more
    xhat, inverse = normed(tokens_ref[...].astype(FULL))
    out_ref[...] = (
        hidden_grad_ref[...] + norm_back(grad, gain_ref[...], xhat, inverse)
    ).astype(LOW)
    sums = [
        jnp.sum(grad * xhat, axis=0, keepdims=True),
        jnp.sum(grad, axis=0, keepdims=True),
    ]

    @pl.when(step == 0)
    def _():
        for i, part in enumerate(sums):
            sums_ref[i : i + 1, :] = part

    @pl.when(step > 0)
    def _():
        for i, part in enumerate(sums):
            sums_ref[i : i + 1, :] += part


def first_back(stacked, weight, tokens, gain, hidden_grad, rows=256):
    count, width = tokens.shape
    by_row = pl.BlockSpec((rows, width), lambda i: (i, 0))
    return pl.pallas_call(
        functools.partial(first_back_kernel, len(stacked)),
        grid=(count // rows,),
        in_specs=[whole(weight.shape), by_row, whole((1, width)), by_row]
        + [pl.BlockSpec((3, rows, part.shape[2]), lambda i: (0, i, 0)) for part in stacked],
        out_specs=[by_row, whole((8, width))],
        out_shape=[shape_of((count, width), LOW), shape_of((8, width), FULL)],
        compiler_params=params(),
        name="first_back",
        cost_estimate=cost(),
    )(weight, tokens, gain, hidden_grad, *stacked)


def merge_kernel(shape, flagged, at_ref, *refs):
    count = sum(sum(groups) for groups in shape)
    place = 0
    for out_ref, groups in zip(refs[count:], shape):
        column = 0
        for size in groups:
            total = None
            for i in range(place, place + size):
                part = refs[i][0].astype(FULL)
                if flagged[i]:
                    part = jnp.where(at_ref[count + i] == 1, part, 0.0)
                total = part if total is None else total + part
            place += size
            cols = total.shape[1]
            out_ref[:, column : column + cols] = total.astype(out_ref.dtype)
            column += cols


def merge_all(results, dtype=LOW, tile=512):
    terms = [term for groups in results for group in groups for term in group]
    flagged = [len(term) > 2 for term in terms]
    counts = [term[2] if len(term) > 2 else 1 for term in terms]
    terms = [term[:2] for term in terms]
    rows = terms[0][0].shape[1]
    widths = [sum(group[0][0].shape[2] for group in groups) for groups in results]
    tile = min(tile, rows)
    columns = sum(widths) + sum(blocks.shape[2] for blocks, _ in terms)
    while tile > 16 and tile * columns * 4 > VMEM_BYTES // 2:
        tile //= 2
    at = jnp.stack([jnp.asarray(x, jnp.int32) for x in [index for _, index in terms] + counts])
    return pl.pallas_call(
        functools.partial(
            merge_kernel, [[len(group) for group in groups] for groups in results], flagged
        ),
        grid_spec=pltpu.PrefetchScalarGridSpec(
            num_scalar_prefetch=1,
            grid=(rows // tile,),
            in_specs=[
                pl.BlockSpec((1, tile, blocks.shape[2]), lambda i, at, j=j: (at[j], i, 0))
                for j, (blocks, _) in enumerate(terms)
            ],
            out_specs=[pl.BlockSpec((tile, width), lambda i, at: (i, 0)) for width in widths],
        ),
        out_shape=[shape_of((rows, width), dtype) for width in widths],
        compiler_params=params(),
        name="merge",
        cost_estimate=cost(),
    )(at, *[blocks for blocks, _ in terms])


def merge(groups, dtype=LOW):
    return merge_all([groups], dtype)[0]


def one(values):
    return (values[None], 0)


def swap_cores(values):
    size = lax.axis_size("wide")
    return lax.ppermute(values, "wide", [(i, i ^ 1) for i in range(size)])


def finish_kernel(width, lines_ref, out_weight_ref, qkv_ref, small_ref):
    total = jnp.sum(lines_ref[...].astype(FULL), axis=0)
    half = width // 2
    out_weight_ref[...] = total[:, :width]
    for i in range(3):
        for part in range(2):
            to = (2 * i + part) * half
            at = width + (3 * part + i) * half
            qkv_ref[:, to : to + half] = total[:, at : at + half]
    small_ref[...] = total[:, 4 * width :]


def finish(lines, width):
    rows = lines.shape[1]
    columns = lines.shape[2] - 4 * width
    return pl.pallas_call(
        functools.partial(finish_kernel, width),
        out_shape=[
            shape_of((rows, width), FULL),
            shape_of((rows, 3 * width), FULL),
            shape_of((rows, columns), FULL),
        ],
        compiler_params=params(),
        name="finish",
        cost_estimate=cost(),
    )(lines)


def flat(blocks):
    return (blocks.reshape(1, -1, blocks.shape[-1]), 0)


def all_of(blocks):
    return [(blocks, i) for i in range(blocks.shape[0])]


def swap_chips(values):
    size = lax.axis_size("wide")
    groups = [list(range(core, size, 2)) for core in range(2)]
    blocks = values.reshape(size // 2, -1, values.shape[1])
    return lax.all_to_all(
        blocks, "wide", split_axis=0, concat_axis=0, tiled=True, axis_index_groups=groups
    )


def swap_narrow(values):
    blocks = values.reshape(lax.axis_size("narrow"), -1, values.shape[1])
    return lax.all_to_all(blocks, "narrow", split_axis=0, concat_axis=0, tiled=True)


def cores_apart(values_ref, core, kept_ref, sent_ref):
    chips = kept_ref.shape[0]
    rows = kept_ref.shape[1]
    for chip in range(chips):
        kept_ref[chip] = values_ref[pl.ds((2 * chip + core) * rows, rows), :].astype(LOW)
        sent_ref[chip] = values_ref[pl.ds((2 * chip + 1 - core) * rows, rows), :].astype(LOW)


def body(
    tokens,
    segment_ids,
    expert_ids,
    first_gain,
    first_shift,
    qkv_weight,
    query_bias,
    value_bias,
    out_weight,
    out_bias,
    second_gain,
    second_shift,
    up_weights,
    up_bias,
    down_weights,
    down_bias,
    cotangent,
):
    row_length, width = tokens.shape
    wide_size = lax.axis_size("wide")
    narrow_size = lax.axis_size("narrow")
    expert_total = wide_size * up_weights.shape[0]
    capacity = max(2, row_length * 5 // (4 * expert_total))
    slots = expert_total * capacity
    reach = min(REACH, row_length) // TILE + 1

    def line(vector):
        return vector.reshape(1, -1)

    def swap(rows):
        return lax.all_to_all(
            rows.reshape(expert_total, capacity, -1),
            "wide",
            split_axis=0,
            concat_axis=0,
            tiled=True,
        ).reshape(slots, -1)

    slot_line = slots_of(expert_ids.reshape(1, -1), expert_total, capacity)
    slot_column = slot_line.reshape(-1, 1)
    segment = segment_ids[0]
    opening = segment[::TILE]
    begins = jnp.sum((segment[None, :] < opening[:, None]).astype(jnp.int32), axis=1)
    counts = jnp.arange(opening.shape[0], dtype=jnp.int32) - begins // TILE + 1
    segment_column, segment_line = segment[:, None], segment[None, :]

    assert narrow_size == 4
    place = lax.axis_index("narrow")
    inward = [(0, 1), (3, 2)]
    outward = [(1, 0), (2, 3)]
    across = [(1, 2), (2, 1)]
    low_side = (place < 2).astype(jnp.int32)
    is_inner = ((place == 1) | (place == 2)).astype(jnp.int32)
    first_half = (place % 2).astype(jnp.int32)
    far, middle, near, outer = 3 * low_side, 1 + low_side, 2 - low_side, 3 - 3 * low_side
    core = (lax.axis_index("wide") % 2).astype(jnp.int32).reshape(1)

    def along(values, pairs):
        return lax.ppermute(values, "narrow", pairs)

    send_grad = dispatch(slot_line, cotangent, slots)
    got_grad = swap(send_grad)

    bias = jnp.concatenate([query_bias, jnp.zeros_like(query_bias), value_bias])
    normed_low, projected = project(
        after(tokens, send_grad), line(first_gain), line(first_shift), qkv_weight, line(bias)
    )
    attended, logs = attend(counts, projected, segment_column, segment_line, reach)
    attended, got_grad = lax.optimization_barrier((attended, got_grad))
    next_grad = along(got_grad, inward)
    hidden, send_rows = mix(
        attended,
        out_weight,
        line(out_bias),
        tokens,
        line(second_gain),
        line(second_shift),
        slot_line,
        slots,
        (width,),
    )
    got_rows = swap(send_rows)
    next_rows = along(got_rows, inward)
    rows = [got_rows]

    active, slope, down_first = expert_first(first_half, rows, got_grad, up_weights, up_bias)
    first_blocks = down_first.reshape(2, -1, width)
    active, slope = expert_first(
        1 - first_half,
        rows,
        got_grad,
        up_weights,
        up_bias,
        (active, slope),
    )
    up_low, up_bias_local, up_far, up_middle, up_near, up_outer = expert_second(
        [far, middle, near, outer], rows, after(got_grad, next_grad), down_weights, slope
    )
    from_far, from_middle, from_near = [along(up, inward) for up in (up_far, up_middle, up_near)]
    back = expert_back(up_low, up_weights)
    returned_back = swap(back)
    far_part = neighbour_down(
        jnp.stack([first_half, is_inner]),
        [next_rows],
        after(next_grad, back),
        up_weights,
        up_bias,
        down_first,
    )
    crossed = along(far_part, across).reshape(2, -1, width)
    result = expert_out(active, after(down_weights, far_part), down_bias)
    near_send = merge([[(after(first_blocks, result), low_side)]])
    near_part = along(near_send, inward)
    down_second = down_grad(1 - first_half, active, after(got_grad, near_send))
    returned = swap(after(result, down_second))
    second_blocks = down_second.reshape(2, -1, width)

    hidden_grad, attended_grad, out_weight_kept, out_weight_sent, middle_sums = middle_back(
        core,
        slot_column,
        after(returned_back, down_second),
        hidden,
        cotangent,
        line(second_gain),
        out_weight,
        attended,
    )
    out_weight_got = swap_cores(out_weight_sent)
    def heads_back(part, grad):
        return attend_back(
            counts, projected, attended, grad, logs, segment_column, segment_line, reach, part, 2
        )

    far_send = merge([[one(up_far), one(after(from_far, attended_grad))]])
    far_crossed = along(far_send, across)
    stacked_first, bias_first = heads_back(0, after(attended_grad, far_send))
    stacked_second, bias_second = heads_back(1, after(attended_grad, stacked_first))
    outer_send = merge(
        [[(second_blocks, 1 - low_side), (after(crossed, stacked_second), 1 - low_side)]]
    )
    outer_part = along(outer_send, outward)
    first_kept, first_sent = project_grad(core, normed_low, after(stacked_first, outer_send))
    first_got = swap_cores(first_sent)
    middle_send = merge([[one(up_middle), one(after(from_middle, first_sent))]])
    middle_crossed = along(middle_send, across)
    first_group = merge(
        [
            [flat(out_weight_kept), flat(out_weight_got)],
            [flat(first_kept), flat(after(first_got, middle_send))],
        ]
    )
    first_chips = swap_chips(first_group)
    up_outer_send = merge([[one(up_outer), one(after(far_crossed, first_group))]])
    up_outer_part = along(up_outer_send, outward)
    second_kept, second_sent = project_grad(
        core, normed_low, after(stacked_second, up_outer_send, returned, near_part)
    )
    second_got = swap_cores(second_sent)
    input_grad, first_sums = first_back(
        [stacked_first, stacked_second],
        qkv_weight,
        tokens,
        line(first_gain),
        after(hidden_grad, second_sent, outer_part),
    )
    vectors = jnp.concatenate(
        [
            first_sums[:2],
            jnp.concatenate([bias_first[:2], bias_second[:2]], axis=1),
            middle_sums[2:3],
            middle_sums[:2],
            first_sums[:1],
        ],
        axis=0,
    )
    columns = jnp.pad(vectors.T, ((0, 0), (0, TILE - vectors.shape[0]))).astype(LOW)
    columns = columns.reshape(wide_size // 2, 2, -1, TILE)
    vector_kept = lax.dynamic_index_in_dim(columns, core[0], 1, keepdims=False)
    vector_got = swap_cores(lax.dynamic_index_in_dim(columns, 1 - core[0], 1, keepdims=False))
    second_group = merge(
        [
            [flat(second_kept), flat(after(second_got, input_grad, first_chips, middle_crossed, from_near))],
            [flat(vector_kept), flat(vector_got)],
        ]
    )
    second_chips = swap_chips(second_group)
    output = combine(slot_column, returned, after(hidden, second_group))

    lane_rows = width // wide_size
    down_bias_local = jnp.sum(got_grad.astype(FULL), axis=0)
    expert_bias = jnp.concatenate(
        [up_bias_local.reshape(narrow_size, -1), down_bias_local.reshape(narrow_size, -1)], axis=1
    )
    own_rows = lane_rows // narrow_size
    bias_columns = -(-expert_bias.shape[1] // (own_rows * TILE)) * TILE
    expert_bias = jnp.pad(
        expert_bias, ((0, 0), (0, bias_columns * own_rows - expert_bias.shape[1]))
    ).reshape(lane_rows, bias_columns)
    down_sum = merge(
        [
            [
                (second_blocks, low_side, is_inner),
                (first_blocks, 1 - low_side, 1 - is_inner),
                one(after(near_part, output)),
                one(outer_part),
                (crossed, place - 2 + 2 * low_side),
            ]
        ],
        FULL,
    )
    own_group = merge(
        [
            all_of(first_chips),
            all_of(after(second_chips, down_sum, up_outer_part)),
            [one(expert_bias.astype(LOW))],
        ]
    )
    lines = swap_narrow(own_group)

    out_weight_grad, qkv_grad, small = finish(lines, width)
    vector_sum = small[:, : vectors.shape[0]].T
    bias_sum = small[:, TILE:].reshape(1, -1)
    up_share = up_bias.shape[1] // narrow_size
    down_share = width // narrow_size
    up_sum = merge(
        [
            [
                one(up_near) + (is_inner,),
                one(up_outer) + (1 - is_inner,),
                one(from_near),
                one(up_outer_part),
                one(middle_crossed),
            ]
        ],
        FULL,
    )
    return (
        output,
        input_grad,
        vector_sum[0],
        vector_sum[1],
        qkv_grad,
        vector_sum[2],
        vector_sum[3],
        out_weight_grad,
        vector_sum[4],
        vector_sum[5],
        vector_sum[6],
        up_sum[None],
        bias_sum[:, :up_share],
        down_sum[None],
        bias_sum[:, up_share : up_share + down_share],
    )


def solution(mesh):
    return jax.shard_map(
        body,
        mesh=mesh,
        in_specs=(
            P(("wide", "narrow"), None),
            P(("wide", "narrow"), None),
            P(("wide", "narrow"), None),
            P(),
            P(),
            P(),
            P(),
            P(),
            P(),
            P(),
            P(),
            P(),
            P("wide", None, None),
            P("wide", None),
            P("wide", None, None),
            P("wide", None),
            P(("wide", "narrow"), None),
        ),
        out_specs=(
            P(("wide", "narrow"), None),
            P(("wide", "narrow"), None),
            P(("wide", "narrow")),
            P(("wide", "narrow")),
            P(("wide", "narrow"), None),
            P(("wide", "narrow")),
            P(("wide", "narrow")),
            P(("wide", "narrow"), None),
            P(("wide", "narrow")),
            P(("wide", "narrow")),
            P(("wide", "narrow")),
            P("wide", "narrow", None),
            P("wide", "narrow"),
            P("wide", "narrow", None),
            P("wide", "narrow"),
        ),
        check_vma=False,
    )
```

```python
import functools

import jax
import jax.numpy as jnp
from jax import lax
from jax.experimental import pallas as pl
from jax.experimental.pallas import tpu as pltpu
from jax.sharding import PartitionSpec as P

HEAD_DIM = 64
EPSILON = 1e-05
MASKED = -1e30
TILE = 128
REACH = 512
LOW = jnp.bfloat16
FULL = jnp.float32
VMEM_BYTES = 56 * 2**20


def params():
    return pltpu.CompilerParams(vmem_limit_bytes=VMEM_BYTES)


def cost():
    return pl.CostEstimate(flops=1024, bytes_accessed=1024, transcendentals=0)


def shape_of(dims, dtype):
    return jax.ShapeDtypeStruct(dims, dtype)


def whole(dims):
    return pl.BlockSpec(dims, lambda *_: (0,) * len(dims))


def dot_nn(a, b):
    return jnp.dot(a, b, preferred_element_type=FULL)


def dot_nt(a, b):
    return lax.dot_general(a, b, (((1,), (1,)), ((), ())), preferred_element_type=FULL)


def dot_tn(a, b):
    return lax.dot_general(a, b, (((0,), (0,)), ((), ())), preferred_element_type=FULL)


def after(values, *others):
    return lax.optimization_barrier((values,) + others)[0]


def after2(first, *values):
    return lax.optimization_barrier(values + (first,))[:-1]


def normed(values):
    average = jnp.mean(values, axis=-1, keepdims=True)
    centred = values - average
    spread = jnp.mean(centred * centred, axis=-1, keepdims=True)
    inverse = lax.rsqrt(spread + EPSILON)
    return centred * inverse, inverse


def norm_back(grad, gain, xhat, inverse):
    scaled = grad * gain
    first = jnp.mean(scaled, axis=-1, keepdims=True)
    second = jnp.mean(scaled * xhat, axis=-1, keepdims=True)
    return inverse * (scaled - first - xhat * second)


GELU_SLOPE = 0.7978845608028654
GELU_CUBE = 0.044715 * GELU_SLOPE
LOG2_E = 1.4426950408889634


def gelu_gate(v, square):
    power = v * (-2.0 * LOG2_E * GELU_SLOPE - (2.0 * LOG2_E * GELU_CUBE) * square)
    below = 1.0 + jnp.exp2(jnp.minimum(power, 100.0))
    guess = pl.reciprocal(below, approx=True)
    return guess * (2.0 - below * guess)


def gelu(v):
    return v * gelu_gate(v, v * v)


def gelu_pair(v):
    square = v * v
    gate = gelu_gate(v, square)
    active = v * gate
    grad = gate + (active - active * gate) * (2.0 * GELU_SLOPE + (6.0 * GELU_CUBE) * square)
    return active, grad


def project_kernel(tokens_ref, gain_ref, shift_ref, weight_ref, bias_ref, normed_ref, out_ref):
    xhat, _ = normed(tokens_ref[...].astype(FULL))
    low = (xhat * gain_ref[...] + shift_ref[...]).astype(LOW)
    normed_ref[...] = low
    out_ref[...] = (dot_nn(low, weight_ref[...]) + bias_ref[...]).astype(LOW)


def project(tokens, gain, shift, weight, bias, rows=256):
    count, width = tokens.shape
    out = weight.shape[1]
    return pl.pallas_call(
        project_kernel,
        grid=(count // rows,),
        in_specs=[
            pl.BlockSpec((rows, width), lambda i: (i, 0)),
            whole((1, width)),
            whole((1, width)),
            whole((width, out)),
            whole((1, out)),
        ],
        out_specs=[
            pl.BlockSpec((rows, width), lambda i: (i, 0)),
            pl.BlockSpec((rows, out), lambda i: (i, 0)),
        ],
        out_shape=[shape_of((count, width), LOW), shape_of((count, out), LOW)],
        compiler_params=params(),
        name="project",
        cost_estimate=cost(),
    )(tokens, gain, shift, weight, bias)


def fill_mask(column_ref, line_ref, mask_ref, reach):
    blocks = line_ref.shape[1] // TILE
    key_row = lax.broadcasted_iota(jnp.int32, (TILE, TILE), 0)
    query_lane = lax.broadcasted_iota(jnp.int32, (TILE, TILE), 1)
    for i in range(blocks):
        line = line_ref[:, i * TILE : (i + 1) * TILE]
        for step in range(reach):
            j = i - (reach - 1) + step
            if j < 0:
                continue
            same = column_ref[j * TILE : (j + 1) * TILE, :] == line
            if j == i:
                same = same & (key_row <= query_lane)
            mask_ref[i, step * TILE : (step + 1) * TILE, :] = jnp.where(same, 0.0, MASKED)


def split_heads(block):
    lane = lax.broadcasted_iota(jnp.int32, block.shape, 1)
    zero = jnp.zeros_like(block)
    return jnp.concatenate(
        [jnp.where(lane < HEAD_DIM, block, zero), jnp.where(lane < HEAD_DIM, zero, block)], axis=0
    )


def join_heads(pair):
    return jnp.concatenate([pair[:HEAD_DIM, :TILE], pair[HEAD_DIM : 2 * HEAD_DIM, TILE:]], axis=0)


def twice(values):
    return jnp.concatenate([values, values], axis=1)


def attend_kernel(
    reach, count_ref, q_ref, k_ref, v_ref, column_ref, line_ref, out_ref, log_ref, mask_ref, vt_ref
):
    pairs = [slice(p * TILE, (p + 1) * TILE) for p in range(q_ref.shape[1] // TILE)]

    @pl.when(pl.program_id(0) == 0)
    def _():
        fill_mask(column_ref, line_ref, mask_ref, reach)

    for p, cols in enumerate(pairs):
        vt_ref[p, :TILE, :] = v_ref[:, cols].T
        vt_ref[p, TILE:, :] = jnp.ones((vt_ref.shape[1] - TILE, vt_ref.shape[2]), LOW)

    def block(i, carry):
        here = pl.ds(pl.multiple_of(i * TILE, TILE), TILE)
        for n in range(1, reach + 1):

            @pl.when(count_ref[i] == n)
            def _():
                window = pl.ds(pl.multiple_of((i - (n - 1)) * TILE, TILE), n * TILE)
                mask = twice(mask_ref[i, (reach - n) * TILE :, :])
                queries = [split_heads(q_ref[here, c] * jnp.asarray(HEAD_DIM**-0.5, LOW)) for c in pairs]
                scores = [dot_nt(k_ref[window, c], q) + mask for c, q in zip(pairs, queries)]
                highest = [jnp.max(s, axis=0, keepdims=True) for s in scores]
                weights = [jnp.exp(s - h).astype(LOW) for s, h in zip(scores, highest)]
                mixed = [dot_nn(vt_ref[p, :, window], w) for p, w in enumerate(weights)]
                for p, cols in enumerate(pairs):
                    totals = mixed[p][TILE : TILE + 1, :]
                    value = mixed[p][:TILE, :] * (1.0 / totals)
                    out_ref[here, cols] = join_heads(value).T.astype(LOW)
                    logs = highest[p] + jnp.log(totals)
                    log_ref[p, 0:1, here] = logs[:, :TILE]
                    log_ref[p, 1:2, here] = logs[:, TILE:]

        return carry

    lax.fori_loop(0, q_ref.shape[0] // TILE, block, 0)


def attend(counts, projected, column, line, reach, group=8):
    rows = projected.shape[0]
    width = projected.shape[1] // 3
    steps = width // (TILE * group)
    cols = TILE * group
    return pl.pallas_call(
        functools.partial(attend_kernel, reach),
        grid_spec=pltpu.PrefetchScalarGridSpec(
            num_scalar_prefetch=1,
            grid=(steps,),
            in_specs=[
                pl.BlockSpec((rows, cols), lambda j, _: (0, j)),
                pl.BlockSpec((rows, cols), lambda j, _: (0, j + steps)),
                pl.BlockSpec((rows, cols), lambda j, _: (0, j + 2 * steps)),
                whole((rows, 1)),
                whole((1, rows)),
            ],
            out_specs=[
                pl.BlockSpec((rows, cols), lambda j, _: (0, j)),
                pl.BlockSpec((group, 8, rows), lambda j, _: (j, 0, 0)),
            ],
            scratch_shapes=[
                pltpu.VMEM((rows // TILE, reach * TILE, TILE), FULL),
                pltpu.VMEM((group, TILE + 16, rows), LOW),
            ],
        ),
        out_shape=[shape_of((rows, width), LOW), shape_of((width // TILE, 8, rows), FULL)],
        compiler_params=params(),
        name="attend",
        cost_estimate=cost(),
    )(counts, projected, projected, projected, column, line)


def attend_back_kernel(
    reach,
    count_ref,
    q_ref,
    k_ref,
    v_ref,
    out_ref,
    grad_ref,
    log_ref,
    column_ref,
    line_ref,
    back_ref,
    bias_ref,
    mask_ref,
    kt_ref,
    dk_ref,
    dv_ref,
):
    pairs = [slice(p * TILE, (p + 1) * TILE) for p in range(q_ref.shape[1] // TILE)]

    @pl.when(pl.program_id(0) == 0)
    def _():
        fill_mask(column_ref, line_ref, mask_ref, reach)

    scale = HEAD_DIM**-0.5
    for p, cols in enumerate(pairs):
        kt_ref[p] = k_ref[:, cols].T
    dk_ref[...] = jnp.zeros_like(dk_ref)
    dv_ref[...] = jnp.zeros_like(dv_ref)

    def block(i, carry):
        here = pl.ds(pl.multiple_of(i * TILE, TILE), TILE)
        for n in range(1, reach + 1):

            @pl.when(count_ref[i] == n)
            def _():
                window = pl.ds(pl.multiple_of((i - (n - 1)) * TILE, TILE), n * TILE)
                mask = twice(mask_ref[i, (reach - n) * TILE :, :])
                queries = [split_heads(q_ref[here, c] * jnp.asarray(scale, LOW)) for c in pairs]
                grads = [split_heads(grad_ref[here, c]) for c in pairs]
                dots = []
                logs = []
                for p, c in enumerate(pairs):
                    product = (grad_ref[here, c].astype(FULL) * out_ref[here, c].astype(FULL)).T
                    dots.append(
                        jnp.concatenate(
                            [
                                jnp.sum(product[:HEAD_DIM, :], axis=0, keepdims=True),
                                jnp.sum(product[HEAD_DIM:, :], axis=0, keepdims=True),
                            ],
                            axis=1,
                        )
                    )
                    logs.append(
                        jnp.concatenate([log_ref[p, 0:1, here], log_ref[p, 1:2, here]], axis=1)
                    )
                scores = [dot_nt(k_ref[window, c], q) + mask for c, q in zip(pairs, queries)]
                prob_grad = [dot_nt(v_ref[window, c], g) for c, g in zip(pairs, grads)]
                exact = [jnp.exp(s - l) for s, l in zip(scores, logs)]
                score_grad = [
                    (e * (g - d)).astype(LOW) for e, g, d in zip(exact, prob_grad, dots)
                ]
                for p, c in enumerate(pairs):
                    dv_ref[window, c] += dot_nn(exact[p].astype(LOW), grads[p])
                    dk_ref[window, c] += dot_nn(score_grad[p], queries[p])
                    back = join_heads(dot_nn(kt_ref[p, :, window], score_grad[p])) * scale
                    back_ref[0, here, c] = back.T.astype(LOW)

        return carry

    lax.fori_loop(0, q_ref.shape[0] // TILE, block, 0)
    back_ref[1, :, :] = dk_ref[...].astype(LOW)
    value_grad = dv_ref[...].astype(LOW)
    back_ref[2, :, :] = value_grad
    bias_ref[0:1, :] = jnp.sum(back_ref[0, :, :].astype(FULL), axis=0, keepdims=True)
    bias_ref[1:2, :] = jnp.sum(value_grad.astype(FULL), axis=0, keepdims=True)


def attend_back(counts, projected, attended, grad, logs, column, line, reach, part, parts):
    rows = projected.shape[0]
    width = projected.shape[1] // 3
    cols = width // parts
    group = cols // TILE
    return pl.pallas_call(
        functools.partial(attend_back_kernel, reach),
        grid_spec=pltpu.PrefetchScalarGridSpec(
            num_scalar_prefetch=1,
            grid=(1,),
            in_specs=[
                pl.BlockSpec((rows, cols), lambda j, _: (0, part)),
                pl.BlockSpec((rows, cols), lambda j, _: (0, part + parts)),
                pl.BlockSpec((rows, cols), lambda j, _: (0, part + 2 * parts)),
                pl.BlockSpec((rows, cols), lambda j, _: (0, part)),
                pl.BlockSpec((rows, cols), lambda j, _: (0, part)),
                pl.BlockSpec((group, 8, rows), lambda j, _: (part, 0, 0)),
                whole((rows, 1)),
                whole((1, rows)),
            ],
            out_specs=[whole((3, rows, cols)), whole((8, cols))],
            scratch_shapes=[
                pltpu.VMEM((rows // TILE, reach * TILE, TILE), FULL),
                pltpu.VMEM((group, TILE, rows), LOW),
                pltpu.VMEM((rows, cols), FULL),
                pltpu.VMEM((rows, cols), FULL),
            ],
        ),
        out_shape=[shape_of((3, rows, cols), LOW), shape_of((8, cols), FULL)],
        compiler_params=params(),
        name="attend_back",
        cost_estimate=cost(),
    )(counts, projected, projected, projected, attended, grad, logs, column, line)


def slots_kernel(experts, capacity, chosen_ref, out_ref):
    count = chosen_ref.shape[1]
    place = lax.broadcasted_iota(jnp.int32, (experts, count), 0)
    mine = place == chosen_ref[...]
    earlier = lax.broadcasted_iota(jnp.int32, (count, count), 0) < lax.broadcasted_iota(
        jnp.int32, (count, count), 1
    )
    before = dot_nn(one_hot(mine), one_hot(earlier))
    base = (place * capacity).astype(FULL)
    out_ref[...] = jnp.sum(jnp.where(mine, before + base, 0.0), axis=0, keepdims=True).astype(
        jnp.int32
    )


def slots_of(chosen, experts, capacity):
    return pl.pallas_call(
        functools.partial(slots_kernel, experts, capacity),
        out_shape=shape_of(chosen.shape, jnp.int32),
        compiler_params=params(),
        name="slots",
        cost_estimate=cost(),
    )(chosen)


def one_hot(hit):
    return jnp.where(hit, 1.0, 0.0).astype(LOW)


def dispatch_kernel(slot_ref, rows_ref, out_ref):
    tile = out_ref.shape[0]
    place = pl.program_id(0) * tile + lax.broadcasted_iota(jnp.int32, (tile, slot_ref.shape[1]), 0)
    out_ref[...] = dot_nn(one_hot(place == slot_ref[...]), rows_ref[...]).astype(LOW)


def dispatch(slot_line, rows, slots, tile=256):
    count, width = rows.shape
    return pl.pallas_call(
        dispatch_kernel,
        grid=(slots // tile,),
        in_specs=[whole((1, count)), whole((count, width))],
        out_specs=pl.BlockSpec((tile, width), lambda i: (i, 0)),
        out_shape=shape_of((slots, width), LOW),
        compiler_params=params(),
        name="dispatch",
        cost_estimate=cost(),
    )(slot_line, rows)


def picked(slot_ref, slotted):
    lane = lax.broadcasted_iota(jnp.int32, (slot_ref.shape[0], slotted.shape[0]), 1)
    return dot_nn(one_hot(lane == slot_ref[...]), slotted)


def combine_kernel(slot_ref, slotted_ref, hidden_ref, out_ref):
    out_ref[...] = (hidden_ref[...] + picked(slot_ref, slotted_ref[...])).astype(LOW)


def combine(slot_column, slotted, hidden, rows=256):
    count, width = hidden.shape
    return pl.pallas_call(
        combine_kernel,
        grid=(count // rows,),
        in_specs=[
            pl.BlockSpec((rows, 1), lambda i: (i, 0)),
            whole(slotted.shape),
            pl.BlockSpec((rows, width), lambda i: (i, 0)),
        ],
        out_specs=pl.BlockSpec((rows, width), lambda i: (i, 0)),
        out_shape=shape_of((count, width), LOW),
        compiler_params=params(),
        name="combine",
        cost_estimate=cost(),
    )(slot_column, slotted, hidden)


def mix_kernel(
    tiles,
    attended_ref,
    weight_ref,
    bias_ref,
    tokens_ref,
    gain_ref,
    shift_ref,
    slot_ref,
    hidden_ref,
    *refs,
):
    *send_refs, rows_ref = refs
    step = pl.program_id(0)
    size = attended_ref.shape[0]

    @pl.when(step < tiles)
    def _():
        branch = dot_nn(attended_ref[...], weight_ref[...]) + bias_ref[...]
        hidden = tokens_ref[...].astype(FULL) + branch
        hidden_ref[...] = hidden
        xhat, _ = normed(hidden)
        rows_ref[pl.ds(pl.multiple_of(step * size, size), size), :] = (
            xhat * gain_ref[...] + shift_ref[...]
        ).astype(LOW)

    @pl.when(step >= tiles)
    def _():
        tile = send_refs[0].shape[0]
        place = (step - tiles) * tile + lax.broadcasted_iota(
            jnp.int32, (tile, slot_ref.shape[1]), 0
        )
        spread = dot_nn(one_hot(place == slot_ref[...]), rows_ref[...]).astype(LOW)
        at = 0
        for send_ref in send_refs:
            cols = send_ref.shape[1]
            send_ref[...] = spread[:, at : at + cols]
            at += cols


def mix(attended, weight, bias, tokens, gain, shift, slot_line, slots, sizes, rows=256, tile=256):
    count, width = tokens.shape
    tiles = count // rows
    by_row = pl.BlockSpec((rows, width), lambda i: (jnp.minimum(i, tiles - 1), 0))
    return pl.pallas_call(
        functools.partial(mix_kernel, tiles),
        grid=(tiles + slots // tile,),
        in_specs=[
            by_row,
            whole(weight.shape),
            whole((1, width)),
            by_row,
            whole((1, width)),
            whole((1, width)),
            whole((1, count)),
        ],
        out_specs=[by_row]
        + [pl.BlockSpec((tile, cols), lambda i: (jnp.maximum(i - tiles, 0), 0)) for cols in sizes],
        out_shape=[shape_of((count, width), FULL)]
        + [shape_of((slots, cols), LOW) for cols in sizes],
        scratch_shapes=[pltpu.VMEM((count, width), LOW)],
        compiler_params=params(),
        name="mix",
        cost_estimate=cost(),
    )(attended, weight, bias, tokens, gain, shift, slot_line)


def up_product(rows_refs, part, up):
    total = None
    at = 0
    for rows_ref in rows_refs:
        cols = rows_ref.shape[1]
        more = dot_nn(rows_ref[part, :], up[at : at + cols, :])
        total = more if total is None else total + more
        at += cols
    return total


def expert_first_kernel(steps, at_ref, rows_ref, grad_ref, up_ref, bias_ref, *refs):
    active_ref, slope_ref, down_ref = refs
    size = 256
    for r in range(grad_ref.shape[0] // size):
        part = slice(r * size, (r + 1) * size)
        active, slope = gelu_pair(dot_nn(rows_ref[part, :], up_ref[0]) + bias_ref[...])
        active_ref[part, :] = active.astype(LOW)
        slope_ref[part, :] = slope.astype(LOW)

    @pl.when(pl.program_id(0) < steps)
    def _():
        down_ref[...] = dot_tn(active_ref[...], grad_ref[...]).astype(LOW)


def expert_first(half, rows, grads, up, bias, chunk=512):
    count, width = grads.shape
    hidden = up.shape[2]
    steps = hidden // (2 * chunk)

    def chunk_of(i, at):
        return (at[0] + i // steps) % 2 * steps + i % steps

    by_chunk = pl.BlockSpec((count, chunk), lambda i, at: (0, chunk_of(i, at)))
    return pl.pallas_call(
        functools.partial(expert_first_kernel, steps),
        grid_spec=pltpu.PrefetchScalarGridSpec(
            num_scalar_prefetch=1,
            grid=(2 * steps,),
            in_specs=[
                whole((count, width)),
                whole((count, width)),
                pl.BlockSpec((1, width, chunk), lambda i, at: (0, 0, chunk_of(i, at))),
                pl.BlockSpec((1, chunk), lambda i, at: (0, chunk_of(i, at))),
            ],
            out_specs=[
                by_chunk,
                by_chunk,
                pl.BlockSpec((chunk, width), lambda i, at: (jnp.minimum(i, steps - 1), 0)),
            ],
        ),
        out_shape=[
            shape_of((count, hidden), LOW),
            shape_of((count, hidden), LOW),
            shape_of((hidden // 2, width), LOW),
        ],
        compiler_params=params(),
        name="expert_first",
        cost_estimate=cost(),
    )(half.reshape(1), rows, grads, up, bias)


def down_grad_kernel(at_ref, active_ref, grad_ref, out_ref):
    out_ref[...] = dot_tn(active_ref[...], grad_ref[...]).astype(LOW)


def down_grad(half, active, grads, chunk=512):
    count, width = grads.shape
    size = active.shape[1] // 2
    steps = size // chunk
    return pl.pallas_call(
        down_grad_kernel,
        grid_spec=pltpu.PrefetchScalarGridSpec(
            num_scalar_prefetch=1,
            grid=(steps,),
            in_specs=[
                pl.BlockSpec((count, chunk), lambda i, at: (0, at[0] * steps + i)),
                whole((count, width)),
            ],
            out_specs=pl.BlockSpec((chunk, width), lambda i, at: (i, 0)),
        ),
        out_shape=shape_of((size, width), LOW),
        compiler_params=params(),
        name="down_grad",
        cost_estimate=cost(),
    )(half.reshape(1), active, grads)


def neighbour_kernel(parts, at_ref, *refs):
    rows_refs, refs = refs[:parts], refs[parts:]
    grad_ref, up_ref, bias_ref, own_ref, down_ref, active_ref = refs

    @pl.when(at_ref[1] == 1)
    def _():
        size = 256
        for r in range(grad_ref.shape[0] // size):
            part = slice(r * size, (r + 1) * size)
            active = gelu(up_product(rows_refs, part, up_ref[0]) + bias_ref[...])
            active_ref[part, :] = active.astype(LOW)
        down = dot_tn(active_ref[...], grad_ref[...])
        down_ref[...] = (own_ref[...].astype(FULL) + down).astype(LOW)


def neighbour_down(at, rows, grads, up, bias, own, chunk=512):
    count, width = grads.shape
    half = up.shape[2] // 2
    steps = half // chunk
    return pl.pallas_call(
        functools.partial(neighbour_kernel, len(rows)),
        grid_spec=pltpu.PrefetchScalarGridSpec(
            num_scalar_prefetch=1,
            grid=(steps,),
            in_specs=[whole(part.shape) for part in rows]
            + [
                whole((count, width)),
                pl.BlockSpec((1, width, chunk), lambda i, at: (0, 0, at[0] * steps + i)),
                pl.BlockSpec((1, chunk), lambda i, at: (0, at[0] * steps + i)),
                pl.BlockSpec((chunk, width), lambda i, at: (i, 0)),
            ],
            out_specs=pl.BlockSpec((chunk, width), lambda i, at: (i, 0)),
            scratch_shapes=[pltpu.VMEM((count, chunk), LOW)],
        ),
        out_shape=shape_of((half, width), LOW),
        compiler_params=params(),
        name="neighbour_down",
        cost_estimate=cost(),
    )(at, *rows, grads, up, bias, own)


def expert_second_kernel(parts, at_ref, *refs):
    rows_refs, refs = refs[:parts], refs[parts:]
    grad_ref, down_ref, slope_ref, low_ref, bias_ref, *block_refs, product_ref = refs
    low = (dot_nt(grad_ref[...], down_ref[0]) * slope_ref[...].astype(FULL)).astype(LOW)
    low_ref[...] = low
    bias_ref[...] = jnp.sum(low.astype(FULL), axis=0, keepdims=True)
    at = 0
    for rows_ref in rows_refs:
        cols = rows_ref.shape[1]
        product_ref[at : at + cols, :] = dot_tn(rows_ref[...], low).astype(LOW)
        at += cols
    for i, block_ref in enumerate(block_refs):
        size = block_ref.shape[0]
        block_ref[...] = product_ref[pl.ds(pl.multiple_of(at_ref[i] * size, size), size), :]


def expert_second(order, rows, grads, down, slope, chunk=512):
    count, width = grads.shape
    hidden = slope.shape[1]
    blocks = len(order)
    by_chunk = pl.BlockSpec((count, chunk), lambda i, _: (0, i))
    return pl.pallas_call(
        functools.partial(expert_second_kernel, len(rows)),
        grid_spec=pltpu.PrefetchScalarGridSpec(
            num_scalar_prefetch=1,
            grid=(hidden // chunk,),
            in_specs=[whole(part.shape) for part in rows]
            + [
                whole((count, width)),
                pl.BlockSpec((1, chunk, width), lambda i, _: (0, i, 0)),
                by_chunk,
            ],
            out_specs=[by_chunk, pl.BlockSpec((1, chunk), lambda i, _: (0, i))]
            + [pl.BlockSpec((width // blocks, chunk), lambda i, _: (0, i))] * blocks,
            scratch_shapes=[pltpu.VMEM((width, chunk), LOW)],
        ),
        out_shape=[shape_of((count, hidden), LOW), shape_of((1, hidden), FULL)]
        + [shape_of((width // blocks, hidden), LOW)] * blocks,
        compiler_params=params(),
        name="expert_second",
        cost_estimate=cost(),
    )(jnp.stack(order).astype(jnp.int32), *rows, grads, down, slope)


def expert_back_kernel(low_ref, up_ref, out_ref):
    out_ref[...] = dot_nt(low_ref[...], up_ref[0]).astype(LOW)


def expert_back(low, up, rows=256):
    count, hidden = low.shape
    width = up.shape[1]
    return pl.pallas_call(
        expert_back_kernel,
        grid=(count // rows,),
        in_specs=[pl.BlockSpec((rows, hidden), lambda i: (i, 0)), whole((1, width, hidden))],
        out_specs=pl.BlockSpec((rows, width), lambda i: (i, 0)),
        out_shape=shape_of((count, width), LOW),
        compiler_params=params(),
        name="expert_back",
        cost_estimate=cost(),
    )(low, up)


def expert_out_kernel(active_ref, down_ref, bias_ref, out_ref):
    out_ref[...] = (dot_nn(active_ref[...], down_ref[0]) + bias_ref[...]).astype(LOW)


def expert_out(active, down, bias, rows=256):
    count, hidden = active.shape
    width = down.shape[2]
    return pl.pallas_call(
        expert_out_kernel,
        grid=(count // rows,),
        in_specs=[
            pl.BlockSpec((rows, hidden), lambda i: (i, 0)),
            whole((1, hidden, width)),
            whole((1, width)),
        ],
        out_specs=pl.BlockSpec((rows, width), lambda i: (i, 0)),
        out_shape=shape_of((count, width), LOW),
        compiler_params=params(),
        name="expert_out",
        cost_estimate=cost(),
    )(active, down, bias)


def middle_back_kernel(
    core_ref,
    slot_ref,
    slotted_ref,
    hidden_ref,
    cotangent_ref,
    gain_ref,
    weight_ref,
    attended_ref,
    hidden_grad_ref,
    attended_grad_ref,
    kept_ref,
    sent_ref,
    sums_ref,
    total_ref,
):
    step = pl.program_id(0)
    grad = picked(slot_ref, slotted_ref[...])
    xhat, inverse = normed(hidden_ref[...])
    hidden_grad = cotangent_ref[...].astype(FULL) + norm_back(grad, gain_ref[...], xhat, inverse)
    hidden_grad_ref[...] = hidden_grad
    low = hidden_grad.astype(LOW)
    attended_grad_ref[...] = dot_nt(low, weight_ref[...]).astype(LOW)
    weight_grad = dot_tn(attended_ref[...], low)
    sums = [
        jnp.sum(grad * xhat, axis=0, keepdims=True),
        jnp.sum(grad, axis=0, keepdims=True),
        jnp.sum(hidden_grad, axis=0, keepdims=True),
    ]

    @pl.when(step == 0)
    def _():
        total_ref[...] = weight_grad
        for i, part in enumerate(sums):
            sums_ref[i : i + 1, :] = part

    @pl.when(step > 0)
    def _():
        total_ref[...] += weight_grad
        for i, part in enumerate(sums):
            sums_ref[i : i + 1, :] += part

    @pl.when(step == pl.num_programs(0) - 1)
    def _():
        cores_apart(total_ref, core_ref[0], kept_ref, sent_ref)


def middle_back(
    core, slot_column, slotted, hidden, cotangent, gain, weight, attended, rows=256
):
    count, width = hidden.shape
    wide = lax.axis_size("wide")
    part = (wide // 2, width // wide, width)
    by_row = pl.BlockSpec((rows, width), lambda i, _: (i, 0))
    return pl.pallas_call(
        middle_back_kernel,
        grid_spec=pltpu.PrefetchScalarGridSpec(
            num_scalar_prefetch=1,
            grid=(count // rows,),
            in_specs=[
                pl.BlockSpec((rows, 1), lambda i, _: (i, 0)),
                whole(slotted.shape),
                by_row,
                by_row,
                whole((1, width)),
                whole(weight.shape),
                by_row,
            ],
            out_specs=[by_row, by_row, whole(part), whole(part), whole((8, width))],
            scratch_shapes=[pltpu.VMEM(weight.shape, FULL)],
        ),
        out_shape=[
            shape_of((count, width), FULL),
            shape_of((count, width), LOW),
            shape_of(part, LOW),
            shape_of(part, LOW),
            shape_of((8, width), FULL),
        ],
        compiler_params=params(),
        name="middle_back",
        cost_estimate=cost(),
    )(core, slot_column, slotted, hidden, cotangent, gain, weight, attended)


def project_grad_kernel(core_ref, normed_ref, stacked_ref, kept_ref, sent_ref, product_ref):
    product_ref[...] = dot_tn(normed_ref[...], stacked_ref[0])
    cores_apart(product_ref, core_ref[0], kept_ref, sent_ref)


def project_grad(core, normed_low, stacked):
    count, width = normed_low.shape
    chunk = stacked.shape[2]
    wide = lax.axis_size("wide")
    part = (wide // 2, width // wide)
    half = pl.BlockSpec(part + (chunk,), lambda i, _: (0, 0, i))
    return pl.pallas_call(
        project_grad_kernel,
        grid_spec=pltpu.PrefetchScalarGridSpec(
            num_scalar_prefetch=1,
            grid=(3,),
            in_specs=[
                whole((count, width)),
                pl.BlockSpec((1, count, chunk), lambda i, _: (i, 0, 0)),
            ],
            out_specs=[half, half],
            scratch_shapes=[pltpu.VMEM((width, chunk), FULL)],
        ),
        out_shape=[shape_of(part + (3 * chunk,), LOW)] * 2,
        compiler_params=params(),
        name="project_grad",
        cost_estimate=cost(),
    )(core, normed_low, stacked)


def first_back_kernel(
    parts, weight_ref, tokens_ref, gain_ref, hidden_grad_ref, *refs
):
    stacked_refs, (out_ref, sums_ref) = refs[:parts], refs[parts:]
    step = pl.program_id(0)
    width = tokens_ref.shape[1]
    cols = width // parts
    grad = None
    for part, stacked_ref in enumerate(stacked_refs):
        for i in range(3):
            at = i * width + part * cols
            more = dot_nt(stacked_ref[i], weight_ref[:, at : at + cols])
            grad = more if grad is None else grad + more
    xhat, inverse = normed(tokens_ref[...].astype(FULL))
    out_ref[...] = (
        hidden_grad_ref[...] + norm_back(grad, gain_ref[...], xhat, inverse)
    ).astype(LOW)
    sums = [
        jnp.sum(grad * xhat, axis=0, keepdims=True),
        jnp.sum(grad, axis=0, keepdims=True),
    ]

    @pl.when(step == 0)
    def _():
        for i, part in enumerate(sums):
            sums_ref[i : i + 1, :] = part

    @pl.when(step > 0)
    def _():
        for i, part in enumerate(sums):
            sums_ref[i : i + 1, :] += part


def first_back(stacked, weight, tokens, gain, hidden_grad, rows=256):
    count, width = tokens.shape
    by_row = pl.BlockSpec((rows, width), lambda i: (i, 0))
    return pl.pallas_call(
        functools.partial(first_back_kernel, len(stacked)),
        grid=(count // rows,),
        in_specs=[whole(weight.shape), by_row, whole((1, width)), by_row]
        + [pl.BlockSpec((3, rows, part.shape[2]), lambda i: (0, i, 0)) for part in stacked],
        out_specs=[by_row, whole((8, width))],
        out_shape=[shape_of((count, width), LOW), shape_of((8, width), FULL)],
        compiler_params=params(),
        name="first_back",
        cost_estimate=cost(),
    )(weight, tokens, gain, hidden_grad, *stacked)


def merge_kernel(shape, flagged, at_ref, *refs):
    count = sum(sum(groups) for groups in shape)
    place = 0
    for out_ref, groups in zip(refs[count:], shape):
        column = 0
        for size in groups:
            total = None
            for i in range(place, place + size):
                part = refs[i][0].astype(FULL)
                if flagged[i]:
                    part = jnp.where(at_ref[count + i] == 1, part, 0.0)
                total = part if total is None else total + part
            place += size
            cols = total.shape[1]
            out_ref[:, column : column + cols] = total.astype(out_ref.dtype)
            column += cols


def merge_all(results, dtype=LOW, tile=512):
    terms = [term for groups in results for group in groups for term in group]
    flagged = [len(term) > 2 for term in terms]
    counts = [term[2] if len(term) > 2 else 1 for term in terms]
    terms = [term[:2] for term in terms]
    rows = terms[0][0].shape[1]
    widths = [sum(group[0][0].shape[2] for group in groups) for groups in results]
    tile = min(tile, rows)
    columns = sum(widths) + sum(blocks.shape[2] for blocks, _ in terms)
    while tile > 16 and tile * columns * 4 > VMEM_BYTES // 2:
        tile //= 2
    at = jnp.stack([jnp.asarray(x, jnp.int32) for x in [index for _, index in terms] + counts])
    return pl.pallas_call(
        functools.partial(
            merge_kernel, [[len(group) for group in groups] for groups in results], flagged
        ),
        grid_spec=pltpu.PrefetchScalarGridSpec(
            num_scalar_prefetch=1,
            grid=(rows // tile,),
            in_specs=[
                pl.BlockSpec((1, tile, blocks.shape[2]), lambda i, at, j=j: (at[j], i, 0))
                for j, (blocks, _) in enumerate(terms)
            ],
            out_specs=[pl.BlockSpec((tile, width), lambda i, at: (i, 0)) for width in widths],
        ),
        out_shape=[shape_of((rows, width), dtype) for width in widths],
        compiler_params=params(),
        name="merge",
        cost_estimate=cost(),
    )(at, *[blocks for blocks, _ in terms])


def merge(groups, dtype=LOW):
    return merge_all([groups], dtype)[0]


def one(values):
    return (values[None], 0)


def swap_cores(values):
    size = lax.axis_size("wide")
    return lax.ppermute(values, "wide", [(i, i ^ 1) for i in range(size)])


def finish_kernel(width, lines_ref, out_weight_ref, qkv_ref, small_ref):
    total = jnp.sum(lines_ref[...].astype(FULL), axis=0)
    half = width // 2
    out_weight_ref[...] = total[:, :width]
    for i in range(3):
        for part in range(2):
            to = (2 * i + part) * half
            at = width + (3 * part + i) * half
            qkv_ref[:, to : to + half] = total[:, at : at + half]
    small_ref[...] = total[:, 4 * width :]


def finish(lines, width):
    rows = lines.shape[1]
    columns = lines.shape[2] - 4 * width
    return pl.pallas_call(
        functools.partial(finish_kernel, width),
        out_shape=[
            shape_of((rows, width), FULL),
            shape_of((rows, 3 * width), FULL),
            shape_of((rows, columns), FULL),
        ],
        compiler_params=params(),
        name="finish",
        cost_estimate=cost(),
    )(lines)


def flat(blocks):
    return (blocks.reshape(1, -1, blocks.shape[-1]), 0)


def all_of(blocks):
    return [(blocks, i) for i in range(blocks.shape[0])]


def swap_chips(values):
    size = lax.axis_size("wide")
    groups = [list(range(core, size, 2)) for core in range(2)]
    blocks = values.reshape(size // 2, -1, values.shape[1])
    return lax.all_to_all(
        blocks, "wide", split_axis=0, concat_axis=0, tiled=True, axis_index_groups=groups
    )


def swap_narrow(values):
    blocks = values.reshape(lax.axis_size("narrow"), -1, values.shape[1])
    return lax.all_to_all(blocks, "narrow", split_axis=0, concat_axis=0, tiled=True)


def cores_apart(values_ref, core, kept_ref, sent_ref):
    chips = kept_ref.shape[0]
    rows = kept_ref.shape[1]
    for chip in range(chips):
        kept_ref[chip] = values_ref[pl.ds((2 * chip + core) * rows, rows), :].astype(LOW)
        sent_ref[chip] = values_ref[pl.ds((2 * chip + 1 - core) * rows, rows), :].astype(LOW)


def body(
    tokens,
    segment_ids,
    expert_ids,
    first_gain,
    first_shift,
    qkv_weight,
    query_bias,
    value_bias,
    out_weight,
    out_bias,
    second_gain,
    second_shift,
    up_weights,
    up_bias,
    down_weights,
    down_bias,
    cotangent,
):
    row_length, width = tokens.shape
    wide_size = lax.axis_size("wide")
    narrow_size = lax.axis_size("narrow")
    expert_total = wide_size * up_weights.shape[0]
    capacity = max(2, row_length * 5 // (4 * expert_total))
    slots = expert_total * capacity
    reach = min(REACH, row_length) // TILE + 1

    def line(vector):
        return vector.reshape(1, -1)

    def swap(rows):
        return lax.all_to_all(
            rows.reshape(expert_total, capacity, -1),
            "wide",
            split_axis=0,
            concat_axis=0,
            tiled=True,
        ).reshape(slots, -1)

    slot_line = slots_of(expert_ids.reshape(1, -1), expert_total, capacity)
    slot_column = slot_line.reshape(-1, 1)
    segment = segment_ids[0]
    opening = segment[::TILE]
    begins = jnp.sum((segment[None, :] < opening[:, None]).astype(jnp.int32), axis=1)
    counts = jnp.arange(opening.shape[0], dtype=jnp.int32) - begins // TILE + 1
    segment_column, segment_line = segment[:, None], segment[None, :]

    assert narrow_size == 4
    place = lax.axis_index("narrow")
    inward = [(0, 1), (3, 2)]
    outward = [(1, 0), (2, 3)]
    across = [(1, 2), (2, 1)]
    low_side = (place < 2).astype(jnp.int32)
    is_inner = ((place == 1) | (place == 2)).astype(jnp.int32)
    first_half = (place % 2).astype(jnp.int32)
    far, middle, near, outer = 3 * low_side, 1 + low_side, 2 - low_side, 3 - 3 * low_side
    core = (lax.axis_index("wide") % 2).astype(jnp.int32).reshape(1)

    def along(values, pairs):
        return lax.ppermute(values, "narrow", pairs)

    send_grad = dispatch(slot_line, cotangent, slots)
    got_grad = swap(send_grad)

    bias = jnp.concatenate([query_bias, jnp.zeros_like(query_bias), value_bias])
    normed_low, projected = project(
        after(tokens, send_grad), line(first_gain), line(first_shift), qkv_weight, line(bias)
    )
    attended, logs = attend(counts, projected, segment_column, segment_line, reach)
    attended, got_grad = lax.optimization_barrier((attended, got_grad))
    next_grad = along(got_grad, inward)
    hidden, send_rows = mix(
        attended,
        out_weight,
        line(out_bias),
        tokens,
        line(second_gain),
        line(second_shift),
        slot_line,
        slots,
        (width,),
    )
    got_rows = swap(send_rows)
    next_rows = along(got_rows, inward)
    rows = [got_rows]

    active, slope, down_first = expert_first(
        first_half, got_rows, got_grad, up_weights, up_bias
    )
    first_blocks = down_first.reshape(2, -1, width)
    up_low, up_bias_local, up_far, up_middle, up_near, up_outer = expert_second(
        [far, middle, near, outer], rows, after(got_grad, next_grad), down_weights, slope
    )
    from_far, from_middle, from_near = [along(up, inward) for up in (up_far, up_middle, up_near)]
    back = expert_back(up_low, up_weights)
    returned_back = swap(back)
    far_part = neighbour_down(
        jnp.stack([first_half, is_inner]),
        [next_rows],
        after(next_grad, back),
        up_weights,
        up_bias,
        down_first,
    )
    crossed = along(far_part, across).reshape(2, -1, width)
    result = expert_out(active, after(down_weights, far_part), down_bias)
    near_send = merge([[(after(first_blocks, result), low_side)]])
    near_part = along(near_send, inward)
    down_second = down_grad(1 - first_half, active, after(got_grad, near_send))
    returned = swap(after(result, down_second))
    second_blocks = down_second.reshape(2, -1, width)

    hidden_grad, attended_grad, out_weight_kept, out_weight_sent, middle_sums = middle_back(
        core,
        slot_column,
        after(returned_back, down_second),
        hidden,
        cotangent,
        line(second_gain),
        out_weight,
        attended,
    )
    out_weight_got = swap_cores(out_weight_sent)
    def heads_back(part, grad):
        return attend_back(
            counts, projected, attended, grad, logs, segment_column, segment_line, reach, part, 2
        )

    far_send = merge([[one(up_far), one(after(from_far, attended_grad))]])
    far_crossed = along(far_send, across)
    stacked_first, bias_first = heads_back(0, after(attended_grad, far_send))
    stacked_second, bias_second = heads_back(1, after(attended_grad, stacked_first))
    outer_send = merge(
        [[(second_blocks, 1 - low_side), (after(crossed, stacked_second), 1 - low_side)]]
    )
    outer_part = along(outer_send, outward)
    first_kept, first_sent = project_grad(core, normed_low, after(stacked_first, outer_send))
    first_got = swap_cores(first_sent)
    middle_send = merge([[one(up_middle), one(after(from_middle, first_sent))]])
    middle_crossed = along(middle_send, across)
    first_group = merge(
        [
            [flat(out_weight_kept), flat(out_weight_got)],
            [flat(first_kept), flat(after(first_got, middle_send))],
        ]
    )
    first_chips = swap_chips(first_group)
    up_outer_send = merge([[one(up_outer), one(after(far_crossed, first_group))]])
    up_outer_part = along(up_outer_send, outward)
    second_kept, second_sent = project_grad(
        core, normed_low, after(stacked_second, up_outer_send, returned, near_part)
    )
    second_got = swap_cores(second_sent)
    second_group = merge([[flat(second_kept), flat(after(second_got, outer_part))]])
    second_chips = swap_chips(second_group)
    input_grad, first_sums = first_back(
        [stacked_first, stacked_second],
        qkv_weight,
        tokens,
        line(first_gain),
        after(hidden_grad, second_group, first_chips),
    )
    vectors = jnp.concatenate(
        [
            first_sums[:2],
            jnp.concatenate([bias_first[:2], bias_second[:2]], axis=1),
            middle_sums[2:3],
            middle_sums[:2],
            first_sums[:1],
        ],
        axis=0,
    )
    lane_rows = width // wide_size
    down_bias_local = jnp.sum(got_grad.astype(FULL), axis=0)
    expert_bias = jnp.concatenate(
        [up_bias_local.reshape(narrow_size, -1), down_bias_local.reshape(narrow_size, -1)], axis=1
    )
    own_rows = lane_rows // narrow_size
    bias_columns = -(-expert_bias.shape[1] // (own_rows * TILE)) * TILE
    expert_bias = jnp.pad(
        expert_bias, ((0, 0), (0, bias_columns * own_rows - expert_bias.shape[1]))
    ).reshape(lane_rows, bias_columns)
    columns = jnp.pad(vectors.T, ((0, 0), (0, TILE - vectors.shape[0]))).astype(LOW)
    vector_blocks = lax.all_to_all(
        columns.reshape(wide_size, -1, TILE), "wide", split_axis=0, concat_axis=0, tiled=True
    )

    output = combine(slot_column, returned, after(hidden, input_grad))
    own_group = merge(
        [
            all_of(first_chips),
            all_of(after(second_chips, middle_crossed, from_near, up_outer_part, output)),
            all_of(vector_blocks),
            [one(expert_bias.astype(LOW))],
        ]
    )
    lines = swap_narrow(own_group)
    down_sum = merge(
        [
            [
                (second_blocks, low_side, is_inner),
                (first_blocks, 1 - low_side, 1 - is_inner),
                one(after(near_part, own_group)),
                one(outer_part),
                (crossed, place - 2 + 2 * low_side),
            ]
        ],
        FULL,
    )

    out_weight_grad, qkv_grad, small = finish(lines, width)
    vector_sum = small[:, : vectors.shape[0]].T
    bias_sum = small[:, TILE:].reshape(1, -1)
    up_share = up_bias.shape[1] // narrow_size
    down_share = width // narrow_size
    up_sum = merge(
        [
            [
                one(up_near) + (is_inner,),
                one(up_outer) + (1 - is_inner,),
                one(from_near),
                one(up_outer_part),
                one(middle_crossed),
            ]
        ],
        FULL,
    )
    return (
        output,
        input_grad,
        vector_sum[0],
        vector_sum[1],
        qkv_grad,
        vector_sum[2],
        vector_sum[3],
        out_weight_grad,
        vector_sum[4],
        vector_sum[5],
        vector_sum[6],
        up_sum[None],
        bias_sum[:, :up_share],
        down_sum[None],
        bias_sum[:, up_share : up_share + down_share],
    )


def solution(mesh):
    return jax.shard_map(
        body,
        mesh=mesh,
        in_specs=(
            P(("wide", "narrow"), None),
            P(("wide", "narrow"), None),
            P(("wide", "narrow"), None),
            P(),
            P(),
            P(),
            P(),
            P(),
            P(),
            P(),
            P(),
            P(),
            P("wide", None, None),
            P("wide", None),
            P("wide", None, None),
            P("wide", None),
            P(("wide", "narrow"), None),
        ),
        out_specs=(
            P(("wide", "narrow"), None),
            P(("wide", "narrow"), None),
            P(("wide", "narrow")),
            P(("wide", "narrow")),
            P(("wide", "narrow"), None),
            P(("wide", "narrow")),
            P(("wide", "narrow")),
            P(("wide", "narrow"), None),
            P(("wide", "narrow")),
            P(("wide", "narrow")),
            P(("wide", "narrow")),
            P("wide", "narrow", None),
            P("wide", "narrow"),
            P("wide", "narrow", None),
            P("wide", "narrow"),
        ),
        check_vma=False,
    )
```

```python
import functools

import jax
import jax.numpy as jnp
from jax import lax
from jax.experimental import pallas as pl
from jax.experimental.pallas import tpu as pltpu
from jax.sharding import PartitionSpec as P

HEAD_DIM = 64
EPSILON = 1e-05
MASKED = -1e30
TILE = 128
REACH = 512
LOW = jnp.bfloat16
FULL = jnp.float32
VMEM_BYTES = 56 * 2**20


def params():
    return pltpu.CompilerParams(vmem_limit_bytes=VMEM_BYTES)


def cost():
    return pl.CostEstimate(flops=1024, bytes_accessed=1024, transcendentals=0)


def shape_of(dims, dtype):
    return jax.ShapeDtypeStruct(dims, dtype)


def whole(dims):
    return pl.BlockSpec(dims, lambda *_: (0,) * len(dims))


def dot_nn(a, b):
    return jnp.dot(a, b, preferred_element_type=FULL)


def dot_nt(a, b):
    return lax.dot_general(a, b, (((1,), (1,)), ((), ())), preferred_element_type=FULL)


def dot_tn(a, b):
    return lax.dot_general(a, b, (((0,), (0,)), ((), ())), preferred_element_type=FULL)


def after(values, *others):
    return lax.optimization_barrier((values,) + others)[0]


def after2(first, *values):
    return lax.optimization_barrier(values + (first,))[:-1]


def normed(values):
    average = jnp.mean(values, axis=-1, keepdims=True)
    centred = values - average
    spread = jnp.mean(centred * centred, axis=-1, keepdims=True)
    inverse = lax.rsqrt(spread + EPSILON)
    return centred * inverse, inverse


def norm_back(grad, gain, xhat, inverse):
    scaled = grad * gain
    first = jnp.mean(scaled, axis=-1, keepdims=True)
    second = jnp.mean(scaled * xhat, axis=-1, keepdims=True)
    return inverse * (scaled - first - xhat * second)


GELU_SLOPE = 0.7978845608028654
GELU_CUBE = 0.044715 * GELU_SLOPE
LOG2_E = 1.4426950408889634


def gelu_gate(v, square):
    power = v * (-2.0 * LOG2_E * GELU_SLOPE - (2.0 * LOG2_E * GELU_CUBE) * square)
    below = 1.0 + jnp.exp2(jnp.minimum(power, 100.0))
    guess = pl.reciprocal(below, approx=True)
    return guess * (2.0 - below * guess)


def gelu(v):
    return v * gelu_gate(v, v * v)


def gelu_pair(v):
    square = v * v
    gate = gelu_gate(v, square)
    active = v * gate
    grad = gate + (active - active * gate) * (2.0 * GELU_SLOPE + (6.0 * GELU_CUBE) * square)
    return active, grad


def project_kernel(tokens_ref, gain_ref, shift_ref, weight_ref, bias_ref, normed_ref, out_ref):
    xhat, _ = normed(tokens_ref[...].astype(FULL))
    low = (xhat * gain_ref[...] + shift_ref[...]).astype(LOW)
    normed_ref[...] = low
    out_ref[...] = (dot_nn(low, weight_ref[...]) + bias_ref[...]).astype(LOW)


def project(tokens, gain, shift, weight, bias, rows=256):
    count, width = tokens.shape
    out = weight.shape[1]
    return pl.pallas_call(
        project_kernel,
        grid=(count // rows,),
        in_specs=[
            pl.BlockSpec((rows, width), lambda i: (i, 0)),
            whole((1, width)),
            whole((1, width)),
            whole((width, out)),
            whole((1, out)),
        ],
        out_specs=[
            pl.BlockSpec((rows, width), lambda i: (i, 0)),
            pl.BlockSpec((rows, out), lambda i: (i, 0)),
        ],
        out_shape=[shape_of((count, width), LOW), shape_of((count, out), LOW)],
        compiler_params=params(),
        name="project",
        cost_estimate=cost(),
    )(tokens, gain, shift, weight, bias)


def fill_mask(column_ref, line_ref, mask_ref, reach):
    blocks = line_ref.shape[1] // TILE
    key_row = lax.broadcasted_iota(jnp.int32, (TILE, TILE), 0)
    query_lane = lax.broadcasted_iota(jnp.int32, (TILE, TILE), 1)
    for i in range(blocks):
        line = line_ref[:, i * TILE : (i + 1) * TILE]
        for step in range(reach):
            j = i - (reach - 1) + step
            if j < 0:
                continue
            same = column_ref[j * TILE : (j + 1) * TILE, :] == line
            if j == i:
                same = same & (key_row <= query_lane)
            mask_ref[i, step * TILE : (step + 1) * TILE, :] = jnp.where(same, 0.0, MASKED)


def split_heads(block):
    lane = lax.broadcasted_iota(jnp.int32, block.shape, 1)
    zero = jnp.zeros_like(block)
    return jnp.concatenate(
        [jnp.where(lane < HEAD_DIM, block, zero), jnp.where(lane < HEAD_DIM, zero, block)], axis=0
    )


def join_heads(pair):
    return jnp.concatenate([pair[:HEAD_DIM, :TILE], pair[HEAD_DIM : 2 * HEAD_DIM, TILE:]], axis=0)


def twice(values):
    return jnp.concatenate([values, values], axis=1)


def attend_kernel(
    reach, count_ref, q_ref, k_ref, v_ref, column_ref, line_ref, out_ref, log_ref, mask_ref, vt_ref
):
    pairs = [slice(p * TILE, (p + 1) * TILE) for p in range(q_ref.shape[1] // TILE)]

    @pl.when(pl.program_id(0) == 0)
    def _():
        fill_mask(column_ref, line_ref, mask_ref, reach)

    for p, cols in enumerate(pairs):
        vt_ref[p, :TILE, :] = v_ref[:, cols].T
        vt_ref[p, TILE:, :] = jnp.ones((vt_ref.shape[1] - TILE, vt_ref.shape[2]), LOW)

    def block(i, carry):
        here = pl.ds(pl.multiple_of(i * TILE, TILE), TILE)
        for n in range(1, reach + 1):

            @pl.when(count_ref[i] == n)
            def _():
                window = pl.ds(pl.multiple_of((i - (n - 1)) * TILE, TILE), n * TILE)
                mask = twice(mask_ref[i, (reach - n) * TILE :, :])
                queries = [split_heads(q_ref[here, c] * jnp.asarray(HEAD_DIM**-0.5, LOW)) for c in pairs]
                scores = [dot_nt(k_ref[window, c], q) + mask for c, q in zip(pairs, queries)]
                highest = [jnp.max(s, axis=0, keepdims=True) for s in scores]
                weights = [jnp.exp(s - h).astype(LOW) for s, h in zip(scores, highest)]
                mixed = [dot_nn(vt_ref[p, :, window], w) for p, w in enumerate(weights)]
                for p, cols in enumerate(pairs):
                    totals = mixed[p][TILE : TILE + 1, :]
                    value = mixed[p][:TILE, :] * (1.0 / totals)
                    out_ref[here, cols] = join_heads(value).T.astype(LOW)
                    logs = highest[p] + jnp.log(totals)
                    log_ref[p, 0:1, here] = logs[:, :TILE]
                    log_ref[p, 1:2, here] = logs[:, TILE:]

        return carry

    lax.fori_loop(0, q_ref.shape[0] // TILE, block, 0)


def attend(counts, projected, column, line, reach, group=8):
    rows = projected.shape[0]
    width = projected.shape[1] // 3
    steps = width // (TILE * group)
    cols = TILE * group
    return pl.pallas_call(
        functools.partial(attend_kernel, reach),
        grid_spec=pltpu.PrefetchScalarGridSpec(
            num_scalar_prefetch=1,
            grid=(steps,),
            in_specs=[
                pl.BlockSpec((rows, cols), lambda j, _: (0, j)),
                pl.BlockSpec((rows, cols), lambda j, _: (0, j + steps)),
                pl.BlockSpec((rows, cols), lambda j, _: (0, j + 2 * steps)),
                whole((rows, 1)),
                whole((1, rows)),
            ],
            out_specs=[
                pl.BlockSpec((rows, cols), lambda j, _: (0, j)),
                pl.BlockSpec((group, 8, rows), lambda j, _: (j, 0, 0)),
            ],
            scratch_shapes=[
                pltpu.VMEM((rows // TILE, reach * TILE, TILE), FULL),
                pltpu.VMEM((group, TILE + 16, rows), LOW),
            ],
        ),
        out_shape=[shape_of((rows, width), LOW), shape_of((width // TILE, 8, rows), FULL)],
        compiler_params=params(),
        name="attend",
        cost_estimate=cost(),
    )(counts, projected, projected, projected, column, line)


def attend_back_kernel(
    reach,
    count_ref,
    q_ref,
    k_ref,
    v_ref,
    out_ref,
    grad_ref,
    log_ref,
    column_ref,
    line_ref,
    back_ref,
    bias_ref,
    mask_ref,
    kt_ref,
    dk_ref,
    dv_ref,
):
    pairs = [slice(p * TILE, (p + 1) * TILE) for p in range(q_ref.shape[1] // TILE)]

    @pl.when(pl.program_id(0) == 0)
    def _():
        fill_mask(column_ref, line_ref, mask_ref, reach)

    scale = HEAD_DIM**-0.5
    for p, cols in enumerate(pairs):
        kt_ref[p] = k_ref[:, cols].T
    dk_ref[...] = jnp.zeros_like(dk_ref)
    dv_ref[...] = jnp.zeros_like(dv_ref)

    def block(i, carry):
        here = pl.ds(pl.multiple_of(i * TILE, TILE), TILE)
        for n in range(1, reach + 1):

            @pl.when(count_ref[i] == n)
            def _():
                window = pl.ds(pl.multiple_of((i - (n - 1)) * TILE, TILE), n * TILE)
                mask = twice(mask_ref[i, (reach - n) * TILE :, :])
                queries = [split_heads(q_ref[here, c] * jnp.asarray(scale, LOW)) for c in pairs]
                grads = [split_heads(grad_ref[here, c]) for c in pairs]
                dots = []
                logs = []
                for p, c in enumerate(pairs):
                    product = (grad_ref[here, c].astype(FULL) * out_ref[here, c].astype(FULL)).T
                    dots.append(
                        jnp.concatenate(
                            [
                                jnp.sum(product[:HEAD_DIM, :], axis=0, keepdims=True),
                                jnp.sum(product[HEAD_DIM:, :], axis=0, keepdims=True),
                            ],
                            axis=1,
                        )
                    )
                    logs.append(
                        jnp.concatenate([log_ref[p, 0:1, here], log_ref[p, 1:2, here]], axis=1)
                    )
                scores = [dot_nt(k_ref[window, c], q) + mask for c, q in zip(pairs, queries)]
                prob_grad = [dot_nt(v_ref[window, c], g) for c, g in zip(pairs, grads)]
                exact = [jnp.exp(s - l) for s, l in zip(scores, logs)]
                score_grad = [
                    (e * (g - d)).astype(LOW) for e, g, d in zip(exact, prob_grad, dots)
                ]
                for p, c in enumerate(pairs):
                    dv_ref[window, c] += dot_nn(exact[p].astype(LOW), grads[p])
                    dk_ref[window, c] += dot_nn(score_grad[p], queries[p])
                    back = join_heads(dot_nn(kt_ref[p, :, window], score_grad[p])) * scale
                    back_ref[0, here, c] = back.T.astype(LOW)

        return carry

    lax.fori_loop(0, q_ref.shape[0] // TILE, block, 0)
    back_ref[1, :, :] = dk_ref[...].astype(LOW)
    value_grad = dv_ref[...].astype(LOW)
    back_ref[2, :, :] = value_grad
    bias_ref[0:1, :] = jnp.sum(back_ref[0, :, :].astype(FULL), axis=0, keepdims=True)
    bias_ref[1:2, :] = jnp.sum(value_grad.astype(FULL), axis=0, keepdims=True)


def attend_back(counts, projected, attended, grad, logs, column, line, reach, part, parts):
    rows = projected.shape[0]
    width = projected.shape[1] // 3
    cols = width // parts
    group = cols // TILE
    return pl.pallas_call(
        functools.partial(attend_back_kernel, reach),
        grid_spec=pltpu.PrefetchScalarGridSpec(
            num_scalar_prefetch=1,
            grid=(1,),
            in_specs=[
                pl.BlockSpec((rows, cols), lambda j, _: (0, part)),
                pl.BlockSpec((rows, cols), lambda j, _: (0, part + parts)),
                pl.BlockSpec((rows, cols), lambda j, _: (0, part + 2 * parts)),
                pl.BlockSpec((rows, cols), lambda j, _: (0, part)),
                pl.BlockSpec((rows, cols), lambda j, _: (0, part)),
                pl.BlockSpec((group, 8, rows), lambda j, _: (part, 0, 0)),
                whole((rows, 1)),
                whole((1, rows)),
            ],
            out_specs=[whole((3, rows, cols)), whole((8, cols))],
            scratch_shapes=[
                pltpu.VMEM((rows // TILE, reach * TILE, TILE), FULL),
                pltpu.VMEM((group, TILE, rows), LOW),
                pltpu.VMEM((rows, cols), FULL),
                pltpu.VMEM((rows, cols), FULL),
            ],
        ),
        out_shape=[shape_of((3, rows, cols), LOW), shape_of((8, cols), FULL)],
        compiler_params=params(),
        name="attend_back",
        cost_estimate=cost(),
    )(counts, projected, projected, projected, attended, grad, logs, column, line)


def slots_kernel(experts, capacity, chosen_ref, out_ref):
    count = chosen_ref.shape[1]
    place = lax.broadcasted_iota(jnp.int32, (experts, count), 0)
    mine = place == chosen_ref[...]
    earlier = lax.broadcasted_iota(jnp.int32, (count, count), 0) < lax.broadcasted_iota(
        jnp.int32, (count, count), 1
    )
    before = dot_nn(one_hot(mine), one_hot(earlier))
    base = (place * capacity).astype(FULL)
    out_ref[...] = jnp.sum(jnp.where(mine, before + base, 0.0), axis=0, keepdims=True).astype(
        jnp.int32
    )


def slots_of(chosen, experts, capacity):
    return pl.pallas_call(
        functools.partial(slots_kernel, experts, capacity),
        out_shape=shape_of(chosen.shape, jnp.int32),
        compiler_params=params(),
        name="slots",
        cost_estimate=cost(),
    )(chosen)


def one_hot(hit):
    return jnp.where(hit, 1.0, 0.0).astype(LOW)


def dispatch_kernel(slot_ref, rows_ref, out_ref):
    tile = out_ref.shape[0]
    place = pl.program_id(0) * tile + lax.broadcasted_iota(jnp.int32, (tile, slot_ref.shape[1]), 0)
    out_ref[...] = dot_nn(one_hot(place == slot_ref[...]), rows_ref[...]).astype(LOW)


def dispatch(slot_line, rows, slots, tile=256):
    count, width = rows.shape
    return pl.pallas_call(
        dispatch_kernel,
        grid=(slots // tile,),
        in_specs=[whole((1, count)), whole((count, width))],
        out_specs=pl.BlockSpec((tile, width), lambda i: (i, 0)),
        out_shape=shape_of((slots, width), LOW),
        compiler_params=params(),
        name="dispatch",
        cost_estimate=cost(),
    )(slot_line, rows)


def picked(slot_ref, slotted):
    lane = lax.broadcasted_iota(jnp.int32, (slot_ref.shape[0], slotted.shape[0]), 1)
    return dot_nn(one_hot(lane == slot_ref[...]), slotted)


def combine_kernel(slot_ref, slotted_ref, hidden_ref, out_ref):
    out_ref[...] = (hidden_ref[...] + picked(slot_ref, slotted_ref[...])).astype(LOW)


def combine(slot_column, slotted, hidden, rows=256):
    count, width = hidden.shape
    return pl.pallas_call(
        combine_kernel,
        grid=(count // rows,),
        in_specs=[
            pl.BlockSpec((rows, 1), lambda i: (i, 0)),
            whole(slotted.shape),
            pl.BlockSpec((rows, width), lambda i: (i, 0)),
        ],
        out_specs=pl.BlockSpec((rows, width), lambda i: (i, 0)),
        out_shape=shape_of((count, width), LOW),
        compiler_params=params(),
        name="combine",
        cost_estimate=cost(),
    )(slot_column, slotted, hidden)


def mix_kernel(
    tiles,
    attended_ref,
    weight_ref,
    bias_ref,
    tokens_ref,
    gain_ref,
    shift_ref,
    slot_ref,
    hidden_ref,
    *refs,
):
    *send_refs, rows_ref = refs
    step = pl.program_id(0)
    size = attended_ref.shape[0]

    @pl.when(step < tiles)
    def _():
        branch = dot_nn(attended_ref[...], weight_ref[...]) + bias_ref[...]
        hidden = tokens_ref[...].astype(FULL) + branch
        hidden_ref[...] = hidden
        xhat, _ = normed(hidden)
        rows_ref[pl.ds(pl.multiple_of(step * size, size), size), :] = (
            xhat * gain_ref[...] + shift_ref[...]
        ).astype(LOW)

    @pl.when(step >= tiles)
    def _():
        tile = send_refs[0].shape[0]
        place = (step - tiles) * tile + lax.broadcasted_iota(
            jnp.int32, (tile, slot_ref.shape[1]), 0
        )
        spread = dot_nn(one_hot(place == slot_ref[...]), rows_ref[...]).astype(LOW)
        at = 0
        for send_ref in send_refs:
            cols = send_ref.shape[1]
            send_ref[...] = spread[:, at : at + cols]
            at += cols


def mix(attended, weight, bias, tokens, gain, shift, slot_line, slots, sizes, rows=256, tile=256):
    count, width = tokens.shape
    tiles = count // rows
    by_row = pl.BlockSpec((rows, width), lambda i: (jnp.minimum(i, tiles - 1), 0))
    return pl.pallas_call(
        functools.partial(mix_kernel, tiles),
        grid=(tiles + slots // tile,),
        in_specs=[
            by_row,
            whole(weight.shape),
            whole((1, width)),
            by_row,
            whole((1, width)),
            whole((1, width)),
            whole((1, count)),
        ],
        out_specs=[by_row]
        + [pl.BlockSpec((tile, cols), lambda i: (jnp.maximum(i - tiles, 0), 0)) for cols in sizes],
        out_shape=[shape_of((count, width), FULL)]
        + [shape_of((slots, cols), LOW) for cols in sizes],
        scratch_shapes=[pltpu.VMEM((count, width), LOW)],
        compiler_params=params(),
        name="mix",
        cost_estimate=cost(),
    )(attended, weight, bias, tokens, gain, shift, slot_line)


def up_product(rows_refs, part, up):
    total = None
    at = 0
    for rows_ref in rows_refs:
        cols = rows_ref.shape[1]
        more = dot_nn(rows_ref[part, :], up[at : at + cols, :])
        total = more if total is None else total + more
        at += cols
    return total


def expert_first_kernel(steps, at_ref, rows_ref, grad_ref, up_ref, bias_ref, *refs):
    active_ref, slope_ref, down_ref = refs
    size = 256
    for r in range(grad_ref.shape[0] // size):
        part = slice(r * size, (r + 1) * size)
        active, slope = gelu_pair(dot_nn(rows_ref[part, :], up_ref[0]) + bias_ref[...])
        active_ref[part, :] = active.astype(LOW)
        slope_ref[part, :] = slope.astype(LOW)

    @pl.when(pl.program_id(0) < steps)
    def _():
        down_ref[...] = dot_tn(active_ref[...], grad_ref[...]).astype(LOW)


def expert_first(half, rows, grads, up, bias, chunk=512):
    count, width = grads.shape
    hidden = up.shape[2]
    steps = hidden // (2 * chunk)

    def chunk_of(i, at):
        return (at[0] + i // steps) % 2 * steps + i % steps

    by_chunk = pl.BlockSpec((count, chunk), lambda i, at: (0, chunk_of(i, at)))
    return pl.pallas_call(
        functools.partial(expert_first_kernel, steps),
        grid_spec=pltpu.PrefetchScalarGridSpec(
            num_scalar_prefetch=1,
            grid=(2 * steps,),
            in_specs=[
                whole((count, width)),
                whole((count, width)),
                pl.BlockSpec((1, width, chunk), lambda i, at: (0, 0, chunk_of(i, at))),
                pl.BlockSpec((1, chunk), lambda i, at: (0, chunk_of(i, at))),
            ],
            out_specs=[
                by_chunk,
                by_chunk,
                pl.BlockSpec((chunk, width), lambda i, at: (jnp.minimum(i, steps - 1), 0)),
            ],
        ),
        out_shape=[
            shape_of((count, hidden), LOW),
            shape_of((count, hidden), LOW),
            shape_of((hidden // 2, width), LOW),
        ],
        compiler_params=params(),
        name="expert_first",
        cost_estimate=cost(),
    )(half.reshape(1), rows, grads, up, bias)


def down_grad_kernel(at_ref, active_ref, grad_ref, out_ref):
    out_ref[...] = dot_tn(active_ref[...], grad_ref[...]).astype(LOW)


def down_grad(half, active, grads, chunk=512):
    count, width = grads.shape
    size = active.shape[1] // 2
    steps = size // chunk
    return pl.pallas_call(
        down_grad_kernel,
        grid_spec=pltpu.PrefetchScalarGridSpec(
            num_scalar_prefetch=1,
            grid=(steps,),
            in_specs=[
                pl.BlockSpec((count, chunk), lambda i, at: (0, at[0] * steps + i)),
                whole((count, width)),
            ],
            out_specs=pl.BlockSpec((chunk, width), lambda i, at: (i, 0)),
        ),
        out_shape=shape_of((size, width), LOW),
        compiler_params=params(),
        name="down_grad",
        cost_estimate=cost(),
    )(half.reshape(1), active, grads)


def neighbour_kernel(parts, at_ref, *refs):
    rows_refs, refs = refs[:parts], refs[parts:]
    grad_ref, up_ref, bias_ref, own_ref, down_ref, active_ref = refs

    @pl.when(at_ref[1] == 1)
    def _():
        size = 256
        for r in range(grad_ref.shape[0] // size):
            part = slice(r * size, (r + 1) * size)
            active = gelu(up_product(rows_refs, part, up_ref[0]) + bias_ref[...])
            active_ref[part, :] = active.astype(LOW)
        down = dot_tn(active_ref[...], grad_ref[...])
        down_ref[...] = (own_ref[...].astype(FULL) + down).astype(LOW)


def neighbour_down(at, rows, grads, up, bias, own, chunk=512):
    count, width = grads.shape
    half = up.shape[2] // 2
    steps = half // chunk
    return pl.pallas_call(
        functools.partial(neighbour_kernel, len(rows)),
        grid_spec=pltpu.PrefetchScalarGridSpec(
            num_scalar_prefetch=1,
            grid=(steps,),
            in_specs=[whole(part.shape) for part in rows]
            + [
                whole((count, width)),
                pl.BlockSpec((1, width, chunk), lambda i, at: (0, 0, at[0] * steps + i)),
                pl.BlockSpec((1, chunk), lambda i, at: (0, at[0] * steps + i)),
                pl.BlockSpec((chunk, width), lambda i, at: (i, 0)),
            ],
            out_specs=pl.BlockSpec((chunk, width), lambda i, at: (i, 0)),
            scratch_shapes=[pltpu.VMEM((count, chunk), LOW)],
        ),
        out_shape=shape_of((half, width), LOW),
        compiler_params=params(),
        name="neighbour_down",
        cost_estimate=cost(),
    )(at, *rows, grads, up, bias, own)


def expert_second_kernel(parts, at_ref, *refs):
    rows_refs, refs = refs[:parts], refs[parts:]
    grad_ref, down_ref, slope_ref, low_ref, bias_ref, *block_refs, product_ref = refs
    low = (dot_nt(grad_ref[...], down_ref[0]) * slope_ref[...].astype(FULL)).astype(LOW)
    low_ref[...] = low
    bias_ref[...] = jnp.sum(low.astype(FULL), axis=0, keepdims=True)
    at = 0
    for rows_ref in rows_refs:
        cols = rows_ref.shape[1]
        product_ref[at : at + cols, :] = dot_tn(rows_ref[...], low).astype(LOW)
        at += cols
    for i, block_ref in enumerate(block_refs):
        size = block_ref.shape[0]
        block_ref[...] = product_ref[pl.ds(pl.multiple_of(at_ref[i] * size, size), size), :]


def expert_second(order, rows, grads, down, slope, chunk=512):
    count, width = grads.shape
    hidden = slope.shape[1]
    blocks = len(order)
    by_chunk = pl.BlockSpec((count, chunk), lambda i, _: (0, i))
    return pl.pallas_call(
        functools.partial(expert_second_kernel, len(rows)),
        grid_spec=pltpu.PrefetchScalarGridSpec(
            num_scalar_prefetch=1,
            grid=(hidden // chunk,),
            in_specs=[whole(part.shape) for part in rows]
            + [
                whole((count, width)),
                pl.BlockSpec((1, chunk, width), lambda i, _: (0, i, 0)),
                by_chunk,
            ],
            out_specs=[by_chunk, pl.BlockSpec((1, chunk), lambda i, _: (0, i))]
            + [pl.BlockSpec((width // blocks, chunk), lambda i, _: (0, i))] * blocks,
            scratch_shapes=[pltpu.VMEM((width, chunk), LOW)],
        ),
        out_shape=[shape_of((count, hidden), LOW), shape_of((1, hidden), FULL)]
        + [shape_of((width // blocks, hidden), LOW)] * blocks,
        compiler_params=params(),
        name="expert_second",
        cost_estimate=cost(),
    )(jnp.stack(order).astype(jnp.int32), *rows, grads, down, slope)


def expert_back_kernel(low_ref, up_ref, out_ref):
    out_ref[...] = dot_nt(low_ref[...], up_ref[0]).astype(LOW)


def expert_back(low, up, rows=256):
    count, hidden = low.shape
    width = up.shape[1]
    return pl.pallas_call(
        expert_back_kernel,
        grid=(count // rows,),
        in_specs=[pl.BlockSpec((rows, hidden), lambda i: (i, 0)), whole((1, width, hidden))],
        out_specs=pl.BlockSpec((rows, width), lambda i: (i, 0)),
        out_shape=shape_of((count, width), LOW),
        compiler_params=params(),
        name="expert_back",
        cost_estimate=cost(),
    )(low, up)


def expert_out_kernel(active_ref, down_ref, bias_ref, out_ref):
    out_ref[...] = (dot_nn(active_ref[...], down_ref[0]) + bias_ref[...]).astype(LOW)


def expert_out(active, down, bias, rows=256):
    count, hidden = active.shape
    width = down.shape[2]
    return pl.pallas_call(
        expert_out_kernel,
        grid=(count // rows,),
        in_specs=[
            pl.BlockSpec((rows, hidden), lambda i: (i, 0)),
            whole((1, hidden, width)),
            whole((1, width)),
        ],
        out_specs=pl.BlockSpec((rows, width), lambda i: (i, 0)),
        out_shape=shape_of((count, width), LOW),
        compiler_params=params(),
        name="expert_out",
        cost_estimate=cost(),
    )(active, down, bias)


def middle_back_kernel(
    core_ref,
    slot_ref,
    slotted_ref,
    hidden_ref,
    cotangent_ref,
    gain_ref,
    weight_ref,
    attended_ref,
    hidden_grad_ref,
    attended_grad_ref,
    kept_ref,
    sent_ref,
    sums_ref,
    total_ref,
):
    step = pl.program_id(0)
    grad = picked(slot_ref, slotted_ref[...])
    xhat, inverse = normed(hidden_ref[...])
    hidden_grad = cotangent_ref[...].astype(FULL) + norm_back(grad, gain_ref[...], xhat, inverse)
    hidden_grad_ref[...] = hidden_grad
    low = hidden_grad.astype(LOW)
    attended_grad_ref[...] = dot_nt(low, weight_ref[...]).astype(LOW)
    weight_grad = dot_tn(attended_ref[...], low)
    sums = [
        jnp.sum(grad * xhat, axis=0, keepdims=True),
        jnp.sum(grad, axis=0, keepdims=True),
        jnp.sum(hidden_grad, axis=0, keepdims=True),
    ]

    @pl.when(step == 0)
    def _():
        total_ref[...] = weight_grad
        for i, part in enumerate(sums):
            sums_ref[i : i + 1, :] = part

    @pl.when(step > 0)
    def _():
        total_ref[...] += weight_grad
        for i, part in enumerate(sums):
            sums_ref[i : i + 1, :] += part

    @pl.when(step == pl.num_programs(0) - 1)
    def _():
        cores_apart(total_ref, core_ref[0], kept_ref, sent_ref)


def middle_back(
    core, slot_column, slotted, hidden, cotangent, gain, weight, attended, rows=256
):
    count, width = hidden.shape
    wide = lax.axis_size("wide")
    part = (wide // 2, width // wide, width)
    by_row = pl.BlockSpec((rows, width), lambda i, _: (i, 0))
    return pl.pallas_call(
        middle_back_kernel,
        grid_spec=pltpu.PrefetchScalarGridSpec(
            num_scalar_prefetch=1,
            grid=(count // rows,),
            in_specs=[
                pl.BlockSpec((rows, 1), lambda i, _: (i, 0)),
                whole(slotted.shape),
                by_row,
                by_row,
                whole((1, width)),
                whole(weight.shape),
                by_row,
            ],
            out_specs=[by_row, by_row, whole(part), whole(part), whole((8, width))],
            scratch_shapes=[pltpu.VMEM(weight.shape, FULL)],
        ),
        out_shape=[
            shape_of((count, width), FULL),
            shape_of((count, width), LOW),
            shape_of(part, LOW),
            shape_of(part, LOW),
            shape_of((8, width), FULL),
        ],
        compiler_params=params(),
        name="middle_back",
        cost_estimate=cost(),
    )(core, slot_column, slotted, hidden, cotangent, gain, weight, attended)


def project_grad_kernel(core_ref, normed_ref, stacked_ref, kept_ref, sent_ref, product_ref):
    product_ref[...] = dot_tn(normed_ref[...], stacked_ref[0])
    cores_apart(product_ref, core_ref[0], kept_ref, sent_ref)


def project_grad(core, normed_low, stacked):
    count, width = normed_low.shape
    chunk = stacked.shape[2]
    wide = lax.axis_size("wide")
    part = (wide // 2, width // wide)
    half = pl.BlockSpec(part + (chunk,), lambda i, _: (0, 0, i))
    return pl.pallas_call(
        project_grad_kernel,
        grid_spec=pltpu.PrefetchScalarGridSpec(
            num_scalar_prefetch=1,
            grid=(3,),
            in_specs=[
                whole((count, width)),
                pl.BlockSpec((1, count, chunk), lambda i, _: (i, 0, 0)),
            ],
            out_specs=[half, half],
            scratch_shapes=[pltpu.VMEM((width, chunk), FULL)],
        ),
        out_shape=[shape_of(part + (3 * chunk,), LOW)] * 2,
        compiler_params=params(),
        name="project_grad",
        cost_estimate=cost(),
    )(core, normed_low, stacked)


def first_back_kernel(
    parts, weight_ref, tokens_ref, gain_ref, hidden_grad_ref, *refs
):
    stacked_refs, (out_ref, sums_ref) = refs[:parts], refs[parts:]
    step = pl.program_id(0)
    width = tokens_ref.shape[1]
    cols = width // parts
    grad = None
    for part, stacked_ref in enumerate(stacked_refs):
        for i in range(3):
            at = i * width + part * cols
            more = dot_nt(stacked_ref[i], weight_ref[:, at : at + cols])
            grad = more if grad is None else grad + more
    xhat, inverse = normed(tokens_ref[...].astype(FULL))
    out_ref[...] = (
        hidden_grad_ref[...] + norm_back(grad, gain_ref[...], xhat, inverse)
    ).astype(LOW)
    sums = [
        jnp.sum(grad * xhat, axis=0, keepdims=True),
        jnp.sum(grad, axis=0, keepdims=True),
    ]

    @pl.when(step == 0)
    def _():
        for i, part in enumerate(sums):
            sums_ref[i : i + 1, :] = part

    @pl.when(step > 0)
    def _():
        for i, part in enumerate(sums):
            sums_ref[i : i + 1, :] += part


def first_back(stacked, weight, tokens, gain, hidden_grad, rows=256):
    count, width = tokens.shape
    by_row = pl.BlockSpec((rows, width), lambda i: (i, 0))
    return pl.pallas_call(
        functools.partial(first_back_kernel, len(stacked)),
        grid=(count // rows,),
        in_specs=[whole(weight.shape), by_row, whole((1, width)), by_row]
        + [pl.BlockSpec((3, rows, part.shape[2]), lambda i: (0, i, 0)) for part in stacked],
        out_specs=[by_row, whole((8, width))],
        out_shape=[shape_of((count, width), LOW), shape_of((8, width), FULL)],
        compiler_params=params(),
        name="first_back",
        cost_estimate=cost(),
    )(weight, tokens, gain, hidden_grad, *stacked)


def merge_kernel(shape, flagged, fixed, *refs):
    at_ref, refs = (None, refs) if fixed else (refs[0], refs[1:])
    count = sum(sum(groups) for groups in shape)
    place = 0
    for out_ref, groups in zip(refs[count:], shape):
        column = 0
        for size in groups:
            total = None
            for i in range(place, place + size):
                part = refs[i][0].astype(FULL)
                if flagged[i]:
                    part = jnp.where(at_ref[count + i] == 1, part, 0.0)
                total = part if total is None else total + part
            place += size
            cols = total.shape[1]
            out_ref[:, column : column + cols] = total.astype(out_ref.dtype)
            column += cols


def merge_all(results, dtype=LOW, tile=512):
    terms = [term for groups in results for group in groups for term in group]
    flagged = [len(term) > 2 for term in terms]
    counts = [term[2] if len(term) > 2 else 1 for term in terms]
    terms = [term[:2] for term in terms]
    rows = terms[0][0].shape[1]
    widths = [sum(group[0][0].shape[2] for group in groups) for groups in results]
    tile = min(tile, rows)
    columns = sum(widths) + sum(blocks.shape[2] for blocks, _ in terms)
    while tile > 16 and tile * columns * 4 > VMEM_BYTES // 2:
        tile //= 2
    kernel_shape = [[len(group) for group in groups] for groups in results]
    fixed = not any(flagged) and all(isinstance(index, int) for _, index in terms)
    kernel = functools.partial(merge_kernel, kernel_shape, flagged, fixed)
    out_shape = [shape_of((rows, width), dtype) for width in widths]
    if fixed:
        return pl.pallas_call(
            kernel,
            grid=(rows // tile,),
            in_specs=[
                pl.BlockSpec((1, tile, blocks.shape[2]), lambda i, index=index: (index, i, 0))
                for blocks, index in terms
            ],
            out_specs=[pl.BlockSpec((tile, width), lambda i: (i, 0)) for width in widths],
            out_shape=out_shape,
            compiler_params=params(),
            name="merge",
            cost_estimate=cost(),
        )(*[blocks for blocks, _ in terms])
    at = jnp.stack([jnp.asarray(x, jnp.int32) for x in [index for _, index in terms] + counts])
    return pl.pallas_call(
        kernel,
        grid_spec=pltpu.PrefetchScalarGridSpec(
            num_scalar_prefetch=1,
            grid=(rows // tile,),
            in_specs=[
                pl.BlockSpec((1, tile, blocks.shape[2]), lambda i, at, j=j: (at[j], i, 0))
                for j, (blocks, _) in enumerate(terms)
            ],
            out_specs=[pl.BlockSpec((tile, width), lambda i, at: (i, 0)) for width in widths],
        ),
        out_shape=out_shape,
        compiler_params=params(),
        name="merge",
        cost_estimate=cost(),
    )(at, *[blocks for blocks, _ in terms])


def merge(groups, dtype=LOW):
    return merge_all([groups], dtype)[0]


def one(values):
    return (values[None], 0)


def swap_cores(values):
    size = lax.axis_size("wide")
    return lax.ppermute(values, "wide", [(i, i ^ 1) for i in range(size)])


def finish_kernel(width, lines_ref, out_weight_ref, qkv_ref, small_ref):
    total = jnp.sum(lines_ref[...].astype(FULL), axis=0)
    half = width // 2
    out_weight_ref[...] = total[:, :width]
    for i in range(3):
        for part in range(2):
            to = (2 * i + part) * half
            at = width + (3 * part + i) * half
            qkv_ref[:, to : to + half] = total[:, at : at + half]
    small_ref[...] = total[:, 4 * width :]


def finish(lines, width):
    rows = lines.shape[1]
    columns = lines.shape[2] - 4 * width
    return pl.pallas_call(
        functools.partial(finish_kernel, width),
        out_shape=[
            shape_of((rows, width), FULL),
            shape_of((rows, 3 * width), FULL),
            shape_of((rows, columns), FULL),
        ],
        compiler_params=params(),
        name="finish",
        cost_estimate=cost(),
    )(lines)


def flat(blocks):
    return (blocks.reshape(1, -1, blocks.shape[-1]), 0)


def all_of(blocks):
    return [(blocks, i) for i in range(blocks.shape[0])]


def swap_chips(values):
    size = lax.axis_size("wide")
    groups = [list(range(core, size, 2)) for core in range(2)]
    blocks = values.reshape(size // 2, -1, values.shape[1])
    return lax.all_to_all(
        blocks, "wide", split_axis=0, concat_axis=0, tiled=True, axis_index_groups=groups
    )


def swap_narrow(values):
    blocks = values.reshape(lax.axis_size("narrow"), -1, values.shape[1])
    return lax.all_to_all(blocks, "narrow", split_axis=0, concat_axis=0, tiled=True)


def cores_apart(values_ref, core, kept_ref, sent_ref):
    chips = kept_ref.shape[0]
    rows = kept_ref.shape[1]
    for chip in range(chips):
        kept_ref[chip] = values_ref[pl.ds((2 * chip + core) * rows, rows), :].astype(LOW)
        sent_ref[chip] = values_ref[pl.ds((2 * chip + 1 - core) * rows, rows), :].astype(LOW)


def body(
    tokens,
    segment_ids,
    expert_ids,
    first_gain,
    first_shift,
    qkv_weight,
    query_bias,
    value_bias,
    out_weight,
    out_bias,
    second_gain,
    second_shift,
    up_weights,
    up_bias,
    down_weights,
    down_bias,
    cotangent,
):
    row_length, width = tokens.shape
    wide_size = lax.axis_size("wide")
    narrow_size = lax.axis_size("narrow")
    expert_total = wide_size * up_weights.shape[0]
    capacity = max(2, row_length * 5 // (4 * expert_total))
    slots = expert_total * capacity
    reach = min(REACH, row_length) // TILE + 1

    def line(vector):
        return vector.reshape(1, -1)

    def swap(rows):
        return lax.all_to_all(
            rows.reshape(expert_total, capacity, -1),
            "wide",
            split_axis=0,
            concat_axis=0,
            tiled=True,
        ).reshape(slots, -1)

    slot_line = slots_of(expert_ids.reshape(1, -1), expert_total, capacity)
    slot_column = slot_line.reshape(-1, 1)
    segment = segment_ids[0]
    opening = segment[::TILE]
    begins = jnp.sum((segment[None, :] < opening[:, None]).astype(jnp.int32), axis=1)
    counts = jnp.arange(opening.shape[0], dtype=jnp.int32) - begins // TILE + 1
    segment_column, segment_line = segment[:, None], segment[None, :]

    assert narrow_size == 4
    place = lax.axis_index("narrow")
    inward = [(0, 1), (3, 2)]
    outward = [(1, 0), (2, 3)]
    across = [(1, 2), (2, 1)]
    low_side = (place < 2).astype(jnp.int32)
    is_inner = ((place == 1) | (place == 2)).astype(jnp.int32)
    first_half = (place % 2).astype(jnp.int32)
    far, middle, near, outer = 3 * low_side, 1 + low_side, 2 - low_side, 3 - 3 * low_side
    core = (lax.axis_index("wide") % 2).astype(jnp.int32).reshape(1)

    def along(values, pairs):
        return lax.ppermute(values, "narrow", pairs)

    send_grad = dispatch(slot_line, cotangent, slots)
    got_grad = swap(send_grad)

    bias = jnp.concatenate([query_bias, jnp.zeros_like(query_bias), value_bias])
    normed_low, projected = project(
        after(tokens, send_grad), line(first_gain), line(first_shift), qkv_weight, line(bias)
    )
    attended, logs = attend(counts, projected, segment_column, segment_line, reach)
    attended, got_grad = lax.optimization_barrier((attended, got_grad))
    next_grad = along(got_grad, inward)
    hidden, send_rows = mix(
        attended,
        out_weight,
        line(out_bias),
        tokens,
        line(second_gain),
        line(second_shift),
        slot_line,
        slots,
        (width,),
    )
    got_rows = swap(send_rows)
    next_rows = along(got_rows, inward)
    rows = [got_rows]

    active, slope, down_first = expert_first(
        first_half, got_rows, got_grad, up_weights, up_bias
    )
    first_blocks = down_first.reshape(2, -1, width)
    up_low, up_bias_local, up_far, up_middle, up_near, up_outer = expert_second(
        [far, middle, near, outer], rows, after(got_grad, next_grad), down_weights, slope
    )
    from_far, from_middle, from_near = [along(up, inward) for up in (up_far, up_middle, up_near)]
    back = expert_back(up_low, up_weights)
    returned_back = swap(back)
    far_part = neighbour_down(
        jnp.stack([first_half, is_inner]),
        [next_rows],
        after(next_grad, back),
        up_weights,
        up_bias,
        down_first,
    )
    crossed = along(far_part, across).reshape(2, -1, width)
    result = expert_out(active, after(down_weights, far_part), down_bias)
    near_send = merge([[(after(first_blocks, result), low_side)]])
    near_part = along(near_send, inward)
    down_second = down_grad(1 - first_half, active, after(got_grad, near_send))
    returned = swap(after(result, down_second))
    second_blocks = down_second.reshape(2, -1, width)

    hidden_grad, attended_grad, out_weight_kept, out_weight_sent, middle_sums = middle_back(
        core,
        slot_column,
        after(returned_back, down_second),
        hidden,
        cotangent,
        line(second_gain),
        out_weight,
        attended,
    )
    out_weight_got = swap_cores(out_weight_sent)
    def heads_back(part, grad):
        return attend_back(
            counts, projected, attended, grad, logs, segment_column, segment_line, reach, part, 2
        )

    far_send = merge([[one(up_far), one(after(from_far, attended_grad))]])
    far_crossed = along(far_send, across)
    stacked_first, bias_first = heads_back(0, after(attended_grad, far_send))
    stacked_second, bias_second = heads_back(1, after(attended_grad, stacked_first))
    outer_send = merge(
        [[(second_blocks, 1 - low_side), (after(crossed, stacked_second), 1 - low_side)]]
    )
    outer_part = along(outer_send, outward)
    first_kept, first_sent = project_grad(core, normed_low, after(stacked_first, outer_send))
    first_got = swap_cores(first_sent)
    middle_send = merge([[one(up_middle), one(after(from_middle, first_sent))]])
    middle_crossed = along(middle_send, across)
    first_group = merge(
        [
            [flat(out_weight_kept), flat(out_weight_got)],
            [flat(first_kept), flat(after(first_got, middle_send))],
        ]
    )
    first_chips = swap_chips(first_group)
    up_outer_send = merge([[one(up_outer), one(after(far_crossed, first_group))]])
    up_outer_part = along(up_outer_send, outward)
    second_kept, second_sent = project_grad(
        core, normed_low, after(stacked_second, up_outer_send, returned, near_part)
    )
    second_got = swap_cores(second_sent)
    second_group = merge([[flat(second_kept), flat(after(second_got, outer_part))]])
    second_chips = swap_chips(second_group)
    input_grad, first_sums = first_back(
        [stacked_first, stacked_second],
        qkv_weight,
        tokens,
        line(first_gain),
        after(hidden_grad, second_group, first_chips),
    )
    vectors = jnp.concatenate(
        [
            first_sums[:2],
            jnp.concatenate([bias_first[:2], bias_second[:2]], axis=1),
            middle_sums[2:3],
            middle_sums[:2],
            first_sums[:1],
        ],
        axis=0,
    )
    lane_rows = width // wide_size
    down_bias_local = jnp.sum(got_grad.astype(FULL), axis=0)
    expert_bias = jnp.concatenate(
        [up_bias_local.reshape(narrow_size, -1), down_bias_local.reshape(narrow_size, -1)], axis=1
    )
    own_rows = lane_rows // narrow_size
    bias_columns = -(-expert_bias.shape[1] // (own_rows * TILE)) * TILE
    expert_bias = jnp.pad(
        expert_bias, ((0, 0), (0, bias_columns * own_rows - expert_bias.shape[1]))
    ).reshape(lane_rows, bias_columns)
    columns = jnp.pad(vectors.T, ((0, 0), (0, TILE - vectors.shape[0]))).astype(LOW)
    vector_blocks = lax.all_to_all(
        columns.reshape(wide_size, -1, TILE), "wide", split_axis=0, concat_axis=0, tiled=True
    )

    output = combine(slot_column, returned, after(hidden, input_grad))
    own_group = merge(
        [
            all_of(first_chips),
            all_of(after(second_chips, middle_crossed, from_near, up_outer_part, output)),
            all_of(vector_blocks),
            [one(expert_bias.astype(LOW))],
        ]
    )
    lines = swap_narrow(own_group)
    down_sum = merge(
        [
            [
                (second_blocks, low_side, is_inner),
                (first_blocks, 1 - low_side, 1 - is_inner),
                one(after(near_part, own_group)),
                one(outer_part),
                (crossed, place - 2 + 2 * low_side),
            ]
        ],
        FULL,
    )

    out_weight_grad, qkv_grad, small = finish(lines, width)
    vector_sum = small[:, : vectors.shape[0]].T
    bias_sum = small[:, TILE:].reshape(1, -1)
    up_share = up_bias.shape[1] // narrow_size
    down_share = width // narrow_size
    up_sum = merge(
        [
            [
                one(up_near) + (is_inner,),
                one(up_outer) + (1 - is_inner,),
                one(from_near),
                one(up_outer_part),
                one(middle_crossed),
            ]
        ],
        FULL,
    )
    return (
        output,
        input_grad,
        vector_sum[0],
        vector_sum[1],
        qkv_grad,
        vector_sum[2],
        vector_sum[3],
        out_weight_grad,
        vector_sum[4],
        vector_sum[5],
        vector_sum[6],
        up_sum[None],
        bias_sum[:, :up_share],
        down_sum[None],
        bias_sum[:, up_share : up_share + down_share],
    )


def solution(mesh):
    return jax.shard_map(
        body,
        mesh=mesh,
        in_specs=(
            P(("wide", "narrow"), None),
            P(("wide", "narrow"), None),
            P(("wide", "narrow"), None),
            P(),
            P(),
            P(),
            P(),
            P(),
            P(),
            P(),
            P(),
            P(),
            P("wide", None, None),
            P("wide", None),
            P("wide", None, None),
            P("wide", None),
            P(("wide", "narrow"), None),
        ),
        out_specs=(
            P(("wide", "narrow"), None),
            P(("wide", "narrow"), None),
            P(("wide", "narrow")),
            P(("wide", "narrow")),
            P(("wide", "narrow"), None),
            P(("wide", "narrow")),
            P(("wide", "narrow")),
            P(("wide", "narrow"), None),
            P(("wide", "narrow")),
            P(("wide", "narrow")),
            P(("wide", "narrow")),
            P("wide", "narrow", None),
            P("wide", "narrow"),
            P("wide", "narrow", None),
            P("wide", "narrow"),
        ),
        check_vma=False,
    )
```
